32 devices in a mesh: rep: 4 (over z), fsdp: 4 (over y, x), seq: 2 (over core).
Axes of the slice: x: 2, y: 2, z: 4, core: 2. Of those that a mesh axis runs over, the one named last changes fastest.
Arguments:
- tokens: bfloat16 [32, 1024, 1024], P(('rep', 'fsdp'), 'seq'), may hold values from -6 to 6
- segment_ids: int32 [32, 1024], P(('rep', 'fsdp'), 'seq'), may hold values from 0 to 3, as said below
- padding: int32 [32, 1024], P(('rep', 'fsdp'), 'seq'), may hold values from 0 to 1, as said below
- cotangent: bfloat16 [32, 1024, 1024], P(('rep', 'fsdp'), 'seq'), may hold values from -6 to 6
- w_query: bfloat16 [1024, 1024], P(('fsdp', 'seq')), may hold values from -0.25 to 0.25
- w_key: bfloat16 [1024, 1024], P(('fsdp', 'seq')), may hold values from -0.1875 to 0.1875
- w_value: bfloat16 [1024, 1024], P(('fsdp', 'seq')), may hold values from -0.1875 to 0.1875
- w_out: bfloat16 [1024, 1024], P(('fsdp', 'seq')), may hold values from -0.75 to 0.75
- b_query: bfloat16 [1024], P(('fsdp', 'seq')), may hold values from -3 to 3
- b_value: bfloat16 [1024], P(('fsdp', 'seq')), may hold values from -3 to 3
- b_out: bfloat16 [1024], P(('fsdp', 'seq')), may hold values from -3 to 3
- gain_one: bfloat16 [1024], P(('fsdp', 'seq')), may hold values from 0.099609375 to 1.8984375
- shift_one: bfloat16 [1024], P(('fsdp', 'seq')), may hold values from -3 to 3
- w_up: bfloat16 [1024, 4096], P(('fsdp', 'seq')), may hold values from -0.1875 to 0.1875
- b_up: bfloat16 [4096], P(('fsdp', 'seq')), may hold values from -3 to 3
- w_down: bfloat16 [4096, 1024], P(('fsdp', 'seq')), may hold values from -0.09375 to 0.09375
- b_down: bfloat16 [1024], P(('fsdp', 'seq')), may hold values from -3 to 3
- gain_two: bfloat16 [1024], P(('fsdp', 'seq')), may hold values from 0.099609375 to 1.8984375
- shift_two: bfloat16 [1024], P(('fsdp', 'seq')), may hold values from -3 to 3
Outputs:
- output: bfloat16 [32, 1024, 1024], P(('rep', 'fsdp'), 'seq')
- input_grad: float32 [32, 1024, 1024], P(('rep', 'fsdp'), 'seq')
- grad_w_query: float32 [1024, 1024], P(('fsdp', 'seq'))
- grad_w_key: float32 [1024, 1024], P(('fsdp', 'seq'))
- grad_w_value: float32 [1024, 1024], P(('fsdp', 'seq'))
- grad_w_out: float32 [1024, 1024], P(('fsdp', 'seq'))
- grad_b_query: float32 [1024], P(('fsdp', 'seq'))
- grad_b_value: float32 [1024], P(('fsdp', 'seq'))
- grad_b_out: float32 [1024], P(('fsdp', 'seq'))
- grad_gain_one: float32 [1024], P(('fsdp', 'seq'))
- grad_shift_one: float32 [1024], P(('fsdp', 'seq'))
- grad_w_up: float32 [1024, 4096], P(('fsdp', 'seq'))
- grad_b_up: float32 [4096], P(('fsdp', 'seq'))
- grad_w_down: float32 [4096, 1024], P(('fsdp', 'seq'))
- grad_b_down: float32 [1024], P(('fsdp', 'seq'))
- grad_gain_two: float32 [1024], P(('fsdp', 'seq'))
- grad_shift_two: float32 [1024], P(('fsdp', 'seq'))
The draws below stay inside these ranges and needn't reach their ends.
Inputs may be any that keep to these rules, and one draw needn't show every extreme that they name: `segment_ids`: along each sequence the ids never fall and start at 0; every document holds a real token; some document of each sequence holds tokens of the first and of the third quarter of the sequence. `padding`: within each sequence the padded tokens form its tail, of 1 to 128 tokens, inside its last document.
All inputs are finite; a program needn't handle non-finite values.
Results may differ from the reference program's by a relative error of at most 0.014.
Values may be sent and summed in bfloat16 or wider, within the bound.
No kernel may reach another device: no remote copies, remote signals or barrier semaphores. Data moves between devices by JAX's collectives and lax.ppermute only.
A program may use at most 320 MiB of HBM per device.

```python
import math
import jax
import jax.numpy as jnp
from jax import lax

D = 1024
HEADS = 16
HEAD_DIM = 64
FF = 4096
LENGTH = 1024
SEQUENCES = 32


def draw_segment_ids(key, part):
    key = jax.random.fold_in(key, 11)
    first_key, second_key = jax.random.split(key)
    quarter = max(LENGTH // 4, 2)
    early = jax.random.randint(first_key, (SEQUENCES, 2), 1, quarter)
    late = jax.random.randint(second_key, (SEQUENCES, 1), 3 * LENGTH // 4, 7 * LENGTH // 8)
    cuts = jnp.concatenate([early, late], 1)
    places = jnp.arange(LENGTH, dtype=jnp.int32)
    return jnp.sum((places[None, :, None] >= cuts[:, None, :]).astype(jnp.int32), -1).astype(jnp.int32)


def draw_padding(key, part):
    key = jax.random.fold_in(key, 23)
    pad_count = jax.random.randint(key, (SEQUENCES, 1), 1, LENGTH // 8 + 1)
    places = jnp.arange(LENGTH, dtype=jnp.int32)
    return (places[None, :] < LENGTH - pad_count).astype(jnp.int32)


def block_scale(stream_key, dims, cuts, low, high):
    def one(axis_at, shards_of):
        steps = jax.random.uniform(jax.random.fold_in(jax.random.fold_in(stream_key, 6), axis_at), (shards_of,), jnp.float32, low / len(cuts), high / len(cuts))
        return jnp.repeat(jnp.exp(steps), dims[axis_at] // shards_of).reshape((-1,) + (1,) * (len(dims) - axis_at - 1))

    factor_of = one(*cuts[0])
    for cut in cuts[1:]:
        factor_of = factor_of * one(*cut)
    return factor_of


def gaussian(key, dims, deviation, limit, pieces=(), held_as=jnp.bfloat16):
    level = block_scale(key, dims, pieces, -0.22, 0.18) if pieces else 1.0
    drawn = jax.random.normal(key, dims, jnp.float32) * deviation * level
    return jnp.minimum(jnp.maximum(drawn, -limit), limit).astype(held_as)


def setup_inputs(seed: int = 0) -> dict:
    seeds = jax.random.split(jax.random.key(seed), 20)
    return {
        "tokens": gaussian(seeds[0], (SEQUENCES, LENGTH, D), 1.0, 6.0, ((0, 16), (1, 2))),
        "segment_ids": draw_segment_ids(jax.random.fold_in(seeds[19], 71), 0),
        "padding": draw_padding(jax.random.fold_in(seeds[19], 71), 0),
        "cotangent": gaussian(seeds[3], (SEQUENCES, LENGTH, D), 1.0, 6.0, ((0, 16), (1, 2))),
        "w_query": gaussian(seeds[4], (D, D), (D // 2) ** -0.5, 0.25, ((0, 8),)),
        "w_key": gaussian(seeds[5], (D, D), D ** -0.5, 0.1875, ((0, 8),)),
        "w_value": gaussian(seeds[6], (D, D), D ** -0.5, 0.1875, ((0, 8),)),
        "w_out": gaussian(seeds[7], (D, D), (D // 16) ** -0.5, 0.75, ((0, 8),)),
        "b_query": gaussian(seeds[8], (D,), 0.5, 3.0, ((0, 8),)),
        "b_value": gaussian(seeds[9], (D,), 0.5, 3.0, ((0, 8),)),
        "b_out": gaussian(seeds[10], (D,), 0.5, 3.0, ((0, 8),)),
        "gain_one": jnp.clip(1.0 + 0.18 * jax.random.normal(seeds[11], (D,), jnp.float32), 0.099609375, 1.8984375).astype(jnp.bfloat16),
        "shift_one": gaussian(seeds[12], (D,), 0.5, 3.0, ((0, 8),)),
        "w_up": gaussian(seeds[13], (D, FF), D ** -0.5, 0.1875, ((0, 8),)),
        "b_up": gaussian(seeds[14], (FF,), 0.5, 3.0, ((0, 8),)),
        "w_down": gaussian(seeds[15], (FF, D), FF ** -0.5, 0.09375, ((0, 8),)),
        "b_down": gaussian(seeds[16], (D,), 0.5, 3.0, ((0, 8),)),
        "gain_two": jnp.clip(1.0 + 0.18 * jax.random.normal(seeds[17], (D,), jnp.float32), 0.099609375, 1.8984375).astype(jnp.bfloat16),
        "shift_two": gaussian(seeds[18], (D,), 0.5, 3.0, ((0, 8),)),
    }


EPSILON = 1e-05
MASKED = -1e+30
HIGHEST = lax.Precision.HIGHEST

@jax.custom_vjp
def low(v):
    return lax.optimization_barrier(v.astype(jnp.bfloat16)).astype(jnp.float32)

@jax.custom_vjp
def low_back(v):
    return v

def low_keep(v):
    return (low(v), None)

def low_pass(kept, grad):
    return (grad,)

def back_keep(v):
    return (v, None)

def back_low(kept, grad):
    return (low(grad),)
low.defvjp(low_keep, low_pass)
low_back.defvjp(back_keep, back_low)

def round_both(value):
    return low_back(low(value))

def product(left, right):
    return jnp.matmul(left, right, precision=HIGHEST)

def layer_norm(values, gain, shift):
    centred = values - lax.optimization_barrier(jnp.mean(values, -1, keepdims=True))
    variance = lax.optimization_barrier(jnp.mean(centred * centred, -1, keepdims=True))
    return centred * lax.rsqrt(variance + EPSILON) * gain + shift

def attend(inputs):
    queries, keys_seq, values_seq, segment, keep_mask = inputs
    length = queries.shape[0]
    split_query = queries.reshape(length, HEADS, HEAD_DIM)
    split_key = keys_seq.reshape(length, HEADS, HEAD_DIM)
    split_value = values_seq.reshape(length, HEADS, HEAD_DIM)
    scores = low_back(jnp.einsum('qhd,khd->hqk', split_query, split_key, precision=HIGHEST) * HEAD_DIM ** (-0.5))
    allowed = (segment[:, None] == segment[None, :]) & (keep_mask[None, :] > 0)
    scores = jnp.where(allowed[None], scores, MASKED)
    shifted = jnp.exp(scores - lax.optimization_barrier(jnp.max(scores, -1, keepdims=True)))
    attn_probs = low(shifted / lax.optimization_barrier(jnp.sum(shifted, -1, keepdims=True)))
    mixed_heads = jnp.einsum('hqk,khd->qhd', attn_probs, split_value, precision=HIGHEST)
    return mixed_heads.reshape(length, HEADS * HEAD_DIM)

def forward(params, inputs, segment, keep_mask):
    w_query, w_key, w_value, w_out, b_query, b_value, b_out, gain_one, shift_one, w_up, b_up, w_down, b_down, gain_two, shift_two = params
    queries = round_both(product(inputs, w_query) + b_query)
    keys_all = round_both(product(inputs, w_key))
    values_all = round_both(product(inputs, w_value) + b_value)
    attended = round_both(lax.map(jax.checkpoint(attend), (queries, keys_all, values_all, segment, keep_mask)))
    branch = low_back(product(attended, w_out) + b_out)
    first = layer_norm(inputs + branch, gain_one, shift_one)
    hidden = low_back(product(low(first), w_up) + b_up)
    activated = low(jax.nn.gelu(hidden, approximate=False))
    second = low_back(product(activated, w_down) + b_down)
    return layer_norm(first + second, gain_two, shift_two)

def reference(tokens, segment_ids, padding, cotangent, w_query, w_key, w_value, w_out, b_query, b_value, b_out, gain_one, shift_one, w_up, b_up, w_down, b_down, gain_two, shift_two):
    params = tuple((param.astype(jnp.float32) for param in (w_query, w_key, w_value, w_out, b_query, b_value, b_out, gain_one, shift_one, w_up, b_up, w_down, b_down, gain_two, shift_two)))
    group = math.gcd(SEQUENCES, max(1, 4096 // LENGTH))
    blocks = SEQUENCES // group

    def regroup(array):
        return array.reshape((blocks, group) + array.shape[1:])

    def one_block(totals, inputs):
        block_tokens, block_segments, block_padding, block_grad = inputs

        def apply_layer(weights, acts):
            return forward(weights, acts, block_segments, block_padding)
        outputs, pullback = jax.vjp(apply_layer, params, block_tokens.astype(jnp.float32))
        weight_grads, block_input_grad = pullback(block_grad.astype(jnp.float32))
        totals = jax.tree.map(lambda total, extra: total + extra, totals, weight_grads)
        return (totals, (outputs.astype(jnp.bfloat16), block_input_grad))
    zeros = tuple((jnp.zeros_like(param) for param in params))
    totals, stacked = lax.scan(one_block, zeros, (regroup(tokens), regroup(segment_ids), regroup(padding), regroup(cotangent)))
    output = stacked[0].reshape(SEQUENCES, LENGTH, D)
    input_grad = stacked[1].reshape(SEQUENCES, LENGTH, D)
    g_query, g_key, g_value, g_out, g_bquery, g_bvalue, g_bout, g_gone, g_sone, g_up, g_bup, g_down, g_bdown, g_gtwo, g_stwo = totals
    return (output, input_grad, g_query, g_key, g_value, g_out, g_bquery, g_bvalue, g_bout, g_gone, g_sone, g_up, g_bup, g_down, g_bdown, g_gtwo, g_stwo)
```

```python
import functools
import math
import jax
import jax.numpy as jnp
from jax import lax
from jax.experimental import pallas as pl
from jax.experimental.pallas import tpu as pltpu
from jax.sharding import PartitionSpec as P

F32 = jnp.float32
BF = jnp.bfloat16
HEAD_DIM = 64
LANES = 128
EPSILON = 1e-05
ROOT_HALF = 0.7071067811865476
INV_ROOT_TAU = 0.3989422804014327
NT = (((1,), (1,)), ((), ()))
TN = (((0,), (0,)), ((), ()))
NN = (((1,), (0,)), ((), ()))
VMEM = 58 << 20
ANY = pl.BlockSpec(memory_space=pl.ANY)


def dg(a, b, dims):
    return lax.dot_general(a, b, dims, preferred_element_type=F32)


def params(limit=VMEM):
    return pltpu.CompilerParams(vmem_limit_bytes=limit)


def cost(flops, bytes_accessed, trans=0):
    return pl.CostEstimate(flops=flops, bytes_accessed=bytes_accessed, transcendentals=trans)


def swap(x, axis, size, xor):
    return lax.ppermute(x, axis, [(i, i ^ xor) for i in range(size)])


class Gathered:
    def __init__(self, arrays, entries, half):
        self.arrays, self.entries, self.half = arrays, entries, half

    def copies(self, refs, ids, targets, sems):
        out = []
        for which, index, half, slot in self.entries:
            low = half * self.half
            for first, rows, dest, stride, offset in targets:
                a, b = max(first, low), min(first + rows, low + self.half)
                if a >= b:
                    continue
                src = refs[which].at[(*index, pl.ds(a - low, b - a))]
                start = pl.multiple_of(ids[slot] * stride + (offset + a - first), 16)
                out.append(pltpu.make_async_copy(src, dest.at[pl.ds(start, b - a)], sems.at[len(out)]))
        return out

    def count(self, targets):
        n = 0
        for _, _, half, _ in self.entries:
            low = half * self.half
            n += sum(max(t[0], low) < min(t[0] + t[1], low + self.half) for t in targets)
        return n


def gather_start(halves, nf):
    if nf == 4:
        one, two = halves
        return {
            "xa": swap(one, "fsdp", nf, 1),
            "yb": swap(two, "fsdp", nf, 2),
            "ya": swap(one, "fsdp", nf, 2),
            "xb": swap(two, "fsdp", nf, 1),
        }
    return {"all": [lax.all_gather(h, "fsdp", axis=0) for h in halves]}


def gather_far(first, nf):
    if nf == 4:
        return swap(first["xa"], "fsdp", nf, 2), swap(first["yb"], "fsdp", nf, 1)
    return ()


def gather_end(halves, first, far, nf, ns):
    half = halves[0].shape[0]
    if nf == 4:
        arrays = [halves[0], halves[1], first["xa"], first["xb"], first["ya"], first["yb"], far[0], far[1]]
        entries = [(w, (), w % 2, 2 * (w // 2)) for w in range(8)]
    else:
        arrays = list(first["all"])
        entries = [(h, (f,), h, 2 * nf + 2 * f) for f in range(nf) for h in range(2)]
    n = len(arrays)
    arrays = arrays + [swap(a, "seq", ns, 1) for a in arrays]
    entries = entries + [(w + n, i, h, s + 1) for w, i, h, s in entries]
    return Gathered(arrays, entries, half)


BIAS_ROWS = 32


def split_kernel(moves, nin, nout, *refs):
    ins, outs, sems = refs[:nin], refs[len(refs) - nout - 1 : -1], refs[-1]
    copies = [
        pltpu.make_async_copy(ins[s].at[pl.ds(first, rows)], outs[d].at[pl.ds(to, rows)], sems.at[i])
        for i, (s, first, rows, d, to) in enumerate(moves)
    ]
    for m in copies:
        m.start()
    for m in copies:
        m.wait()


def split_rows(ins, moves, out_shapes, deps, name):
    return pl.pallas_call(
        functools.partial(split_kernel, moves, len(ins), len(out_shapes)),
        in_specs=[ANY] * (len(ins) + len(deps)),
        out_specs=[ANY] * len(out_shapes),
        out_shape=[jax.ShapeDtypeStruct(o, BF) for o in out_shapes],
        scratch_shapes=[pltpu.SemaphoreType.DMA((len(moves),))],
        compiler_params=params(4 << 20),
        name=name,
    )(*ins, *deps)


def bias_kernel(nvec, *refs):
    vecs, out, tile = refs[:nvec], refs[nvec], refs[nvec + 1]
    part = vecs[0].shape[-1]
    tile[...] = jnp.zeros_like(tile)
    for i in range(8):
        tile[0:1, i * part : (i + 1) * part] = vecs[i][...].astype(F32).reshape(1, part)
    tile[1:2, 0 : 4 * part] = vecs[8][...].astype(F32).reshape(1, 4 * part)
    out[...] = tile[...].astype(BF)


def pack_bias(vecs, width):
    return pl.pallas_call(
        functools.partial(bias_kernel, len(vecs)),
        in_specs=[pl.BlockSpec(memory_space=pltpu.VMEM)] * len(vecs),
        out_specs=pl.BlockSpec(memory_space=pltpu.VMEM),
        out_shape=jax.ShapeDtypeStruct((BIAS_ROWS, width), BF),
        scratch_shapes=[pltpu.VMEM((BIAS_ROWS, width), F32)],
        compiler_params=params(4 << 20),
        name="pack_bias",
    )(*vecs)


def qkv_kernel(got, ids, x_ref, *rest):
    n = len(got.arrays)
    pieces, (q_ref, k_ref, v_ref, p_ref, b_ref, wq, wk, wv, wb, sems) = rest[:n], rest[n:]
    width = x_ref.shape[1]
    nb = wb.shape[0] // BIAS_ROWS
    part = width // nb
    targets = qkv_targets(part, wq, wk, wv, wb)

    @pl.when(pl.program_id(0) == 0)
    def _():
        moves = got.copies(pieces, ids, targets, sems)
        for m in moves:
            m.start()
        for m in moves:
            m.wait()
        for b in range(nb):
            rows = wb[b * BIAS_ROWS : b * BIAS_ROWS + 16, :].astype(F32)
            for vec in range(8):
                p_ref[vec : vec + 1, b * part : (b + 1) * part] = rows[0:1, vec * part : (vec + 1) * part]
            b_ref[0:1, b * 4 * part : (b + 1) * 4 * part] = rows[1:2, 0 : 4 * part]

    x = x_ref[...]
    q_ref[...] = (dg(x, wq[...], NN) + p_ref[0:1, :]).astype(BF)
    k_ref[...] = dg(x, wk[...], NN).astype(BF)
    v_ref[...] = (dg(x, wv[...], NN) + p_ref[1:2, :]).astype(BF)


def qkv_targets(part, wq, wk, wv, wb):
    t = [(0, part, wq, part, 0), (part, part, wk, part, 0), (2 * part, part, wv, part, 0)]
    if wb is not None:
        t.append((3 * part, BIAS_ROWS, wb, BIAS_ROWS, 0))
    return t


def project(x, got, ids, nb, block=256):
    n, width = x.shape
    grid = n // block
    rows = pl.BlockSpec((block, width), lambda i, ids: (i, 0))
    whole = lambda shape: pl.BlockSpec(shape, lambda i, ids: (0, 0))
    count = got.count(qkv_targets(width // nb, 0, 0, 0, 0))
    return pl.pallas_call(
        functools.partial(qkv_kernel, got),
        grid_spec=pltpu.PrefetchScalarGridSpec(
            num_scalar_prefetch=1,
            grid=(grid,),
            in_specs=[rows] + [ANY] * len(got.arrays),
            out_specs=[rows, rows, rows, whole((8, width)), whole((1, 4 * width))],
            scratch_shapes=[pltpu.VMEM((width, width), BF)] * 3
            + [pltpu.VMEM((nb * BIAS_ROWS, width), BF), pltpu.SemaphoreType.DMA((count,))],
        ),
        out_shape=[jax.ShapeDtypeStruct((n, width), BF)] * 3
        + [jax.ShapeDtypeStruct((8, width), F32), jax.ShapeDtypeStruct((1, 4 * width), F32)],
        compiler_params=params(),
        cost_estimate=cost(6 * n * width * width, 2 * n * width * 4 + 6 * width * width),
        name="project",
    )(ids, x, *got.arrays)


def split3(v):
    hi=v.astype(BF); r=v-hi.astype(F32); mid=r.astype(BF); lo=(r-mid.astype(F32)).astype(BF)
    return hi,mid,lo
def attn_fwd_kernel(qb, q_ref,k_ref,v_ref,qf_ref,kf_ref,*rest):
    a_ref,lf_ref=rest[-2:]
    n=q_ref.shape[0]
    lane=lax.broadcasted_iota(jnp.int32,(n,LANES),1)
    left=lane<HEAD_DIM
    q=q_ref[...]*jnp.asarray(0.125,BF); k=k_ref[...]; v=v_ref[...]
    qf=qf_ref[...]; kf=kf_ref[...]
    one=jnp.ones_like(v)
    sides=[]
    for h in range(2):
        own=left if h==0 else ~left
        sides.append((jnp.where(own,q,qf),jnp.where(own,k,kf),jnp.where(own,v,one)))
    lq=lax.broadcasted_iota(jnp.int32,(qb,LANES),1)
    leftq=lq<HEAD_DIM
    for c in range(n//qb):
        rows=slice(c*qb,(c+1)*qb)
        res=[]; lse=[]
        for h in range(2):
            qa,ka,va=sides[h]
            s=dg(qa[rows],ka,NT)
            m=jnp.max(s,-1,keepdims=True)
            p=jnp.exp(s-m).astype(BF)
            o=dg(p,va,NN)
            tot=o[:,64:65] if h==0 else o[:,0:1]
            res.append(o/tot)
            lse.append(m+jnp.log(tot))
        a_ref[rows,:]=jnp.where(leftq,res[0],res[1]).astype(BF)
        lm=jnp.where(leftq,lse[1],lse[0])
        hi,mid,lo=split3(lm)
        j=lq%HEAD_DIM
        base=qf[rows]
        lf_ref[rows,:]=jnp.where(j==4,hi,jnp.where(j==5,mid,jnp.where(j==6,lo,base)))
def attn_fwd(q,k,v,qf,kf,first,npair,deps=(),qb=512):
    n=q.shape[0]
    blk=pl.BlockSpec((n,LANES),lambda i:(0,i+first))
    whole=pl.BlockSpec((n,LANES),lambda i:(0,0))
    out=pl.BlockSpec((n,LANES),lambda i:(0,i))
    return pl.pallas_call(functools.partial(attn_fwd_kernel,qb),grid=(npair,),
        in_specs=[blk,blk,blk,whole,whole]+[ANY]*len(deps),out_specs=[out,out],
        out_shape=[jax.ShapeDtypeStruct((n,npair*LANES),BF)]*2,
        compiler_params=pltpu.CompilerParams(vmem_limit_bytes=50<<20),
        cost_estimate=pl.CostEstimate(flops=npair*2*2*2*n*n*256,bytes_accessed=npair*n*LANES*2*5,transcendentals=npair*2*n*n),
        name="attend_forward")(q,k,v,qf,kf,*deps)
def attn_bwd_kernel(qb,q_ref,k_ref,v_ref,da_ref,a_ref,lf_ref,kf_ref,*rest):
    d_ref,dka,dva=rest[-3:]
    n=q_ref.shape[0]
    lane=lax.broadcasted_iota(jnp.int32,(n,LANES),1)
    left=lane<HEAD_DIM
    q=q_ref[...]*jnp.asarray(0.125,BF); k=k_ref[...]; v=v_ref[...]; da=da_ref[...]
    lf=lf_ref[...]; kf=kf_ref[...]
    prod=da.astype(F32)*a_ref[...].astype(F32)
    j=lane%HEAD_DIM
    zero=jnp.zeros_like(q)
    minus=jnp.where((j>=4)&(j<7),jnp.asarray(-1,BF),jnp.asarray(0,BF))
    sides=[]
    for h in range(2):
        own=left if h==0 else ~left
        d=jnp.sum(jnp.where(own,prod,0.0),-1,keepdims=True)
        hi,mid,lo=split3(d)
        df=jnp.where(j==4,hi,jnp.where(j==5,mid,jnp.where(j==6,lo,zero)))
        sides.append((jnp.where(own,q,lf),jnp.where(own,k,kf),jnp.where(own,v,minus),jnp.where(own,da,df),
                      jnp.where(own,q,zero),jnp.where(own,da,zero)))
    kt=k.T
    for c in range(n//qb):
        rows=slice(c*qb,(c+1)*qb)
        dqs=[]; dk=None; dv=None
        for h in range(2):
            qa,ka,va,daa,qz,daz=sides[h]
            s=dg(ka,qa[rows],NT)
            p=jnp.exp(s)
            dp=dg(va,daa[rows],NT)
            ds=(p*dp).astype(BF)
            pb=p.astype(BF)
            x=dg(pb,daz[rows],NN); dv=x if dv is None else dv+x
            y=dg(ds,qz[rows],NN); dk=y if dk is None else dk+y
            dqs.append(dg(kt[h*64:(h+1)*64],ds,NN))
        d_ref[0,rows,:]=(jnp.concatenate(dqs,0).T*0.125).astype(BF)
        if c==0: dka[...]=dk; dva[...]=dv
        else: dka[...]+=dk; dva[...]+=dv
    d_ref[1]=dka[...].astype(BF)
    d_ref[2]=dva[...].astype(BF)
def attn_bwd(q,k,v,da,a,lf,kf,first,npair,deps=(),qb=256):
    n=q.shape[0]
    blk=pl.BlockSpec((n,LANES),lambda i:(0,i+first))
    whole=pl.BlockSpec((n,LANES),lambda i:(0,0))
    own=pl.BlockSpec((n,LANES),lambda i:(0,i))
    out=pl.BlockSpec((3,n,LANES),lambda i:(0,0,i))
    return pl.pallas_call(functools.partial(attn_bwd_kernel,qb),grid=(npair,),
        in_specs=[blk]*5+[own,whole]+[ANY]*len(deps),out_specs=out,
        out_shape=jax.ShapeDtypeStruct((3,n,npair*LANES),BF),
        scratch_shapes=[pltpu.VMEM((n,LANES),F32)]*2,
        compiler_params=pltpu.CompilerParams(vmem_limit_bytes=50<<20),
        cost_estimate=pl.CostEstimate(flops=npair*2*5*2*n*n*256,bytes_accessed=npair*n*LANES*2*9,transcendentals=npair*2*n*n),
        name="attend_backward")(q,k,v,da,a,lf,kf,*deps)
def seg_features(seg,pad):
    n=seg.shape[0]
    j=lax.broadcasted_iota(jnp.int32,(n,LANES),1)%HEAD_DIM
    same=(seg[:,None]==j)
    qf=jnp.where((j<4)&same,1.0,0.0).astype(BF)
    kf=jnp.where(j<4,jnp.where(same&(pad[:,None]>0),0.0,-1e30),jnp.where(j<7,-1.0,0.0)).astype(BF)
    return qf,kf


def up_kernel(got, part, ids, x_ref, p_ref, bup_ref, *rest):
    n = len(got.arrays)
    *a_refs, wo = rest[: len(rest) - n - 9]
    pieces = rest[len(rest) - n - 9 : len(rest) - 9]
    a_all, y_ref, yb_ref, n_ref, s_ref, g_ref, gp_ref, wu, sems = rest[-9:]
    width = x_ref.shape[1]
    targets = [(0, part, wu, part, 0)]

    @pl.when(pl.program_id(0) == 0)
    def _():
        for m in got.copies(pieces, ids, targets, sems):
            m.start()

    a = jnp.concatenate([r[...] for r in a_refs], 1)
    a_all[...] = a
    r = x_ref[...].astype(F32) + dg(a, wo[...], NN) + p_ref[2:3, :]
    c = r - jnp.mean(r, -1, keepdims=True)
    s = lax.rsqrt(jnp.mean(c * c, -1, keepdims=True) + EPSILON)
    normed = c * s
    y = normed * p_ref[3:4, :] + p_ref[4:5, :]
    y_ref[...] = y
    n_ref[...] = normed.astype(BF)
    s_ref[...] = s
    yb = y.astype(BF)
    yb_ref[...] = yb

    @pl.when(pl.program_id(0) == 0)
    def _():
        for m in got.copies(pieces, ids, targets, sems):
            m.wait()

    step = 512
    for k in range(0, 4 * width, step):
        h = dg(yb, wu[:, k : k + step], NN) + bup_ref[:, k : k + step]
        phi = 0.5 + 0.5 * lax.erf(h * ROOT_HALF)
        g_ref[:, k : k + step] = (h * phi).astype(BF)
        gp_ref[:, k : k + step] = (phi + h * (jnp.exp(-0.5 * h * h) * INV_ROOT_TAU)).astype(BF)


def up_part(x, vecs, bup, a_parts, w_out, got, ids, nb, block=256):
    n, width = x.shape
    part = width // nb
    rows = lambda w: pl.BlockSpec((block, w), lambda i, ids: (i, 0))
    whole = lambda shape: pl.BlockSpec(shape, lambda i, ids: (0, 0))
    count = got.count([(0, part, 0, 0, 0)])
    sds = jax.ShapeDtypeStruct
    return pl.pallas_call(
        functools.partial(up_kernel, got, part),
        grid_spec=pltpu.PrefetchScalarGridSpec(
            num_scalar_prefetch=1,
            grid=(n // block,),
            in_specs=[rows(width), whole((8, width)), whole((1, 4 * width))]
            + [rows(a.shape[1]) for a in a_parts]
            + [whole((width, width))]
            + [ANY] * len(got.arrays),
            out_specs=[rows(width), rows(width), rows(width), rows(width), rows(1), rows(4 * width), rows(4 * width)],
            scratch_shapes=[pltpu.VMEM((width, 4 * width), BF), pltpu.SemaphoreType.DMA((count,))],
        ),
        out_shape=[
            sds((n, width), BF),
            sds((n, width), F32),
            sds((n, width), BF),
            sds((n, width), BF),
            sds((n, 1), F32),
            sds((n, 4 * width), BF),
            sds((n, 4 * width), BF),
        ],
        compiler_params=params(),
        cost_estimate=cost(10 * n * width * width, 28 * n * width + 10 * width * width, 8 * n * width),
        name="out_norm_up",
    )(ids, x, vecs, bup, *a_parts, w_out, *got.arrays)


def down_kernel(g_ref, y_ref, c_ref, p_ref, wd, o_ref, df_ref, dr_ref, sum_ref):
    @pl.when(pl.program_id(0) == 0)
    def _():
        sum_ref[...] = jnp.zeros_like(sum_ref)

    r = y_ref[...] + dg(g_ref[...], wd[...], NN) + p_ref[5:6, :]
    c = r - jnp.mean(r, -1, keepdims=True)
    s = lax.rsqrt(jnp.mean(c * c, -1, keepdims=True) + EPSILON)
    normed = c * s
    gain = p_ref[6:7, :]
    o_ref[...] = (normed * gain + p_ref[7:8, :]).astype(BF)
    ct = c_ref[...].astype(F32)
    e = ct * gain
    dr = s * (e - jnp.mean(e, -1, keepdims=True) - normed * jnp.mean(e * normed, -1, keepdims=True))
    dr_ref[...] = dr
    df = dr.astype(BF)
    df_ref[...] = df
    sum_ref[0:1, :] += jnp.sum(ct * normed, 0, keepdims=True)
    sum_ref[1:2, :] += jnp.sum(ct, 0, keepdims=True)
    sum_ref[2:3, :] += jnp.sum(df.astype(F32), 0, keepdims=True)


def down_part(g, y, ct, vecs, w_down, block=256):
    n, width = y.shape
    rows = lambda w: pl.BlockSpec((block, w), lambda i: (i, 0))
    whole = lambda shape: pl.BlockSpec(shape, lambda i: (0, 0))
    sds = jax.ShapeDtypeStruct
    return pl.pallas_call(
        down_kernel,
        grid=(n // block,),
        in_specs=[rows(4 * width), rows(width), rows(width), whole((8, width)), whole((4 * width, width))],
        out_specs=[rows(width), rows(width), rows(width), whole((8, width))],
        out_shape=[sds((n, width), BF), sds((n, width), BF), sds((n, width), F32), sds((8, width), F32)],
        compiler_params=params(),
        cost_estimate=cost(8 * n * width * width, 22 * n * width + 8 * width * width),
        name="down_norm",
    )(g, y, ct, vecs, w_down)


def hidden_kernel(df_ref, gp_ref, wd, dh_ref, bup_ref):
    @pl.when(pl.program_id(0) == 0)
    def _():
        bup_ref[...] = jnp.zeros_like(bup_ref)

    df = df_ref[...]
    step = 512
    for k in range(0, dh_ref.shape[1], step):
        dh = (dg(df, wd[k : k + step, :], NT) * gp_ref[:, k : k + step].astype(F32)).astype(BF)
        dh_ref[:, k : k + step] = dh
        bup_ref[:, k : k + step] += jnp.sum(dh.astype(F32), 0, keepdims=True)


def hidden_part(df, gp, w_down, block=256):
    n, width = df.shape
    rows = lambda w: pl.BlockSpec((block, w), lambda i: (i, 0))
    whole = lambda shape: pl.BlockSpec(shape, lambda i: (0, 0))
    return pl.pallas_call(
        hidden_kernel,
        grid=(n // block,),
        in_specs=[rows(width), rows(4 * width), whole((4 * width, width))],
        out_specs=[rows(4 * width), whole((1, 4 * width))],
        out_shape=[jax.ShapeDtypeStruct((n, 4 * width), BF), jax.ShapeDtypeStruct((1, 4 * width), F32)],
        compiler_params=params(),
        cost_estimate=cost(8 * n * width * width, 18 * n * width + 8 * width * width),
        name="hidden_gradient",
    )(df, gp, w_down)


def back_kernel(up, part, ids, dh_ref, dr_ref, n_ref, s_ref, p_ref, wo, *rest):
    nu = len(up.arrays)
    pu = rest[:nu]
    dr1_ref, do_ref, da_ref, sum_ref, wu, su = rest[-6:]
    tu = [(0, part, wu, part, 0)]

    @pl.when(pl.program_id(0) == 0)
    def _():
        moves = up.copies(pu, ids, tu, su)
        for m in moves:
            m.start()
        sum_ref[...] = jnp.zeros_like(sum_ref)
        for m in moves:
            m.wait()

    dy = dr_ref[...] + dg(dh_ref[...], wu[...], NT)
    normed = n_ref[...].astype(F32)
    e = dy * p_ref[3:4, :]
    dr = s_ref[...] * (e - jnp.mean(e, -1, keepdims=True) - normed * jnp.mean(e * normed, -1, keepdims=True))
    dr1_ref[...] = dr
    do = dr.astype(BF)
    do_ref[...] = do
    da_ref[...] = dg(do, wo[...], NT).astype(BF)
    sum_ref[0:1, :] += jnp.sum(dy * normed, 0, keepdims=True)
    sum_ref[1:2, :] += jnp.sum(dy, 0, keepdims=True)
    sum_ref[2:3, :] += jnp.sum(do.astype(F32), 0, keepdims=True)


def back_part(dh, dr, normed, inverse, vecs, w_out, up, ids, nb, deps=(), block=256):
    n, width = dr.shape
    part = width // nb
    rows = lambda w: pl.BlockSpec((block, w), lambda i, ids: (i, 0))
    whole = lambda shape: pl.BlockSpec(shape, lambda i, ids: (0, 0))
    sds = jax.ShapeDtypeStruct
    return pl.pallas_call(
        functools.partial(back_kernel, up, part),
        grid_spec=pltpu.PrefetchScalarGridSpec(
            num_scalar_prefetch=1,
            grid=(n // block,),
            in_specs=[rows(4 * width), rows(width), rows(width), rows(1), whole((8, width)), whole((width, width))]
            + [ANY] * (len(up.arrays) + len(deps)),
            out_specs=[rows(width), rows(width), rows(width), whole((8, width))],
            scratch_shapes=[pltpu.VMEM((width, 4 * width), BF), pltpu.SemaphoreType.DMA((up.count([(0, part, 0, 0, 0)]),))],
        ),
        out_shape=[sds((n, width), F32), sds((n, width), BF), sds((n, width), BF), sds((8, width), F32)],
        compiler_params=params(),
        cost_estimate=cost(10 * n * width * width, 22 * n * width + 10 * width * width),
        name="norm_backward",
    )(ids, dh, dr, normed, inverse, vecs, w_out, *up.arrays, *deps)


def grad_rows_kernel(jb, lo, ls, ro, rs, *rest):
    rest[-1][0] = (dg(lo[...], ro[...], TN) + dg(ls[...], rs[...], TN)).astype(BF)


def grad_down(g_own, g_sib, df_own, df_sib, jb, nf, deps=()):
    n, hidden = g_own.shape
    width = df_own.shape[1]
    part = hidden // (2 * nf)
    left = pl.BlockSpec((n, part), lambda j, jb: (0, jb[j]))
    right = pl.BlockSpec((n, width), lambda j, jb: (0, 0))
    return pl.pallas_call(
        grad_rows_kernel,
        grid_spec=pltpu.PrefetchScalarGridSpec(
            num_scalar_prefetch=1,
            grid=(nf,),
            in_specs=[left, left, right, right] + [ANY] * len(deps),
            out_specs=pl.BlockSpec((1, part, width), lambda j, jb: (j, 0, 0)),
        ),
        out_shape=jax.ShapeDtypeStruct((nf, part, width), BF),
        compiler_params=params(),
        cost_estimate=cost(2 * n * hidden * width, 2 * n * hidden + 4 * n * width + hidden * width),
        name="grad_down",
    )(jb, g_own, g_sib, df_own, df_sib, *deps)


def grad_cols_kernel(nl, nr, nf, want_sum, *refs):
    los, lss = refs[1 : 1 + nl], refs[1 + nl : 1 + 2 * nl]
    ros, rss = refs[1 + 2 * nl : 1 + 2 * nl + nr], refs[1 + 2 * nl + nr : 1 + 2 * nl + 2 * nr]
    outs = refs[-3:-1] if want_sum else refs[-2:-1]
    lt = refs[-1]
    n, wide = los[0].shape
    part = nl * wide // nf

    @pl.when(pl.program_id(0) == 0)
    def _():
        for j in range(nl):
            lt[j * wide : (j + 1) * wide, 0:n] = los[j][...].T
            lt[j * wide : (j + 1) * wide, n : 2 * n] = lss[j][...].T

    left = lt[...]
    at = 0
    for k in range(nr):
        planes = ros[k].shape[0]
        for m in range(planes):
            both = jnp.concatenate([ros[k][m], rss[k][m]], 0)
            cols = both.shape[1]
            got = dg(left, both, NN).astype(BF)
            for j in range(nf):
                outs[0][j, :, at : at + cols] = got[j * part : (j + 1) * part]
            if want_sum:
                outs[1][:, at : at + cols] = jnp.broadcast_to(jnp.sum(both.astype(F32), 0, keepdims=True), (8, cols))
            at += cols


def grad_cols(l_own, l_sib, r_own, r_sib, jb, nf, block, name, want_sum=False, deps=(), into=None, at=0, total=None):
    n, width = l_own.shape
    part = width // (2 * nf)
    nr = len(r_own)
    steps = r_own[0].shape[2] // block
    planes = sum(r.shape[0] for r in r_own)
    here = planes * block
    assert steps == 1 or (nr == 1 and planes == 1)
    if part % LANES == 0:
        nl = nf
        lefts = [pl.BlockSpec((n, part), lambda i, jb, j=j: (0, jb[j])) for j in range(nf)]
    else:
        nl = 1
        pick = lambda z: z.reshape(n, 2 * nf, part)[:, jb].reshape(n, nf * part)
        l_own, l_sib = pick(l_own), pick(l_sib)
        lefts = [pl.BlockSpec((n, nf * part), lambda i, jb: (0, 0))]
    rights = [pl.BlockSpec((r.shape[0], n, block), lambda i, jb: (0, 0, i)) for r in r_own]
    shift = at // here
    out_specs = [pl.BlockSpec((nf, part, here), lambda i, jb: (0, 0, i + shift))]
    total = total or here * steps
    out_shape = [jax.ShapeDtypeStruct((nf, part, total), BF)]
    if want_sum:
        out_specs.append(pl.BlockSpec((8, here), lambda i, jb: (0, 0)))
        out_shape.append(jax.ShapeDtypeStruct((8, here), F32))
    alias = {}
    if into is not None:
        alias = {1 + 2 * nl + 2 * nr: 0}
        deps = (into,) + tuple(deps)
    return pl.pallas_call(
        functools.partial(grad_cols_kernel, nl, nr, nf, want_sum),
        grid_spec=pltpu.PrefetchScalarGridSpec(
            num_scalar_prefetch=1,
            grid=(steps,),
            in_specs=lefts * 2 + rights * 2 + [ANY] * len(deps),
            out_specs=out_specs,
            scratch_shapes=[pltpu.VMEM((nf * part, 2 * n), BF)],
        ),
        out_shape=out_shape,
        input_output_aliases=alias,
        compiler_params=params(),
        cost_estimate=cost(2 * n * width * here * steps, 4 * n * (here * steps + width // 2)),
        name=name,
    )(jb, *([l_own] * nl), *([l_sib] * nl), *r_own, *r_sib, *deps)


def input_kernel(got, part, groups, ids, dr_ref, *rest):
    n = len(got.arrays)
    d_refs, pieces = rest[:groups], rest[groups : groups + n]
    out_ref, wq, wk, wv, sems = rest[-5:]
    targets = qkv_targets(part, wq, wk, wv, None)

    @pl.when(pl.program_id(0) == 0)
    def _():
        moves = got.copies(pieces, ids, targets, sems)
        for c in moves:
            c.start()
        for c in moves:
            c.wait()

    total = dr_ref[...]
    for k, w in enumerate((wq, wk, wv)):
        d = jnp.concatenate([r[k] for r in d_refs], 1)
        total += dg(d, w[...], NT)
    out_ref[...] = total


def input_part(dr, grads, got, ids, nb, deps=(), block=256):
    n, width = dr.shape
    rows = pl.BlockSpec((block, width), lambda i, ids: (i, 0))
    three = lambda w: pl.BlockSpec((3, block, w), lambda i, ids: (0, i, 0))
    count = got.count(qkv_targets(width // nb, 0, 0, 0, None))
    return pl.pallas_call(
        functools.partial(input_kernel, got, width // nb, len(grads)),
        grid_spec=pltpu.PrefetchScalarGridSpec(
            num_scalar_prefetch=1,
            grid=(n // block,),
            in_specs=[rows] + [three(a.shape[2]) for a in grads] + [ANY] * (len(got.arrays) + len(deps)),
            out_specs=rows,
            scratch_shapes=[pltpu.VMEM((width, width), BF)] * 3 + [pltpu.SemaphoreType.DMA((count,))],
        ),
        out_shape=jax.ShapeDtypeStruct((n, width), F32),
        compiler_params=params(),
        cost_estimate=cost(6 * n * width * width, 14 * n * width + 6 * width * width),
        name="input_gradient",
    )(ids, dr, *grads, *got.arrays, *deps)


def add_low(a, b):
    return lax.optimization_barrier((a.astype(F32) + b.astype(F32)).astype(BF))


class Chain:
    def __init__(self, parts, nf, nr, extra=None):
        self.nf, self.nr, self.rows = nf, nr, parts.shape[1]
        self.extra = 0 if extra is None else extra.shape[1]
        self.bits = nf.bit_length() - 1
        a, b = parts[:, : self.rows // 2], parts[:, self.rows // 2 :]
        if extra is not None:
            a = jnp.concatenate([a, extra], 1)
        box = lambda z: z.reshape((2,) * self.bits + z.shape[1:])
        self.cur = [box(a), box(b)]
        self.axes = [list(range(self.bits - 1, -1, -1)) for _ in range(2)]
        self.level = 0

    def plane(self):
        for i in range(2):
            level = self.level if i == 0 else self.bits - 1 - self.level
            axes = self.axes[i]
            ax = axes[level]
            keep = lax.index_in_dim(self.cur[i], 0, ax, keepdims=False)
            send = lax.index_in_dim(self.cur[i], 1, ax, keepdims=False)
            self.cur[i] = add_low(keep, swap(send, "fsdp", self.nf, 1 << level))
            self.axes[i] = [z - (z > ax) for z in axes]
        self.level += 1
        return tuple(self.cur)

    def rest(self):
        while self.level < self.bits:
            self.plane()
        return self

    def cur_deps(self):
        return tuple(self.cur)

    def rep_first(self):
        v = jnp.concatenate([self.cur[1], self.cur[0]], 0)
        self.odd = (lax.axis_index("rep") & 1) == 1
        n = v.shape[0] // 2
        low, high = v[:n], v[n:]
        self.kept = add_low(jnp.where(self.odd, high, low), swap(jnp.where(self.odd, low, high), "rep", self.nr, 1))
        return (self.kept,)

    def rep_middle(self):
        xor = 2
        while xor < self.nr:
            self.kept = add_low(self.kept, swap(self.kept, "rep", self.nr, xor))
            xor *= 2
        return (self.kept,)

    def rep_last(self):
        self.other = swap(self.kept, "rep", self.nr, 1)
        return (self.other,)

    def result(self):
        v = jnp.concatenate([jnp.where(self.odd, self.other, self.kept), jnp.where(self.odd, self.kept, self.other)], 0)
        rows, cut = self.rows, self.rows - self.rows // 2
        main = jnp.concatenate([v[cut : cut + rows // 2], v[:cut]], 0).astype(F32)
        return main, v[rows:].astype(F32)


def body(tokens, segment_ids, padding, cotangent, w_query, w_key, w_value, w_out, b_query, b_value, b_out,
         gain_one, shift_one, w_up, b_up, w_down, b_down, gain_two, shift_two, *, nr, nf, ns):
    _, part_len, width = tokens.shape
    f, c = lax.axis_index("fsdp"), lax.axis_index("seq")
    rel = [((f ^ j) * 2 + (c ^ p)) for j in range(nf) for p in range(2)]
    absolute = [(j * 2 + (c ^ p)) for j in range(nf) for p in range(2)]
    ids = jnp.stack(rel + absolute).astype(jnp.int32)
    jb = jnp.stack(rel[::2]).astype(jnp.int32)
    jb_abs = jnp.stack(absolute[::2]).astype(jnp.int32)
    first_core = c == 0

    def both(x):
        y = swap(x, "seq", ns, 1)
        own = jnp.where(first_core, jnp.concatenate([x[0], y[0]]), jnp.concatenate([y[1], x[1]]))
        sib = jnp.where(first_core, jnp.concatenate([x[1], y[1]]), jnp.concatenate([y[0], x[0]]))
        return own, sib

    def unpair(z):
        low, high = z[:part_len], z[part_len:]
        mine, theirs = jnp.where(first_core, low, high), jnp.where(first_core, high, low)
        got = swap(theirs, "seq", ns, 1)
        return jnp.stack([jnp.where(first_core, mine, got), jnp.where(first_core, got, mine)])

    sib_of = lambda z: swap(z, "seq", ns, 1)

    nb = 2 * nf
    part = width // nb
    bias = pack_bias([b_query, b_value, b_out, gain_one, shift_one, b_down, gain_two, shift_two, b_up], width)
    total = 3 * part + BIAS_ROWS
    half = total // 2
    moves = []
    at = 0
    for src, rows in enumerate((part, part, part, BIAS_ROWS)):
        for side in range(2):
            lo, hi = max(at, side * half), min(at + rows, (side + 1) * half)
            if lo < hi:
                moves.append((src, lo - at, hi - lo, side, lo - side * half))
        at += rows
    qkv_halves = split_rows([w_query, w_key, w_value, bias], moves, [(half, width)] * 2, (), "pack_projections")
    first = gather_start(qkv_halves, nf)
    x, x_sib = both(tokens)
    marks, _ = both(jnp.stack([segment_ids, padding], -1))
    qf, kf = seg_features(marks[:, 0], marks[:, 1])
    far = gather_far(first, nf)
    got_qkv = gather_end(qkv_halves, first, far, nf, ns)
    gate = far if far else tuple(first["all"])
    h = part // 2
    up_halves = split_rows(
        [w_up, w_out, w_down],
        [(0, 0, h, 0, 0), (0, h, h, 1, 0), (1, 0, part, 2, 0), (2, 0, 4 * part, 3, 0)],
        [(h, 4 * width), (h, 4 * width), (part, width), (4 * part, width)],
        gate,
        "split_up",
    )
    first_up = gather_start(up_halves[:2], nf)
    full_out = lax.all_gather(up_halves[2], ("fsdp", "seq"), axis=0, tiled=True)
    full_down = lax.all_gather(up_halves[3], ("fsdp", "seq"), axis=0, tiled=True)
    q, k, v, vecs, bup = project(x, got_qkv, ids, nb)
    pairs = width // LANES
    groups = 4
    each = pairs // groups
    fwd = [attn_fwd(q, k, v, qf, kf, 0, each)]
    arrived = tuple(first_up.values()) if nf == 4 else tuple(first_up["all"])
    far_up = gather_far(first_up, nf)
    fwd.append(attn_fwd(q, k, v, qf, kf, each, each, (fwd[0][0],) + arrived))
    got_up = gather_end(up_halves[:2], first_up, far_up, nf, ns)
    fwd.append(attn_fwd(q, k, v, qf, kf, 2 * each, each, (fwd[1][0],)))
    fwd.append(attn_fwd(q, k, v, qf, kf, 3 * each, each, (fwd[2][0],) + tuple(far_up)))
    ct, _ = both(cotangent)
    a_all, y, yb, normed, inverse, g, gp = up_part(x, vecs, bup, [r[0] for r in fwd], full_out, got_up, ids, nb)
    a_sib, yb_sib, g_sib = sib_of(a_all), sib_of(yb), sib_of(g)
    out, df, dr, sums_two = down_part(g, y, ct, vecs, full_down)
    output = unpair(out)
    df_sib = sib_of(df)
    dh, sum_up = hidden_part(df, gp, full_down)
    dh_sib = sib_of(dh)
    g_down = grad_down(g, g_sib, df, df_sib, jb_abs, nf, (dh,))
    down_sum = lax.psum_scatter(g_down.reshape(nf * 4 * part, width), "fsdp", scatter_dimension=0, tiled=True)
    final_down = lax.psum(down_sum, "rep").astype(F32)
    dr1, do, da, sums_one = back_part(dh, dr, normed, inverse, vecs, full_out, got_up, ids, nb, (g_down,))
    do_sib = sib_of(do)
    (g_up,) = grad_cols(yb, yb_sib, [dh[None]], [dh_sib[None]], jb, nf, 512, "grad_up", deps=(da,), total=5 * width)
    (g_up,) = grad_cols(a_all, a_sib, [do[None]], [do_sib[None]], jb, nf, 512, "grad_out", into=g_up, at=4 * width, total=5 * width)
    chain_up = Chain(g_up, nf, nr)

    def back(i, deps):
        return attn_bwd(q, k, v, da, a_all, fwd[i][1], kf, i * each, each, deps)

    grads = [back(0, (g_up,))]
    sibs = [sib_of(grads[0])]
    grads.append(back(1, (grads[0],)))
    sibs.append(sib_of(grads[1]))
    grads.append(back(2, (grads[1],) + chain_up.plane()))
    sibs.append(sib_of(grads[2]))
    g_one, sum_one = grad_cols(x, x_sib, grads[:2], sibs[:2], jb, nf, each * LANES, "grad_qkv", True, (grads[2],) + chain_up.rest().cur_deps())
    chain_one = Chain(g_one, nf, nr)
    grads.append(back(3, (g_one,) + chain_up.rep_first()))
    sibs.append(sib_of(grads[3]))
    vec_sums = jnp.concatenate([sums_one[2:3], sums_one[0:2], sums_two[2:3], sums_two[0:2], sum_up.reshape(4, width)], 0)
    vec_sums = vec_sums + sib_of(vec_sums)
    deps = chain_one.plane() + chain_up.rep_middle()
    g_two, sum_two = grad_cols(x, x_sib, grads[2:], sibs[2:], jb, nf, each * LANES, "grad_qkv", True, (grads[3],) + deps)

    sums = jnp.concatenate([sum_one[0].reshape(2, 3, -1), sum_two[0].reshape(2, 3, -1)], 0)
    bq, bv = sums[:, 0].reshape(-1), sums[:, 2].reshape(-1)
    eight = jnp.concatenate([bq[None], bv[None], vec_sums[:6]], 0)
    by_block = jnp.concatenate(
        [eight.reshape(8, nb, part).transpose(1, 0, 2).reshape(nb, 8 * part), vec_sums[6:].reshape(nb, 4 * part)], 1
    )
    cols = g_two.shape[2]
    lines16 = -(-12 * part // (cols * 16)) * 16
    mine = jnp.pad(by_block[jb], ((0, 0), (0, lines16 * cols - 12 * part))).reshape(nf, lines16, cols).astype(BF)
    chain_two = Chain(g_two, nf, nr, mine)
    input_grad = unpair(input_part(dr1, grads, got_qkv, ids, nb, (g_two,)))
    chain_up.rep_last()
    chain_one.rest().rep_first()
    chain_one.rep_middle()
    chain_one.rep_last()
    chain_two.rest().rep_first()
    chain_two.rep_middle()
    chain_two.rep_last()
    both_up, _ = chain_up.result()
    final_up, final_out = both_up[:, : 4 * width], both_up[:, 4 * width :]
    one, _ = chain_one.result()
    two, small = chain_two.result()
    wide = each * LANES
    pieces = [z[:, (3 * i + m) * wide : (3 * i + m + 1) * wide] for m in range(3) for z in (one, two) for i in range(2)]
    final_q, final_k, final_v = (jnp.concatenate(pieces[4 * m : 4 * m + 4], 1) for m in range(3))
    small = small.reshape(-1)
    v8 = [small[i * part : (i + 1) * part] for i in range(8)]
    final_bup = small[8 * part : 12 * part]
    return (output, input_grad, final_q, final_k, final_v, final_out, v8[0], v8[1], v8[2], v8[3], v8[4],
            final_up, final_bup, final_down, v8[5], v8[6], v8[7])


def solution(mesh):
    tok = P(("rep", "fsdp"), "seq", None)
    ids = P(("rep", "fsdp"), "seq")
    mat = P(("fsdp", "seq"), None)
    vec = P(("fsdp", "seq"))
    sizes = mesh.shape
    return jax.shard_map(
        functools.partial(body, nr=sizes["rep"], nf=sizes["fsdp"], ns=sizes["seq"]),
        mesh=mesh,
        in_specs=(tok, ids, ids, tok) + (mat,) * 4 + (vec,) * 5 + (mat, vec, mat) + (vec,) * 3,
        out_specs=(tok, tok) + (mat,) * 4 + (vec,) * 5 + (mat, vec, mat) + (vec,) * 3,
        check_vma=False,
    )
```

```python
import functools
import math
import jax
import jax.numpy as jnp
from jax import lax
from jax.experimental import pallas as pl
from jax.experimental.pallas import tpu as pltpu
from jax.sharding import PartitionSpec as P

F32 = jnp.float32
BF = jnp.bfloat16
HEAD_DIM = 64
LANES = 128
EPSILON = 1e-05
ROOT_HALF = 0.7071067811865476
INV_ROOT_TAU = 0.3989422804014327
NT = (((1,), (1,)), ((), ()))
TN = (((0,), (0,)), ((), ()))
NN = (((1,), (0,)), ((), ()))
VMEM = 58 << 20
ANY = pl.BlockSpec(memory_space=pl.ANY)


def dg(a, b, dims):
    return lax.dot_general(a, b, dims, preferred_element_type=F32)


def params(limit=VMEM):
    return pltpu.CompilerParams(vmem_limit_bytes=limit)


def cost(flops, bytes_accessed, trans=0):
    return pl.CostEstimate(flops=flops, bytes_accessed=bytes_accessed, transcendentals=trans)


def swap(x, axis, size, xor):
    return lax.ppermute(x, axis, [(i, i ^ xor) for i in range(size)])


class Gathered:
    def __init__(self, arrays, entries, half):
        self.arrays, self.entries, self.half = arrays, entries, half

    def copies(self, refs, ids, targets, sems):
        out = []
        for which, index, base, half, slot in self.entries:
            low = half * self.half
            for first, rows, dest, stride, offset in targets:
                a, b = max(first, low), min(first + rows, low + self.half)
                if a >= b:
                    continue
                src = refs[which].at[(*index, pl.ds(base + a - low, b - a))]
                start = pl.multiple_of(ids[slot] * stride + (offset + a - first), 16)
                out.append(pltpu.make_async_copy(src, dest.at[pl.ds(start, b - a)], sems.at[len(out)]))
        return out

    def count(self, targets):
        n = 0
        for _, _, _, half, _ in self.entries:
            low = half * self.half
            n += sum(max(t[0], low) < min(t[0] + t[1], low + self.half) for t in targets)
        return n


def gather_start(shard, nf):
    if nf == 4:
        return [swap(shard, "fsdp", nf, 1), swap(shard, "fsdp", nf, 2)]
    return [lax.all_gather(shard, "fsdp", axis=0)]


def gather_far(first, nf):
    if nf == 4:
        half = first[0].shape[0] // 2
        return [swap(first[0][:half], "fsdp", nf, 2), swap(first[1][half:], "fsdp", nf, 1)]
    return []


def gather_end(shard, first, far, nf, ns):
    half = shard.shape[0] // 2
    if nf == 4:
        arrays = [shard, *first, *far]
        entries = [(w, (), h * half, h, 2 * w) for w in range(3) for h in range(2)]
        entries += [(3, (), 0, 0, 6), (4, (), 0, 1, 6)]
    else:
        arrays = list(first)
        entries = [(0, (f,), h * half, h, 2 * nf + 2 * f) for f in range(nf) for h in range(2)]
    n = len(arrays)
    arrays = arrays + [swap(a, "seq", ns, 1) for a in arrays]
    entries = entries + [(w + n, i, r, h, s + 1) for w, i, r, h, s in entries]
    return Gathered(arrays, entries, half)


BIAS_ROWS = 32


def split_kernel(moves, nin, nout, *refs):
    ins, outs, sems = refs[:nin], refs[len(refs) - nout - 1 : -1], refs[-1]
    copies = [
        pltpu.make_async_copy(ins[s].at[pl.ds(first, rows)], outs[d].at[pl.ds(to, rows)], sems.at[i])
        for i, (s, first, rows, d, to) in enumerate(moves)
    ]
    for m in copies:
        m.start()
    for m in copies:
        m.wait()


def split_rows(ins, moves, out_shapes, deps, name):
    return pl.pallas_call(
        functools.partial(split_kernel, moves, len(ins), len(out_shapes)),
        in_specs=[ANY] * (len(ins) + len(deps)),
        out_specs=[pl.BlockSpec(memory_space=pltpu.VMEM)] * len(out_shapes),
        out_shape=[jax.ShapeDtypeStruct(o, BF) for o in out_shapes],
        scratch_shapes=[pltpu.SemaphoreType.DMA((len(moves),))],
        compiler_params=params(),
        name=name,
    )(*ins, *deps)


def bias_kernel(nvec, *refs):
    vecs, out, tile = refs[:nvec], refs[nvec], refs[nvec + 1]
    part = vecs[0].shape[-1]
    tile[...] = jnp.zeros_like(tile)
    for i in range(8):
        tile[0:1, i * part : (i + 1) * part] = vecs[i][...].astype(F32).reshape(1, part)
    tile[1:2, 0 : 4 * part] = vecs[8][...].astype(F32).reshape(1, 4 * part)
    out[...] = tile[...].astype(BF)


def pack_bias(vecs, width):
    return pl.pallas_call(
        functools.partial(bias_kernel, len(vecs)),
        in_specs=[pl.BlockSpec(memory_space=pltpu.VMEM)] * len(vecs),
        out_specs=pl.BlockSpec(memory_space=pltpu.VMEM),
        out_shape=jax.ShapeDtypeStruct((BIAS_ROWS, width), BF),
        scratch_shapes=[pltpu.VMEM((BIAS_ROWS, width), F32)],
        compiler_params=params(4 << 20),
        name="pack_bias",
    )(*vecs)


def pair_kernel(count, core, *refs):
    ins, outs, sems = refs[: 2 * len(count)], refs[len(refs) - 1 - sum(count) : -1], refs[-1]
    c = core[0]
    at, moves = 0, []
    for i, n in enumerate(count):
        mine, theirs = ins[2 * i], ins[2 * i + 1]
        half = mine.shape[1]
        for k in range(n):
            which = c if k == 0 else 1 - c
            for src, place in ((mine, c), (theirs, 1 - c)):
                start = pl.multiple_of(place * half, half)
                moves.append(pltpu.make_async_copy(src.at[which], outs[at].at[pl.ds(start, half)], sems.at[len(moves)]))
            at += 1
    for m in moves:
        m.start()
    for m in moves:
        m.wait()


def pair_up(core, items, deps=()):
    count = [n for _, _, n in items]
    flat = [z for a, b, _ in items for z in (a, b)]
    shapes = [jax.ShapeDtypeStruct((2 * a.shape[1], a.shape[2]), a.dtype) for a, _, n in items for _ in range(n)]
    return pl.pallas_call(
        functools.partial(pair_kernel, count),
        grid_spec=pltpu.PrefetchScalarGridSpec(
            num_scalar_prefetch=1,
            grid=(1,),
            in_specs=[ANY] * (len(flat) + len(deps)),
            out_specs=[pl.BlockSpec(z.shape, lambda i, core: (0, 0)) for z in shapes],
            scratch_shapes=[pltpu.SemaphoreType.DMA((2 * len(shapes),))],
        ),
        out_shape=shapes,
        compiler_params=params(),
        name="pair_up",
    )(core, *flat, *deps)


def unpair_kernel(core, own, theirs, *rest):
    out, sems = rest[-2:]
    c = core[0]
    half = out.shape[1]
    start = pl.multiple_of(c * half, half)
    cut = lambda z: z.at[pl.ds(start, half)] if z.shape[0] > half else z
    one = pltpu.make_async_copy(cut(own), out.at[c], sems.at[0])
    two = pltpu.make_async_copy(cut(theirs), out.at[1 - c], sems.at[1])
    one.start()
    two.start()
    one.wait()
    two.wait()


def unpair_up(core, own, theirs, half, deps=()):
    width = own.shape[1]
    return pl.pallas_call(
        unpair_kernel,
        grid_spec=pltpu.PrefetchScalarGridSpec(
            num_scalar_prefetch=1,
            grid=(1,),
            in_specs=[ANY] * (2 + len(deps)),
            out_specs=pl.BlockSpec((2, half, width), lambda i, core: (0, 0, 0)),
            scratch_shapes=[pltpu.SemaphoreType.DMA((2,))],
        ),
        out_shape=jax.ShapeDtypeStruct((2, half, width), own.dtype),
        compiler_params=params(),
        name="unpair",
    )(core, own, theirs, *deps)


def qkv_kernel(got, ids, x_ref, *rest):
    n = len(got.arrays)
    pieces, (q_ref, k_ref, v_ref, p_ref, b_ref, wq, wk, wv, wb, sems) = rest[:n], rest[-10:]
    width = x_ref.shape[1]
    nb = wb.shape[0] // BIAS_ROWS
    part = width // nb
    targets = qkv_targets(part, wq, wk, wv, wb)

    @pl.when(pl.program_id(0) == 0)
    def _():
        moves = got.copies(pieces, ids, targets, sems)
        for m in moves:
            m.start()
        for m in moves:
            m.wait()
        for b in range(nb):
            rows = wb[b * BIAS_ROWS : b * BIAS_ROWS + 16, :].astype(F32)
            for vec in range(8):
                p_ref[vec : vec + 1, b * part : (b + 1) * part] = rows[0:1, vec * part : (vec + 1) * part]
            b_ref[0:1, b * 4 * part : (b + 1) * 4 * part] = rows[1:2, 0 : 4 * part]

    x = x_ref[...]
    q_ref[...] = (dg(x, wq[...], NN) + p_ref[0:1, :]).astype(BF)
    k_ref[...] = dg(x, wk[...], NN).astype(BF)
    v_ref[...] = (dg(x, wv[...], NN) + p_ref[1:2, :]).astype(BF)


def qkv_targets(part, wq, wk, wv, wb):
    t = [(0, part, wq, part, 0), (part, part, wk, part, 0), (2 * part, part, wv, part, 0)]
    if wb is not None:
        t.append((3 * part, BIAS_ROWS, wb, BIAS_ROWS, 0))
    return t


def project(x, got, ids, nb, deps=(), block=256):
    n, width = x.shape
    grid = n // block
    rows = pl.BlockSpec((block, width), lambda i, ids: (i, 0))
    whole = lambda shape: pl.BlockSpec(shape, lambda i, ids: (0, 0))
    count = got.count(qkv_targets(width // nb, 0, 0, 0, 0))
    return pl.pallas_call(
        functools.partial(qkv_kernel, got),
        grid_spec=pltpu.PrefetchScalarGridSpec(
            num_scalar_prefetch=1,
            grid=(grid,),
            in_specs=[rows] + [ANY] * (len(got.arrays) + len(deps)),
            out_specs=[rows, rows, rows, whole((8, width)), whole((1, 4 * width))],
            scratch_shapes=[pltpu.VMEM((width, width), BF)] * 3
            + [pltpu.VMEM((nb * BIAS_ROWS, width), BF), pltpu.SemaphoreType.DMA((count,))],
        ),
        out_shape=[jax.ShapeDtypeStruct((n, width), BF)] * 3
        + [jax.ShapeDtypeStruct((8, width), F32), jax.ShapeDtypeStruct((1, 4 * width), F32)],
        compiler_params=params(),
        cost_estimate=cost(6 * n * width * width, 2 * n * width * 4 + 6 * width * width),
        name="project",
    )(ids, x, *got.arrays, *deps)


def split3(v):
    hi=v.astype(BF); r=v-hi.astype(F32); mid=r.astype(BF); lo=(r-mid.astype(F32)).astype(BF)
    return hi,mid,lo
def attn_fwd_kernel(qb, q_ref,k_ref,v_ref,qf_ref,kf_ref,*rest):
    a_ref,lf_ref=rest[-2:]
    n=q_ref.shape[0]
    lane=lax.broadcasted_iota(jnp.int32,(n,LANES),1)
    left=lane<HEAD_DIM
    q=q_ref[...]*jnp.asarray(0.125,BF); k=k_ref[...]; v=v_ref[...]
    qf=qf_ref[...]; kf=kf_ref[...]
    one=jnp.ones_like(v)
    sides=[]
    for h in range(2):
        own=left if h==0 else ~left
        sides.append((jnp.where(own,q,qf),jnp.where(own,k,kf),jnp.where(own,v,one)))
    lq=lax.broadcasted_iota(jnp.int32,(qb,LANES),1)
    leftq=lq<HEAD_DIM
    for c in range(n//qb):
        rows=slice(c*qb,(c+1)*qb)
        res=[]; lse=[]
        for h in range(2):
            qa,ka,va=sides[h]
            s=dg(qa[rows],ka,NT)
            m=jnp.max(s,-1,keepdims=True)
            p=jnp.exp(s-m).astype(BF)
            o=dg(p,va,NN)
            tot=o[:,64:65] if h==0 else o[:,0:1]
            res.append(o/tot)
            lse.append(m+jnp.log(tot))
        a_ref[rows,:]=jnp.where(leftq,res[0],res[1]).astype(BF)
        lm=jnp.where(leftq,lse[1],lse[0])
        hi,mid,lo=split3(lm)
        j=lq%HEAD_DIM
        base=qf[rows]
        lf_ref[rows,:]=jnp.where(j==4,hi,jnp.where(j==5,mid,jnp.where(j==6,lo,base)))
def attn_fwd(q,k,v,qf,kf,first,npair,deps=(),qb=512):
    n=q.shape[0]
    blk=pl.BlockSpec((n,LANES),lambda i:(0,i+first))
    whole=pl.BlockSpec((n,LANES),lambda i:(0,0))
    out=pl.BlockSpec((n,LANES),lambda i:(0,i))
    return pl.pallas_call(functools.partial(attn_fwd_kernel,qb),grid=(npair,),
        in_specs=[blk,blk,blk,whole,whole]+[ANY]*len(deps),out_specs=[out,out],
        out_shape=[jax.ShapeDtypeStruct((n,npair*LANES),BF)]*2,
        compiler_params=pltpu.CompilerParams(vmem_limit_bytes=50<<20),
        cost_estimate=pl.CostEstimate(flops=npair*2*2*2*n*n*256,bytes_accessed=npair*n*LANES*2*5,transcendentals=npair*2*n*n),
        name="attend_forward")(q,k,v,qf,kf,*deps)
def attn_bwd_kernel(qb,q_ref,k_ref,v_ref,da_ref,a_ref,lf_ref,kf_ref,*rest):
    d_ref,s_ref,dka,dva=rest[-4:]
    n=q_ref.shape[0]
    lane=lax.broadcasted_iota(jnp.int32,(n,LANES),1)
    left=lane<HEAD_DIM
    q=q_ref[...]*jnp.asarray(0.125,BF); k=k_ref[...]; v=v_ref[...]; da=da_ref[...]
    lf=lf_ref[...]; kf=kf_ref[...]
    prod=da.astype(F32)*a_ref[...].astype(F32)
    j=lane%HEAD_DIM
    zero=jnp.zeros_like(q)
    minus=jnp.where((j>=4)&(j<7),jnp.asarray(-1,BF),jnp.asarray(0,BF))
    sides=[]
    for h in range(2):
        own=left if h==0 else ~left
        d=jnp.sum(jnp.where(own,prod,0.0),-1,keepdims=True)
        hi,mid,lo=split3(d)
        df=jnp.where(j==4,hi,jnp.where(j==5,mid,jnp.where(j==6,lo,zero)))
        sides.append((jnp.where(own,q,lf),jnp.where(own,k,kf),jnp.where(own,v,minus),jnp.where(own,da,df),
                      jnp.where(own,q,zero),jnp.where(own,da,zero)))
    kt=k.T
    sq=jnp.zeros((1,LANES),F32)
    for c in range(n//qb):
        rows=slice(c*qb,(c+1)*qb)
        dqs=[]; dk=None; dv=None
        for h in range(2):
            qa,ka,va,daa,qz,daz=sides[h]
            s=dg(ka,qa[rows],NT)
            p=jnp.exp(s)
            dp=dg(va,daa[rows],NT)
            ds=(p*dp).astype(BF)
            pb=p.astype(BF)
            x=dg(pb,daz[rows],NN); dv=x if dv is None else dv+x
            y=dg(ds,qz[rows],NN); dk=y if dk is None else dk+y
            dqs.append(dg(kt[h*64:(h+1)*64],ds,NN))
        dqb=(jnp.concatenate(dqs,0).T*0.125).astype(BF)
        d_ref[0,rows,:]=dqb
        sq=sq+jnp.sum(dqb.astype(F32),0,keepdims=True)
        if c==0: dka[...]=dk; dva[...]=dv
        else: dka[...]+=dk; dva[...]+=dv
    d_ref[1]=dka[...].astype(BF)
    dvb=dva[...].astype(BF)
    d_ref[2]=dvb
    s_ref[0:1,:]=sq
    s_ref[1:2,:]=jnp.sum(dvb.astype(F32),0,keepdims=True)
def attn_bwd(q,k,v,da,a,lf,kf,first,npair,deps=(),qb=256):
    n=q.shape[0]
    blk=pl.BlockSpec((n,LANES),lambda i:(0,i+first))
    whole=pl.BlockSpec((n,LANES),lambda i:(0,0))
    own=pl.BlockSpec((n,LANES),lambda i:(0,i))
    out=pl.BlockSpec((3,n,LANES),lambda i:(0,0,i))
    return pl.pallas_call(functools.partial(attn_bwd_kernel,qb),grid=(npair,),
        in_specs=[blk]*5+[own,whole]+[ANY]*len(deps),out_specs=[out,pl.BlockSpec((8,LANES),lambda i:(0,i))],
        out_shape=[jax.ShapeDtypeStruct((3,n,npair*LANES),BF),jax.ShapeDtypeStruct((8,npair*LANES),F32)],
        scratch_shapes=[pltpu.VMEM((n,LANES),F32)]*2,
        compiler_params=pltpu.CompilerParams(vmem_limit_bytes=50<<20),
        cost_estimate=pl.CostEstimate(flops=npair*2*5*2*n*n*256,bytes_accessed=npair*n*LANES*2*9,transcendentals=npair*2*n*n),
        name="attend_backward")(q,k,v,da,a,lf,kf,*deps)
def seg_features(seg,pad):
    n=seg.shape[0]
    j=lax.broadcasted_iota(jnp.int32,(n,LANES),1)%HEAD_DIM
    same=(seg[:,None]==j)
    qf=jnp.where((j<4)&same,1.0,0.0).astype(BF)
    kf=jnp.where(j<4,jnp.where(same&(pad[:,None]>0),0.0,-1e30),jnp.where(j<7,-1.0,0.0)).astype(BF)
    return qf,kf


def up_kernel(got, part, ids, x_ref, p_ref, bup_ref, *rest):
    n = len(got.arrays)
    *a_refs, wo = rest[: len(rest) - n - 9]
    pieces = rest[len(rest) - n - 9 : len(rest) - 9]
    a_all, y_ref, yb_ref, n_ref, s_ref, g_ref, gp_ref, wu, sems = rest[-9:]
    width = x_ref.shape[1]
    targets = [(0, part, wu, part, 0)]

    @pl.when(pl.program_id(0) == 0)
    def _():
        for m in got.copies(pieces, ids, targets, sems):
            m.start()

    a = jnp.concatenate([r[...] for r in a_refs], 1)
    a_all[...] = a
    r = x_ref[...].astype(F32) + dg(a, wo[...], NN) + p_ref[2:3, :]
    c = r - jnp.mean(r, -1, keepdims=True)
    s = lax.rsqrt(jnp.mean(c * c, -1, keepdims=True) + EPSILON)
    normed = c * s
    y = normed * p_ref[3:4, :] + p_ref[4:5, :]
    y_ref[...] = y
    n_ref[...] = normed.astype(BF)
    s_ref[...] = s
    yb = y.astype(BF)
    yb_ref[...] = yb

    @pl.when(pl.program_id(0) == 0)
    def _():
        for m in got.copies(pieces, ids, targets, sems):
            m.wait()

    step = 512
    for k in range(0, 4 * width, step):
        h = dg(yb, wu[:, k : k + step], NN) + bup_ref[:, k : k + step]
        phi = 0.5 + 0.5 * lax.erf(h * ROOT_HALF)
        g_ref[:, k : k + step] = (h * phi).astype(BF)
        gp_ref[:, k : k + step] = (phi + h * (jnp.exp(-0.5 * h * h) * INV_ROOT_TAU)).astype(BF)


def up_part(x, vecs, bup, a_parts, w_out, got, ids, nb, block=256):
    n, width = x.shape
    part = width // nb
    rows = lambda w: pl.BlockSpec((block, w), lambda i, ids: (i, 0))
    whole = lambda shape: pl.BlockSpec(shape, lambda i, ids: (0, 0))
    count = got.count([(0, part, 0, 0, 0)])
    sds = jax.ShapeDtypeStruct
    return pl.pallas_call(
        functools.partial(up_kernel, got, part),
        grid_spec=pltpu.PrefetchScalarGridSpec(
            num_scalar_prefetch=1,
            grid=(n // block,),
            in_specs=[rows(width), whole((8, width)), whole((1, 4 * width))]
            + [rows(a.shape[1]) for a in a_parts]
            + [whole((width, width))]
            + [ANY] * len(got.arrays),
            out_specs=[rows(width), rows(width), rows(width), rows(width), rows(1), rows(4 * width), rows(4 * width)],
            scratch_shapes=[pltpu.VMEM((width, 4 * width), BF), pltpu.SemaphoreType.DMA((count,))],
        ),
        out_shape=[
            sds((n, width), BF),
            sds((n, width), F32),
            sds((n, width), BF),
            sds((n, width), BF),
            sds((n, 1), F32),
            sds((n, 4 * width), BF),
            sds((n, 4 * width), BF),
        ],
        compiler_params=params(),
        cost_estimate=cost(10 * n * width * width, 28 * n * width + 10 * width * width, 8 * n * width),
        name="out_norm_up",
    )(ids, x, vecs, bup, *a_parts, w_out, *got.arrays)


def down_kernel(g_ref, y_ref, c_ref, p_ref, wd, o_ref, df_ref, dr_ref, sum_ref):
    @pl.when(pl.program_id(0) == 0)
    def _():
        sum_ref[...] = jnp.zeros_like(sum_ref)

    r = y_ref[...] + dg(g_ref[...], wd[...], NN) + p_ref[5:6, :]
    c = r - jnp.mean(r, -1, keepdims=True)
    s = lax.rsqrt(jnp.mean(c * c, -1, keepdims=True) + EPSILON)
    normed = c * s
    gain = p_ref[6:7, :]
    o_ref[...] = (normed * gain + p_ref[7:8, :]).astype(BF)
    ct = c_ref[...].astype(F32)
    e = ct * gain
    dr = s * (e - jnp.mean(e, -1, keepdims=True) - normed * jnp.mean(e * normed, -1, keepdims=True))
    dr_ref[...] = dr
    df = dr.astype(BF)
    df_ref[...] = df
    sum_ref[0:1, :] += jnp.sum(ct * normed, 0, keepdims=True)
    sum_ref[1:2, :] += jnp.sum(ct, 0, keepdims=True)
    sum_ref[2:3, :] += jnp.sum(df.astype(F32), 0, keepdims=True)


def down_part(g, y, ct, vecs, w_down, block=256):
    n, width = y.shape
    rows = lambda w: pl.BlockSpec((block, w), lambda i: (i, 0))
    whole = lambda shape: pl.BlockSpec(shape, lambda i: (0, 0))
    sds = jax.ShapeDtypeStruct
    return pl.pallas_call(
        down_kernel,
        grid=(n // block,),
        in_specs=[rows(4 * width), rows(width), rows(width), whole((8, width)), whole((4 * width, width))],
        out_specs=[rows(width), rows(width), rows(width), whole((8, width))],
        out_shape=[sds((n, width), BF), sds((n, width), BF), sds((n, width), F32), sds((8, width), F32)],
        compiler_params=params(),
        cost_estimate=cost(8 * n * width * width, 22 * n * width + 8 * width * width),
        name="down_norm",
    )(g, y, ct, vecs, w_down)


def hidden_kernel(df_ref, gp_ref, wd, dh_ref, bup_ref):
    @pl.when(pl.program_id(0) == 0)
    def _():
        bup_ref[...] = jnp.zeros_like(bup_ref)

    df = df_ref[...]
    step = 512
    for k in range(0, dh_ref.shape[1], step):
        dh = (dg(df, wd[k : k + step, :], NT) * gp_ref[:, k : k + step].astype(F32)).astype(BF)
        dh_ref[:, k : k + step] = dh
        bup_ref[:, k : k + step] += jnp.sum(dh.astype(F32), 0, keepdims=True)


def hidden_part(df, gp, w_down, block=256):
    n, width = df.shape
    rows = lambda w: pl.BlockSpec((block, w), lambda i: (i, 0))
    whole = lambda shape: pl.BlockSpec(shape, lambda i: (0, 0))
    return pl.pallas_call(
        hidden_kernel,
        grid=(n // block,),
        in_specs=[rows(width), rows(4 * width), whole((4 * width, width))],
        out_specs=[rows(4 * width), whole((1, 4 * width))],
        out_shape=[jax.ShapeDtypeStruct((n, 4 * width), BF), jax.ShapeDtypeStruct((1, 4 * width), F32)],
        compiler_params=params(),
        cost_estimate=cost(8 * n * width * width, 18 * n * width + 8 * width * width),
        name="hidden_gradient",
    )(df, gp, w_down)


def back_kernel(up, part, ids, dh_ref, dr_ref, n_ref, s_ref, p_ref, wo, *rest):
    nu = len(up.arrays)
    pu = rest[:nu]
    dr1_ref, do_ref, da_ref, sum_ref, wu, su = rest[-6:]
    tu = [(0, part, wu, part, 0)]

    @pl.when(pl.program_id(0) == 0)
    def _():
        moves = up.copies(pu, ids, tu, su)
        for m in moves:
            m.start()
        sum_ref[...] = jnp.zeros_like(sum_ref)
        for m in moves:
            m.wait()

    dy = dr_ref[...] + dg(dh_ref[...], wu[...], NT)
    normed = n_ref[...].astype(F32)
    e = dy * p_ref[3:4, :]
    dr = s_ref[...] * (e - jnp.mean(e, -1, keepdims=True) - normed * jnp.mean(e * normed, -1, keepdims=True))
    dr1_ref[...] = dr
    do = dr.astype(BF)
    do_ref[...] = do
    da_ref[...] = dg(do, wo[...], NT).astype(BF)
    sum_ref[0:1, :] += jnp.sum(dy * normed, 0, keepdims=True)
    sum_ref[1:2, :] += jnp.sum(dy, 0, keepdims=True)
    sum_ref[2:3, :] += jnp.sum(do.astype(F32), 0, keepdims=True)


def back_part(dh, dr, normed, inverse, vecs, w_out, up, ids, nb, deps=(), block=256):
    n, width = dr.shape
    part = width // nb
    rows = lambda w: pl.BlockSpec((block, w), lambda i, ids: (i, 0))
    whole = lambda shape: pl.BlockSpec(shape, lambda i, ids: (0, 0))
    sds = jax.ShapeDtypeStruct
    return pl.pallas_call(
        functools.partial(back_kernel, up, part),
        grid_spec=pltpu.PrefetchScalarGridSpec(
            num_scalar_prefetch=1,
            grid=(n // block,),
            in_specs=[rows(4 * width), rows(width), rows(width), rows(1), whole((8, width)), whole((width, width))]
            + [ANY] * (len(up.arrays) + len(deps)),
            out_specs=[rows(width), rows(width), rows(width), whole((8, width))],
            scratch_shapes=[pltpu.VMEM((width, 4 * width), BF), pltpu.SemaphoreType.DMA((up.count([(0, part, 0, 0, 0)]),))],
        ),
        out_shape=[sds((n, width), F32), sds((n, width), BF), sds((n, width), BF), sds((8, width), F32)],
        compiler_params=params(),
        cost_estimate=cost(10 * n * width * width, 22 * n * width + 10 * width * width),
        name="norm_backward",
    )(ids, dh, dr, normed, inverse, vecs, w_out, *up.arrays, *deps)


def grad_rows_kernel(jb, lo, ls, ro, rs, *rest):
    rest[-1][0] = (dg(lo[...], ro[...], TN) + dg(ls[...], rs[...], TN)).astype(BF)


def grad_down(g_own, g_sib, df_own, df_sib, jb, nf, deps=()):
    n, hidden = g_own.shape
    width = df_own.shape[1]
    part = hidden // (2 * nf)
    left = pl.BlockSpec((n, part), lambda j, jb: (0, jb[j]))
    right = pl.BlockSpec((n, width), lambda j, jb: (0, 0))
    return pl.pallas_call(
        grad_rows_kernel,
        grid_spec=pltpu.PrefetchScalarGridSpec(
            num_scalar_prefetch=1,
            grid=(nf,),
            in_specs=[left, left, right, right] + [ANY] * len(deps),
            out_specs=pl.BlockSpec((1, part, width), lambda j, jb: (j, 0, 0)),
        ),
        out_shape=jax.ShapeDtypeStruct((nf, part, width), BF),
        compiler_params=params(),
        cost_estimate=cost(2 * n * hidden * width, 2 * n * hidden + 4 * n * width + hidden * width),
        name="grad_down",
    )(jb, g_own, g_sib, df_own, df_sib, *deps)


class Job:
    def __init__(self, left, rights):
        self.left, self.rights = left, rights


def grad_cols_kernel(jobs, nl, nf, block, keeps, *refs):
    pos = 1
    step = pl.program_id(0)
    lefts, rights = [], []
    for spans in jobs:
        lefts.append((refs[pos : pos + nl], refs[pos + nl : pos + 2 * nl]))
        pos += 2 * nl
    for spans in jobs:
        for _ in spans:
            rights.append((refs[pos], refs[pos + 1]))
            pos += 2
    outs = refs[len(refs) - len(jobs) - 4 : len(refs) - len(jobs)]
    lts = refs[len(refs) - len(jobs) :]
    n, wide = lefts[0][0][0].shape
    part = nl * wide // nf
    half = part // 2
    at = 0
    for (los, lss), spans, lt in zip(lefts, jobs, lts):

        @pl.when(step == spans[0][0])
        def _():
            for j in range(nl):
                lt[j * wide : (j + 1) * wide, 0:n] = los[j][...].T
                lt[j * wide : (j + 1) * wide, n : 2 * n] = lss[j][...].T

        for begin, count in spans:
            own, sib = rights[at]
            at += 1

            @pl.when((step >= begin) & (step < begin + count))
            def _():
                both = jnp.concatenate([own[0], sib[0]], 0)
                got = dg(lt[...], both, NN).astype(BF)
                for out, (which, side) in zip(outs, keeps):
                    for m, j in enumerate(which):
                        out[m, 0:half, :] = got[j * part + side * half : j * part + (side + 1) * half]


def grad_cols(jobs, jb, nf, block, name, deps=()):
    n, width = jobs[0].left[0].shape
    part = width // (2 * nf)
    spans, step = [], 0
    in_specs, operands, right_specs, right_ops = [], [], [], []
    for job in jobs:
        mine = []
        pick = lambda z: z.reshape(n, 2 * nf, part)[:, jb].reshape(n, nf * part)
        for z in job.left:
            if part % LANES == 0:
                nl = nf
                in_specs += [pl.BlockSpec((n, part), lambda i, jb, j=j: (0, jb[j])) for j in range(nf)]
                operands += [z] * nf
            else:
                nl = 1
                in_specs += [pl.BlockSpec((n, nf * part), lambda i, jb: (0, 0))]
                operands += [pick(z)]
        for own, sib in job.rights:
            planes, _, cols = own.shape
            per = cols // block
            count = planes * per

            def at(i, jb, step=step, count=count, per=per):
                k = jnp.clip(i - step, 0, count - 1)
                return (k // per, 0, k % per)

            right_specs += [pl.BlockSpec((1, n, block), at)] * 2
            right_ops += [own, sib]
            mine.append((step, count))
            step += count
        spans.append(mine)
    half = part // 2
    js = list(range(nf))
    top = nf // 2
    keeps = [([j for j in js if not j & 1], 0), ([j for j in js if j & 1], 0), ([j for j in js if j < top], 1), ([j for j in js if j >= top], 1)]
    out_spec = pl.BlockSpec((nf // 2, half, block), lambda i, jb: (0, 0, i))
    out_shape = jax.ShapeDtypeStruct((nf // 2, half, step * block), BF)
    return pl.pallas_call(
        functools.partial(grad_cols_kernel, spans, nl, nf, block, keeps),
        grid_spec=pltpu.PrefetchScalarGridSpec(
            num_scalar_prefetch=1,
            grid=(step,),
            in_specs=in_specs + right_specs + [ANY] * len(deps),
            out_specs=[out_spec] * 4,
            scratch_shapes=[pltpu.VMEM((nf * part, 2 * n), BF)] * len(jobs),
        ),
        out_shape=[out_shape] * 4,
        compiler_params=params(),
        cost_estimate=cost(2 * n * width * step * block, 4 * n * (step * block + width // 2)),
        name=name,
    )(jb, *operands, *right_ops, *deps)


def input_kernel(got, part, groups, place, ids, dr_ref, *rest):
    n = len(got.arrays)
    d_refs, pieces = rest[1 : 1 + groups], rest[1 + groups : 1 + groups + n]
    out_ref, wq, wk, wv, sems = rest[-5:]
    targets = qkv_targets(part, wq, wk, wv, None)

    @pl.when(pl.program_id(0) == 0)
    def _():
        moves = got.copies(pieces, ids, targets, sems)
        for c in moves:
            c.start()
        for c in moves:
            c.wait()

    total = dr_ref[...]
    for k, w in enumerate((wq, wk, wv)):
        d = jnp.concatenate([r[k] for r in d_refs], 1)
        total += dg(d, w[...], NT)
    out_ref[...] = total


def input_part(dr, grads, got, ids, place, nb, deps=(), block=256):
    n, width = dr.shape
    steps = n // 2 // block
    rows = pl.BlockSpec((block, width), lambda i, ids: (i + ids[ids.shape[0] - 2 + place] * steps, 0))
    three = lambda w: pl.BlockSpec((3, block, w), lambda i, ids: (0, i + ids[ids.shape[0] - 2 + place] * steps, 0))
    count = got.count(qkv_targets(width // nb, 0, 0, 0, None))
    return pl.pallas_call(
        functools.partial(input_kernel, got, width // nb, len(grads), place),
        grid_spec=pltpu.PrefetchScalarGridSpec(
            num_scalar_prefetch=1,
            grid=(steps,),
            in_specs=[rows, ANY] + [three(a.shape[2]) for a in grads] + [ANY] * (len(got.arrays) + len(deps)),
            out_specs=pl.BlockSpec((block, width), lambda i, ids: (i, 0)),
            scratch_shapes=[pltpu.VMEM((width, width), BF)] * 3 + [pltpu.SemaphoreType.DMA((count,))],
        ),
        out_shape=jax.ShapeDtypeStruct((n // 2, width), F32),
        compiler_params=params(),
        cost_estimate=cost(3 * n * width * width, 7 * n * width + 6 * width * width),
        name="input_gradient",
    )(ids, dr, dr, *grads, *got.arrays, *deps)


def add_low(a, b):
    return lax.optimization_barrier((a.astype(F32) + b.astype(F32)).astype(BF))


def stage_kernel(last, odd, ka, ra, kb, rb, *outs):
    add = lambda a, b: (a[...].astype(F32) + b[...].astype(F32)).astype(BF)
    a, b = add(ka, ra), add(kb, rb)
    m = a.shape[0]
    if last:
        swapped = odd[0] == 1
        outs[0][...] = jnp.where(swapped, b, a)
        outs[1][...] = jnp.where(swapped, a, b)
    else:
        for i in range(m // 2):
            outs[0][i], outs[1][i] = a[2 * i], a[2 * i + 1]
            outs[2][i], outs[3][i] = b[i], b[m // 2 + i]


def stage(odd, ka, ra, kb, rb, name, block=512):
    m, rows, cols = ka.shape
    block = min(block, cols)
    while cols % block:
        block //= 2
    last = m == 1
    into = pl.BlockSpec((m, rows, block), lambda i, odd: (0, 0, i))
    mo = max(m // 2, 1)
    out = pl.BlockSpec((mo, rows, block), lambda i, odd: (0, 0, i))
    return pl.pallas_call(
        functools.partial(stage_kernel, last),
        grid_spec=pltpu.PrefetchScalarGridSpec(
            num_scalar_prefetch=1,
            grid=(cols // block,),
            in_specs=[into] * 4,
            out_specs=[out] * (2 if last else 4),
        ),
        out_shape=[jax.ShapeDtypeStruct((mo, rows, cols), BF)] * (2 if last else 4),
        compiler_params=params(16 << 20),
        cost_estimate=cost(0, 12 * m * rows * cols),
        name=name,
    )(odd, ka, ra, kb, rb)


class Chain:
    def __init__(self, parts, nf, nr, odd):
        self.nf, self.nr, self.odd = nf, nr, odd
        self.ka, self.sa, self.kb, self.sb = parts
        self.level, self.bits = 0, nf.bit_length() - 1

    def plane(self):
        a, b = self.level, self.bits - 1 - self.level
        ra, rb = swap(self.sa, "fsdp", self.nf, 1 << a), swap(self.sb, "fsdp", self.nf, 1 << b)
        self.level += 1
        out = stage(self.odd, self.ka, ra, self.kb, rb, "sum_plane")
        if self.level == self.bits:
            self.kept, self.sent = out[0][0], out[1][0]
        else:
            self.ka, self.sa, self.kb, self.sb = out
        return tuple(out)

    def kept_deps(self):
        return (self.kept,)

    def rest(self):
        out = ()
        while self.level < self.bits:
            out = self.plane()
        return out

    def rep_first(self):
        self.kept = add_low(self.kept, swap(self.sent, "rep", self.nr, 1))
        return (self.kept,)

    def rep_middle(self):
        xor = 2
        while xor < self.nr:
            self.kept = add_low(self.kept, swap(self.kept, "rep", self.nr, xor))
            xor *= 2
        return (self.kept,)

    def rep_last(self):
        self.other = swap(self.kept, "rep", self.nr, 1)
        return (self.other,)

    def result(self):
        odd = self.odd[0] == 1
        return jnp.concatenate([jnp.where(odd, self.other, self.kept), jnp.where(odd, self.kept, self.other)], 0).astype(F32)


def body(tokens, segment_ids, padding, cotangent, w_query, w_key, w_value, w_out, b_query, b_value, b_out,
         gain_one, shift_one, w_up, b_up, w_down, b_down, gain_two, shift_two, *, nr, nf, ns):
    _, part_len, width = tokens.shape
    f, c = lax.axis_index("fsdp"), lax.axis_index("seq")
    rel = [((f ^ j) * 2 + (c ^ p)) for j in range(nf) for p in range(2)]
    absolute = [(j * 2 + (c ^ p)) for j in range(nf) for p in range(2)]
    ids = jnp.stack(rel + absolute + [1 - c, c]).astype(jnp.int32)
    jb = jnp.stack(rel[::2]).astype(jnp.int32)
    jb_abs = jnp.stack(absolute[::2]).astype(jnp.int32)
    core = c.astype(jnp.int32).reshape(1)
    odd = (lax.axis_index("rep") & 1).astype(jnp.int32).reshape(1)
    sib_of = lambda z: swap(z, "seq", ns, 1)
    nb = 2 * nf
    part = width // nb

    bias = pack_bias([b_query, b_value, b_out, gain_one, shift_one, b_down, gain_two, shift_two, b_up], width)
    moves, at = [], 0
    for src, rows in enumerate((part, part, part, BIAS_ROWS)):
        moves.append((src, 0, rows, 0, at))
        at += rows
    (qkv_shard,) = split_rows([w_query, w_key, w_value, bias], moves, [(at, width)], (), "pack_projections")
    first = gather_start(qkv_shard, nf)
    x, x_sib, ct = pair_up(core, [(tokens, sib_of(tokens), 2), (cotangent, sib_of(cotangent), 1)])
    marks = jnp.stack([segment_ids, padding])
    theirs = sib_of(marks)
    own = c == 0
    mine_m, their_m = jnp.where(own, marks[:, 0], marks[:, 1]), jnp.where(own, theirs[:, 0], theirs[:, 1])
    whole = jnp.where(own, jnp.concatenate([mine_m, their_m], 1), jnp.concatenate([their_m, mine_m], 1))
    qf, kf = seg_features(whole[0], whole[1])
    far = gather_far(first, nf)
    got_qkv = gather_end(qkv_shard, first, far, nf, ns)
    up_shard, out_shard, down_shard = split_rows(
        [w_up, w_out, w_down],
        [(0, 0, part, 0, 0), (1, 0, part, 1, 0), (2, 0, 4 * part, 2, 0)],
        [w_up.shape, w_out.shape, w_down.shape],
        (x, ct, qf, kf) + tuple(first) + tuple(far),
        "hold_weights",
    )
    full_out = lax.all_gather(out_shard, ("fsdp", "seq"), axis=0, tiled=True)
    full_down = lax.all_gather(down_shard, ("fsdp", "seq"), axis=0, tiled=True)
    first_up = gather_start(up_shard, nf)
    q, k, v, vecs, bup = project(x, got_qkv, ids, nb)

    pairs = width // LANES
    groups = 4
    each = pairs // groups
    fwd = [attn_fwd(q, k, v, qf, kf, 0, each)]
    fwd.append(attn_fwd(q, k, v, qf, kf, each, each, (fwd[0][0],)))
    far_up = gather_far(first_up, nf)
    got_up = gather_end(up_shard, first_up, far_up, nf, ns)
    fwd.append(attn_fwd(q, k, v, qf, kf, 2 * each, each, (fwd[1][0],) + tuple(first_up)))
    fwd.append(attn_fwd(q, k, v, qf, kf, 3 * each, each, (fwd[2][0],)))

    a_all, y, yb, normed, inverse, g, gp = up_part(x, vecs, bup, [r[0] for r in fwd], full_out, got_up, ids, nb)
    a_sib, yb_sib, g_sib = sib_of(a_all), sib_of(yb), sib_of(g)
    out, df, dr, sums_two = down_part(g, y, ct, vecs, full_down)
    df_sib = sib_of(df)
    dh, sum_up = hidden_part(df, gp, full_down)
    dh_sib = sib_of(dh)
    out_sib = sib_of(out)
    g_down = grad_down(g, g_sib, df, df_sib, jb_abs, nf, (dh,))
    down_sum = lax.psum_scatter(g_down.reshape(nf * 4 * part, width), "fsdp", scatter_dimension=0, tiled=True)
    final_down = lax.psum(down_sum, "rep").astype(F32)
    g_up = grad_cols([Job((yb, yb_sib), [(dh[None], dh_sib[None])])], jb, nf, 512, "grad_up", (g_down,))
    chain_up = Chain(g_up, nf, nr, odd)
    dr1, do, da, sums_one = back_part(dh, dr, normed, inverse, vecs, full_out, got_up, ids, nb, (g_up[0],))
    do_sib = sib_of(do)
    output = unpair_up(core, out, out_sib, part_len, (da,))
    vec_sums = jnp.concatenate([sums_one[2:3], sums_one[0:2], sums_two[2:3], sums_two[0:2], sum_up.reshape(4, width)], 0)
    vec_sib = sib_of(vec_sums)

    def back(i, deps):
        return attn_bwd(q, k, v, da, a_all, fwd[i][1], kf, i * each, each, deps)

    grads, sums, sibs = [], [], []

    def run(i, deps):
        d, sm = back(i, deps)
        grads.append(d)
        sums.append(sm)
        sibs.append(sib_of(d))

    run(0, (output,))
    run(1, (grads[0],) + chain_up.plane())
    run(2, (grads[1],) + chain_up.rest())
    g_one = grad_cols(
        [Job((a_all, a_sib), [(do[None], do_sib[None])]), Job((x, x_sib), [(grads[0], sibs[0]), (grads[1], sibs[1])])],
        jb, nf, 256, "grad_out_qkv", (grads[2],) + chain_up.rep_first(),
    )
    chain_one = Chain(g_one, nf, nr, odd)
    run(3, (grads[2], g_one[0]))
    chain_up.rep_middle()
    g_two = grad_cols(
        [Job((x, x_sib), [(grads[2], sibs[2]), (grads[3], sibs[3])])], jb, nf, 256, "grad_qkv", (grads[3],) + chain_one.plane()
    )
    bqv = jnp.concatenate([sm[:2] for sm in sums], 1)
    bqv = bqv + sib_of(bqv)
    vec_sums = vec_sums + vec_sib
    eight = jnp.concatenate([bqv, vec_sums[:6]], 0)
    small = jnp.concatenate([eight, vec_sums[6:].reshape(8, width // 2)], 1)
    rows = 16
    small = jnp.pad(small, ((0, rows - 8), (0, 0))).astype(BF)
    small = jnp.broadcast_to(small[None], (nf // 2,) + small.shape)
    g_two = [jnp.concatenate([z, small], 1) for z in g_two]
    chain_two = Chain(g_two, nf, nr, odd)
    send_half = input_part(dr1, grads, got_qkv, ids, 0, nb, (g_two[0],) + chain_up.kept_deps())
    their_half = sib_of(send_half)
    keep_half = input_part(dr1, grads, got_qkv, ids, 1, nb, (send_half,) + chain_two.plane() + chain_one.rest())
    chain_up.rep_last()
    chain_one.rep_first()
    chain_one.rep_middle()
    chain_one.rep_last()
    chain_two.rest()
    chain_two.rep_first()
    chain_two.rep_middle()
    chain_two.rep_last()
    input_grad = unpair_up(core, keep_half, their_half, part_len)
    final_up = chain_up.result()
    one = chain_one.result()
    two = chain_two.result()
    half = part // 2
    small = two[half : half + 8]
    two = jnp.concatenate([two[:half], two[half + rows : 2 * half + rows]], 0)
    final_out = one[:, :width]
    wide = each * LANES
    third = [one[:, width + k * wide : width + (k + 1) * wide] for k in range(6)] + [two[:, k * wide : (k + 1) * wide] for k in range(6)]
    final_q, final_k, final_v = (jnp.concatenate([third[3 * i + m] for i in range(4)], 1) for m in range(3))
    own_block = 2 * f + c
    v8 = lax.dynamic_slice(small[:, :width], (0, own_block * part), (8, part))
    final_bup = lax.dynamic_slice(small[:, width:].reshape(-1), (own_block * 4 * part,), (4 * part,))
    return (output, input_grad, final_q, final_k, final_v, final_out, v8[0], v8[1], v8[2], v8[3], v8[4],
            final_up, final_bup, final_down, v8[5], v8[6], v8[7])


def solution(mesh):
    tok = P(("rep", "fsdp"), "seq", None)
    ids = P(("rep", "fsdp"), "seq")
    mat = P(("fsdp", "seq"), None)
    vec = P(("fsdp", "seq"))
    sizes = mesh.shape
    return jax.shard_map(
        functools.partial(body, nr=sizes["rep"], nf=sizes["fsdp"], ns=sizes["seq"]),
        mesh=mesh,
        in_specs=(tok, ids, ids, tok) + (mat,) * 4 + (vec,) * 5 + (mat, vec, mat) + (vec,) * 3,
        out_specs=(tok, tok) + (mat,) * 4 + (vec,) * 5 + (mat, vec, mat) + (vec,) * 3,
        check_vma=False,
    )
```

```python
import functools
import math
import jax
import jax.numpy as jnp
from jax import lax
from jax.experimental import pallas as pl
from jax.experimental.pallas import tpu as pltpu
from jax.sharding import PartitionSpec as P

F32 = jnp.float32
BF = jnp.bfloat16
HEAD_DIM = 64
LANES = 128
EPSILON = 1e-05
ROOT_HALF = 0.7071067811865476
INV_ROOT_TAU = 0.3989422804014327
NT = (((1,), (1,)), ((), ()))
TN = (((0,), (0,)), ((), ()))
NN = (((1,), (0,)), ((), ()))
VMEM = 48 << 20
FULL = 58 << 20
SHRINK = 1
ANY = pl.BlockSpec(memory_space=pl.ANY)


def dg(a, b, dims):
    return lax.dot_general(a, b, dims, preferred_element_type=F32)


def params(limit=VMEM):
    return pltpu.CompilerParams(vmem_limit_bytes=limit)


def cost(flops, bytes_accessed, trans=0):
    return pl.CostEstimate(flops=flops // SHRINK, bytes_accessed=bytes_accessed // SHRINK, transcendentals=trans // SHRINK)


def swap(x, axis, size, xor):
    return lax.ppermute(x, axis, [(i, i ^ xor) for i in range(size)])


def after(x, *deps):
    return lax.optimization_barrier((x,) + deps)[0]


class Gathered:
    def __init__(self, arrays, entries, half):
        self.arrays, self.entries, self.half = arrays, entries, half

    def copies(self, refs, ids, targets, sems):
        out = []
        for which, index, base, half, slot in self.entries:
            low = half * self.half
            for first, rows, dest, stride, offset, *column in targets:
                a, b = max(first, low), min(first + rows, low + self.half)
                if a >= b:
                    continue
                place = (*index, pl.ds(base + a - low, b - a))
                if column:
                    place += (pl.ds(column[0], dest.shape[1]),)
                src = refs[which].at[place]
                start = pl.multiple_of(ids[slot] * stride + (offset + a - first), 16)
                out.append(pltpu.make_async_copy(src, dest.at[pl.ds(start, b - a)], sems.at[len(out)]))
        return out

    def count(self, targets):
        n = 0
        for _, _, _, half, _ in self.entries:
            low = half * self.half
            n += sum(max(t[0], low) < min(t[0] + t[1], low + self.half) for t in targets)
        return n


def gather_start(shard, nf):
    if nf == 4:
        return [swap(shard, "fsdp", nf, 1), swap(shard, "fsdp", nf, 2)]
    return [lax.all_gather(shard, "fsdp", axis=0)]


def gather_far(first, nf, deps=()):
    if nf == 4:
        half = first[0].shape[0] // 2
        shape = (half, first[0].shape[1])
        one, two = split_rows(first, [(0, 0, half, 0, 0, 0), (1, half, half, 1, 0, 0)], [shape, shape], deps, "cut_halves")
        return [swap(one, "fsdp", nf, 2), swap(two, "fsdp", nf, 1)]
    return []


def gather_end(shard, first, far, nf, ns, late=()):
    half = shard.shape[0] // 2
    if nf == 4:
        arrays = [shard, *first, *far]
        entries = [(w, (), h * half, h, 2 * w) for w in range(3) for h in range(2)]
        entries += [(3, (), 0, 0, 6), (4, (), 0, 1, 6)]
    else:
        arrays = list(first)
        entries = [(0, (f,), h * half, h, 2 * nf + 2 * f) for f in range(nf) for h in range(2)]
    n = len(arrays)
    swaps = [swap(a, "seq", ns, 1) for a in arrays[: n - len(far)]]
    swaps += [swap(after(a, *late), "seq", ns, 1) for a in arrays[n - len(far) :]]
    arrays = arrays + swaps
    entries = entries + [(w + n, i, r, h, s + 1) for w, i, r, h, s in entries]
    return Gathered(arrays, entries, half), swaps


BIAS_ROWS = 32


def split_kernel(moves, nin, nout, *refs):
    ins, outs, sems = refs[:nin], refs[len(refs) - nout - 1 : -1], refs[-1]
    copies = [
        pltpu.make_async_copy(ins[s].at[pl.ds(first, rows)], outs[d].at[pl.ds(to, rows), pl.ds(col, ins[s].shape[1])], sems.at[i])
        for i, (s, first, rows, d, to, col) in enumerate(moves)
    ]
    for m in copies:
        m.start()
    for m in copies:
        m.wait()


def split_rows(ins, moves, out_shapes, deps, name):
    return pl.pallas_call(
        functools.partial(split_kernel, moves, len(ins), len(out_shapes)),
        in_specs=[ANY] * (len(ins) + len(deps)),
        out_specs=[pl.BlockSpec(memory_space=pltpu.VMEM)] * len(out_shapes),
        out_shape=[jax.ShapeDtypeStruct(o, BF) for o in out_shapes],
        scratch_shapes=[pltpu.SemaphoreType.DMA((len(moves),))],
        compiler_params=params(58 << 20),
        cost_estimate=cost(0, 1 << 20),
        name=name,
    )(*ins, *deps)


def bias_kernel(nvec, *refs):
    vecs, mats, out = refs[:nvec], refs[nvec : nvec + 3], refs[nvec + 3]
    held, tile, sems = refs[nvec + 4 : 2 * nvec + 4], refs[-2], refs[-1]
    part = mats[0].shape[0]
    moves = [pltpu.make_async_copy(m, out.at[pl.ds(i * part, part)], sems.at[i]) for i, m in enumerate(mats)]
    small = [pltpu.make_async_copy(v, h, sems.at[3 + i]) for i, (v, h) in enumerate(zip(vecs, held))]
    for m in small + moves:
        m.start()
    tile[...] = jnp.zeros_like(tile)
    for m in small:
        m.wait()
    for i in range(8):
        tile[0:1, i * part : (i + 1) * part] = held[i][...].astype(F32).reshape(1, part)
    tile[1:2, 0 : 4 * part] = held[8][...].astype(F32).reshape(1, 4 * part)
    out[3 * part :, :] = tile[...].astype(BF)
    for m in moves:
        m.wait()


def pack_first(vecs, mats):
    part, width = mats[0].shape
    n = len(vecs)
    return pl.pallas_call(
        functools.partial(bias_kernel, n),
        in_specs=[ANY] * (n + 3),
        out_specs=pl.BlockSpec(memory_space=pltpu.VMEM),
        out_shape=jax.ShapeDtypeStruct((3 * part + BIAS_ROWS, width), BF),
        scratch_shapes=[pltpu.VMEM(v.shape, BF) for v in vecs] + [pltpu.VMEM((BIAS_ROWS, width), F32), pltpu.SemaphoreType.DMA((n + 3,))],
        compiler_params=params(58 << 20),
        cost_estimate=cost(0, 1 << 20),
        name="pack_first",
    )(*vecs, *mats)


def pair_kernel(count, core, *refs):
    ins, outs, sems = refs[: 2 * len(count)], refs[len(refs) - 1 - sum(count) : -1], refs[-1]
    c = core[0]
    at, moves = 0, []
    for i, n in enumerate(count):
        mine, theirs = ins[2 * i], ins[2 * i + 1]
        half = mine.shape[1]
        for k in range(n):
            which = c if k == 0 else 1 - c
            for src, place in ((mine, c), (theirs, 1 - c)):
                start = pl.multiple_of(place * half, half)
                moves.append(pltpu.make_async_copy(src.at[which], outs[at].at[pl.ds(start, half)], sems.at[len(moves)]))
            at += 1
    for m in moves:
        m.start()
    for m in moves:
        m.wait()


def pair_up(core, items, deps=()):
    count = [n for _, _, n in items]
    flat = [z for a, b, _ in items for z in (a, b)]
    shapes = [jax.ShapeDtypeStruct((2 * a.shape[1], a.shape[2]), a.dtype) for a, _, n in items for _ in range(n)]
    return pl.pallas_call(
        functools.partial(pair_kernel, count),
        grid_spec=pltpu.PrefetchScalarGridSpec(
            num_scalar_prefetch=1,
            grid=(1,),
            in_specs=[ANY] * (len(flat) + len(deps)),
            out_specs=[pl.BlockSpec(z.shape, lambda i, core: (0, 0)) for z in shapes],
            scratch_shapes=[pltpu.SemaphoreType.DMA((2 * len(shapes),))],
        ),
        out_shape=shapes,
        compiler_params=params(58 << 20),
        cost_estimate=cost(0, 1 << 20),
        name="pair_up",
    )(core, *flat, *deps)


def unpair_kernel(core, own, theirs, *rest):
    out, sems = rest[-2:]
    c = core[0]
    half = out.shape[1]
    start = pl.multiple_of(c * half, half)
    cut = lambda z: z.at[pl.ds(start, half)] if z.shape[0] > half else z
    one = pltpu.make_async_copy(cut(own), out.at[c], sems.at[0])
    two = pltpu.make_async_copy(cut(theirs), out.at[1 - c], sems.at[1])
    one.start()
    two.start()
    one.wait()
    two.wait()


def unpair_up(core, own, theirs, half, deps=()):
    width = own.shape[1]
    return pl.pallas_call(
        unpair_kernel,
        grid_spec=pltpu.PrefetchScalarGridSpec(
            num_scalar_prefetch=1,
            grid=(1,),
            in_specs=[ANY] * (2 + len(deps)),
            out_specs=pl.BlockSpec((2, half, width), lambda i, core: (0, 0, 0)),
            scratch_shapes=[pltpu.SemaphoreType.DMA((2,))],
        ),
        out_shape=jax.ShapeDtypeStruct((2, half, width), own.dtype),
        compiler_params=params(58 << 20),
        cost_estimate=cost(0, 1 << 20),
        name="unpair",
    )(core, own, theirs, *deps)


def qkv_kernel(got, ids, x_ref, *rest):
    n = len(got.arrays)
    pieces = rest[:n]
    q_ref, k_ref, v_ref, p_ref, b_ref, wq, wk, wv, wb, sems = rest[-10:]
    width = x_ref.shape[1]
    nb = wb.shape[0] // BIAS_ROWS
    part = width // nb
    targets = qkv_targets(part, wq, wk, wv, wb)

    @pl.when(pl.program_id(0) == 0)
    def _():
        moves = got.copies(pieces, ids, targets, sems)
        for m in moves:
            m.start()
        for m in moves:
            m.wait()
        for b in range(nb):
            rows = wb[b * BIAS_ROWS : b * BIAS_ROWS + 16, :].astype(F32)
            for vec in range(8):
                p_ref[vec : vec + 1, b * part : (b + 1) * part] = rows[0:1, vec * part : (vec + 1) * part]
            b_ref[0:1, b * 4 * part : (b + 1) * 4 * part] = rows[1:2, 0 : 4 * part]

    x = x_ref[...]
    q_ref[...] = (dg(x, wq[...], NN) + p_ref[0:1, :]).astype(BF)
    k_ref[...] = dg(x, wk[...], NN).astype(BF)
    v_ref[...] = (dg(x, wv[...], NN) + p_ref[1:2, :]).astype(BF)


def qkv_targets(part, wq, wk, wv, wb=None):
    t = [(0, part, wq, part, 0), (part, part, wk, part, 0), (2 * part, part, wv, part, 0)]
    return t if wb is None else t + [(3 * part, BIAS_ROWS, wb, BIAS_ROWS, 0)]


def project(x, got, ids, nb, deps=(), block=256):
    n, width = x.shape
    grid = n // block
    rows = pl.BlockSpec((block, width), lambda i, ids: (i, 0))
    whole = lambda shape: pl.BlockSpec(shape, lambda i, ids: (0, 0))
    count = got.count(qkv_targets(width // nb, 0, 0, 0, 0))
    return pl.pallas_call(
        functools.partial(qkv_kernel, got),
        grid_spec=pltpu.PrefetchScalarGridSpec(
            num_scalar_prefetch=1,
            grid=(grid,),
            in_specs=[rows] + [ANY] * (len(got.arrays) + len(deps)),
            out_specs=[rows, rows, rows, whole((8, width)), whole((1, 4 * width))],
            scratch_shapes=[pltpu.VMEM((width, width), BF)] * 3
            + [pltpu.VMEM((nb * BIAS_ROWS, width), BF), pltpu.SemaphoreType.DMA((count,))],
        ),
        out_shape=[jax.ShapeDtypeStruct((n, width), BF)] * 3
        + [jax.ShapeDtypeStruct((8, width), F32), jax.ShapeDtypeStruct((1, 4 * width), F32)],
        compiler_params=params(FULL),
        cost_estimate=cost(6 * n * width * width, 2 * n * width * 4 + 6 * width * width),
        name="project",
    )(ids, x, *got.arrays, *deps)


def split3(v):
    hi=v.astype(BF); r=v-hi.astype(F32); mid=r.astype(BF); lo=(r-mid.astype(F32)).astype(BF)
    return hi,mid,lo
def attn_fwd_kernel(qb, q_ref,k_ref,v_ref,qf_ref,kf_ref,*rest):
    a_ref,lf_ref=rest[-2:]
    n=q_ref.shape[0]
    lane=lax.broadcasted_iota(jnp.int32,(n,LANES),1)
    left=lane<HEAD_DIM
    q=q_ref[...]*jnp.asarray(0.125,BF); k=k_ref[...]; v=v_ref[...]
    qf=qf_ref[...]; kf=kf_ref[...]
    one=jnp.ones_like(v)
    sides=[]
    for h in range(2):
        own=left if h==0 else ~left
        sides.append((jnp.where(own,q,qf),jnp.where(own,k,kf),jnp.where(own,v,one)))
    lq=lax.broadcasted_iota(jnp.int32,(qb,LANES),1)
    leftq=lq<HEAD_DIM
    for c in range(n//qb):
        rows=slice(c*qb,(c+1)*qb)
        res=[]; lse=[]
        for h in range(2):
            qa,ka,va=sides[h]
            s=dg(qa[rows],ka,NT)
            m=jnp.max(s,-1,keepdims=True)
            p=jnp.exp(s-m).astype(BF)
            o=dg(p,va,NN)
            tot=o[:,64:65] if h==0 else o[:,0:1]
            res.append(o/tot)
            lse.append(m+jnp.log(tot))
        a_ref[rows,:]=jnp.where(leftq,res[0],res[1]).astype(BF)
        lm=jnp.where(leftq,lse[1],lse[0])
        hi,mid,lo=split3(lm)
        j=lq%HEAD_DIM
        base=qf[rows]
        lf_ref[rows,:]=jnp.where(j==4,hi,jnp.where(j==5,mid,jnp.where(j==6,lo,base)))
def attn_fwd(q,k,v,qf,kf,first,npair,deps=(),qb=512):
    n=q.shape[0]
    blk=pl.BlockSpec((n,LANES),lambda i:(0,i+first))
    whole=pl.BlockSpec((n,LANES),lambda i:(0,0))
    out=pl.BlockSpec((n,LANES),lambda i:(0,i))
    return pl.pallas_call(functools.partial(attn_fwd_kernel,qb),grid=(npair,),
        in_specs=[blk,blk,blk,whole,whole]+[ANY]*len(deps),out_specs=[out,out],
        out_shape=[jax.ShapeDtypeStruct((n,npair*LANES),BF)]*2,
        compiler_params=pltpu.CompilerParams(vmem_limit_bytes=VMEM),
        cost_estimate=cost(npair*2*2*2*n*n*256,npair*n*LANES*2*5),
        name="attend_forward")(q,k,v,qf,kf,*deps)
def attn_bwd_kernel(qb,q_ref,k_ref,v_ref,da_ref,a_ref,lf_ref,kf_ref,*rest):
    d_ref,dka,dva=rest[-3:]
    n=q_ref.shape[0]
    lane=lax.broadcasted_iota(jnp.int32,(n,LANES),1)
    left=lane<HEAD_DIM
    q=q_ref[...]*jnp.asarray(0.125,BF); k=k_ref[...]; v=v_ref[...]; da=da_ref[...]
    lf=lf_ref[...]; kf=kf_ref[...]
    prod=da.astype(F32)*a_ref[...].astype(F32)
    j=lane%HEAD_DIM
    zero=jnp.zeros_like(q)
    minus=jnp.where((j>=4)&(j<7),jnp.asarray(-1,BF),jnp.asarray(0,BF))
    sides=[]
    for h in range(2):
        own=left if h==0 else ~left
        d=jnp.sum(jnp.where(own,prod,0.0),-1,keepdims=True)
        hi,mid,lo=split3(d)
        df=jnp.where(j==4,hi,jnp.where(j==5,mid,jnp.where(j==6,lo,zero)))
        sides.append((jnp.where(own,q,lf),jnp.where(own,k,kf),jnp.where(own,v,minus),jnp.where(own,da,df),
                      jnp.where(own,q,zero),jnp.where(own,da,zero)))
    kt=k.T
    for c in range(n//qb):
        rows=slice(c*qb,(c+1)*qb)
        dqs=[]; dk=None; dv=None
        for h in range(2):
            qa,ka,va,daa,qz,daz=sides[h]
            s=dg(ka,qa[rows],NT)
            p=jnp.exp(s)
            dp=dg(va,daa[rows],NT)
            ds=(p*dp).astype(BF)
            pb=p.astype(BF)
            x=dg(pb,daz[rows],NN); dv=x if dv is None else dv+x
            y=dg(ds,qz[rows],NN); dk=y if dk is None else dk+y
            dqs.append(dg(kt[h*64:(h+1)*64],ds,NN))
        d_ref[0,rows,:]=(jnp.concatenate(dqs,0).T*0.125).astype(BF)
        if c==0: dka[...]=dk; dva[...]=dv
        else: dka[...]+=dk; dva[...]+=dv
    d_ref[1]=dka[...].astype(BF)
    d_ref[2]=dva[...].astype(BF)
def attn_bwd(q,k,v,da,a,lf,kf,first,npair,skip=0,deps=(),qb=256):
    n=q.shape[0]
    blk=pl.BlockSpec((n,LANES),lambda i:(0,i+first))
    whole=pl.BlockSpec((n,LANES),lambda i:(0,0))
    own=pl.BlockSpec((n,LANES),lambda i:(0,i+skip))
    out=pl.BlockSpec((3,n,LANES),lambda i:(0,0,i))
    return pl.pallas_call(functools.partial(attn_bwd_kernel,qb),grid=(npair,),
        in_specs=[blk]*5+[own,whole]+[ANY]*len(deps),out_specs=out,
        out_shape=jax.ShapeDtypeStruct((3,n,npair*LANES),BF),
        scratch_shapes=[pltpu.VMEM((n,LANES),F32)]*2,
        compiler_params=pltpu.CompilerParams(vmem_limit_bytes=VMEM),
        cost_estimate=cost(npair*2*5*2*n*n*256,npair*n*LANES*2*9),
        name="attend_backward")(q,k,v,da,a,lf,kf,*deps)
def seg_features(seg,pad):
    n=seg.shape[0]
    j=lax.broadcasted_iota(jnp.int32,(n,LANES),1)%HEAD_DIM
    same=(seg[:,None]==j)
    qf=jnp.where((j<4)&same,1.0,0.0).astype(BF)
    kf=jnp.where(j<4,jnp.where(same&(pad[:,None]>0),0.0,-1e30),jnp.where(j<7,-1.0,0.0)).astype(BF)
    return qf,kf


def up_kernel(got, part, ids, x_ref, p_ref, bup_ref, *rest):
    n = len(got.arrays)
    a_refs = rest[: len(rest) - n - 11]
    pieces = rest[len(rest) - n - 11 : len(rest) - 11]
    a_all, y_ref, yb_ref, n_ref, s_ref, g_ref, gp_ref, wu, wo, sems, sems_out = rest[-11:]
    width = x_ref.shape[1]
    targets = [(0, part, wu, part, 0, 0)]

    @pl.when(pl.program_id(0) == 0)
    def _():
        moves = got.copies(pieces, ids, [(0, part, wo, part, 0, 4 * width)], sems_out)
        for m in moves + got.copies(pieces, ids, targets, sems):
            m.start()
        for m in moves:
            m.wait()

    a = jnp.concatenate([r[...] for r in a_refs], 1)
    a_all[...] = a
    r = x_ref[...].astype(F32) + dg(a, wo[...], NN) + p_ref[2:3, :]
    c = r - jnp.mean(r, -1, keepdims=True)
    s = lax.rsqrt(jnp.mean(c * c, -1, keepdims=True) + EPSILON)
    normed = c * s
    y = normed * p_ref[3:4, :] + p_ref[4:5, :]
    y_ref[...] = y
    n_ref[...] = normed.astype(BF)
    s_ref[...] = s
    yb = y.astype(BF)
    yb_ref[...] = yb

    @pl.when(pl.program_id(0) == 0)
    def _():
        for m in got.copies(pieces, ids, targets, sems):
            m.wait()

    step = 512
    for k in range(0, 4 * width, step):
        h = dg(yb, wu[:, k : k + step], NN) + bup_ref[:, k : k + step]
        phi = 0.5 + 0.5 * lax.erf(h * ROOT_HALF)
        g_ref[:, k : k + step] = (h * phi).astype(BF)
        gp_ref[:, k : k + step] = (phi + h * (jnp.exp(-0.5 * h * h) * INV_ROOT_TAU)).astype(BF)


def up_part(x, vecs, bup, a_parts, got, ids, nb, block=256):
    n, width = x.shape
    part = width // nb
    rows = lambda w: pl.BlockSpec((block, w), lambda i, ids: (i, 0))
    whole = lambda shape: pl.BlockSpec(shape, lambda i, ids: (0, 0))
    count = got.count([(0, part, 0, 0, 0)])
    sds = jax.ShapeDtypeStruct
    return pl.pallas_call(
        functools.partial(up_kernel, got, part),
        grid_spec=pltpu.PrefetchScalarGridSpec(
            num_scalar_prefetch=1,
            grid=(n // block,),
            in_specs=[rows(width), whole((8, width)), whole((1, 4 * width))]
            + [rows(a.shape[1]) for a in a_parts]
            + [ANY] * len(got.arrays),
            out_specs=[rows(width), rows(width), rows(width), rows(width), rows(1), rows(4 * width), rows(4 * width)],
            scratch_shapes=[pltpu.VMEM((width, 4 * width), BF), pltpu.VMEM((width, width), BF)] + [pltpu.SemaphoreType.DMA((count,))] * 2,
        ),
        out_shape=[
            sds((n, width), BF),
            sds((n, width), F32),
            sds((n, width), BF),
            sds((n, width), BF),
            sds((n, 1), F32),
            sds((n, 4 * width), BF),
            sds((n, 4 * width), BF),
        ],
        compiler_params=params(FULL),
        cost_estimate=cost(10 * n * width * width, 28 * n * width + 10 * width * width, 8 * n * width),
        name="out_norm_up",
    )(ids, x, vecs, bup, *a_parts, *got.arrays)


def down_kernel(g_ref, y_ref, c_ref, p_ref, wd, o_ref, df_ref, dr_ref, sum_ref):
    @pl.when(pl.program_id(0) == 0)
    def _():
        sum_ref[...] = jnp.zeros_like(sum_ref)

    r = y_ref[...] + dg(g_ref[...], wd[...], NN) + p_ref[5:6, :]
    c = r - jnp.mean(r, -1, keepdims=True)
    s = lax.rsqrt(jnp.mean(c * c, -1, keepdims=True) + EPSILON)
    normed = c * s
    gain = p_ref[6:7, :]
    o_ref[...] = (normed * gain + p_ref[7:8, :]).astype(BF)
    ct = c_ref[...].astype(F32)
    e = ct * gain
    dr = s * (e - jnp.mean(e, -1, keepdims=True) - normed * jnp.mean(e * normed, -1, keepdims=True))
    dr_ref[...] = dr
    df = dr.astype(BF)
    df_ref[...] = df
    sum_ref[0:1, :] += jnp.sum(ct * normed, 0, keepdims=True)
    sum_ref[1:2, :] += jnp.sum(ct, 0, keepdims=True)
    sum_ref[2:3, :] += jnp.sum(df.astype(F32), 0, keepdims=True)


def down_part(g, y, ct, vecs, w_down, block=256):
    n, width = y.shape
    rows = lambda w: pl.BlockSpec((block, w), lambda i: (i, 0))
    whole = lambda shape: pl.BlockSpec(shape, lambda i: (0, 0))
    sds = jax.ShapeDtypeStruct
    return pl.pallas_call(
        down_kernel,
        grid=(n // block,),
        in_specs=[rows(4 * width), rows(width), rows(width), whole((8, width)), whole((4 * width, width))],
        out_specs=[rows(width), rows(width), rows(width), whole((8, width))],
        out_shape=[sds((n, width), BF), sds((n, width), BF), sds((n, width), F32), sds((8, width), F32)],
        compiler_params=params(FULL),
        cost_estimate=cost(8 * n * width * width, 22 * n * width + 8 * width * width),
        name="down_norm",
    )(g, y, ct, vecs, w_down)


def hidden_kernel(df_ref, gp_ref, wd, *rest):
    dh_ref, bup_ref = rest[-2:]

    @pl.when(pl.program_id(0) == 0)
    def _():
        bup_ref[...] = jnp.zeros_like(bup_ref)

    df = df_ref[...]
    width = df.shape[1]
    step = 512
    for k in range(0, dh_ref.shape[1], step):
        dh = (dg(df, wd[k : k + step, :], NT) * gp_ref[:, k : k + step].astype(F32)).astype(BF)
        dh_ref[:, k : k + step] = dh
        row, col = k // width, k % width
        bup_ref[row : row + 1, col : col + step] += jnp.sum(dh.astype(F32), 0, keepdims=True)


def hidden_part(df, gp, w_down, which, deps=(), block=256):
    n, width = df.shape
    cols = w_down.shape[0] // 2
    rows = pl.BlockSpec((block, width), lambda i: (i, 0))
    return pl.pallas_call(
        hidden_kernel,
        grid=(n // block,),
        in_specs=[rows, pl.BlockSpec((block, cols), lambda i: (i, which)), pl.BlockSpec((cols, width), lambda i: (which, 0))]
        + [ANY] * len(deps),
        out_specs=[pl.BlockSpec((block, cols), lambda i: (i, 0)), pl.BlockSpec((8, width), lambda i: (0, 0))],
        out_shape=[jax.ShapeDtypeStruct((n, cols), BF), jax.ShapeDtypeStruct((8, width), F32)],
        compiler_params=params(FULL),
        cost_estimate=cost(2 * n * width * cols, n * (2 * width + 4 * cols) + 2 * width * cols),
        name="hidden_gradient",
    )(df, gp, w_down, *deps)


def back_kernel(up, part, ids, dh_ref, dh2_ref, dr_ref, n_ref, s_ref, p_ref, *rest):
    nu = len(up.arrays)
    pu = rest[:nu]
    dr1_ref, do_ref, da_ref, sum_ref, wu, wo, su, so = rest[-8:]
    width = dr_ref.shape[1]

    @pl.when(pl.program_id(0) == 0)
    def _():
        moves = up.copies(pu, ids, [(0, part, wu, part, 0, 0)], su) + up.copies(pu, ids, [(0, part, wo, part, 0, 4 * width)], so)
        for m in moves:
            m.start()
        sum_ref[...] = jnp.zeros_like(sum_ref)
        for m in moves:
            m.wait()

    cut = dh_ref.shape[1]
    dy = dr_ref[...] + dg(dh_ref[...], wu[:, :cut], NT) + dg(dh2_ref[...], wu[:, cut:], NT)
    normed = n_ref[...].astype(F32)
    e = dy * p_ref[3:4, :]
    dr = s_ref[...] * (e - jnp.mean(e, -1, keepdims=True) - normed * jnp.mean(e * normed, -1, keepdims=True))
    dr1_ref[...] = dr
    do = dr.astype(BF)
    do_ref[...] = do
    da_ref[...] = dg(do, wo[...], NT).astype(BF)
    sum_ref[0:1, :] += jnp.sum(dy * normed, 0, keepdims=True)
    sum_ref[1:2, :] += jnp.sum(dy, 0, keepdims=True)
    sum_ref[2:3, :] += jnp.sum(do.astype(F32), 0, keepdims=True)


def back_part(dh, dr, normed, inverse, vecs, up, ids, nb, deps=(), block=256):
    n, width = dr.shape
    part = width // nb
    rows = lambda w: pl.BlockSpec((block, w), lambda i, ids: (i, 0))
    whole = lambda shape: pl.BlockSpec(shape, lambda i, ids: (0, 0))
    sds = jax.ShapeDtypeStruct
    return pl.pallas_call(
        functools.partial(back_kernel, up, part),
        grid_spec=pltpu.PrefetchScalarGridSpec(
            num_scalar_prefetch=1,
            grid=(n // block,),
            in_specs=[rows(2 * width), rows(2 * width), rows(width), rows(width), rows(1), whole((8, width))]
            + [ANY] * (len(up.arrays) + len(deps)),
            out_specs=[rows(width), rows(width), rows(width), whole((8, width))],
            scratch_shapes=[pltpu.VMEM((width, 4 * width), BF), pltpu.VMEM((width, width), BF)]
            + [pltpu.SemaphoreType.DMA((up.count([(0, part, 0, 0, 0)]),))] * 2,
        ),
        out_shape=[sds((n, width), F32), sds((n, width), BF), sds((n, width), BF), sds((8, width), F32)],
        compiler_params=params(FULL),
        cost_estimate=cost(10 * n * width * width, 22 * n * width + 10 * width * width),
        name="norm_backward",
    )(ids, *dh, dr, normed, inverse, vecs, *up.arrays, *deps)


def sums_kernel(one, two, up0, up1, *rest):
    out = rest[-1]
    out[...] = jnp.zeros_like(out)
    for r, (src, at) in enumerate(((one, 2), (one, 0), (one, 1), (two, 2), (two, 0), (two, 1))):
        out[1 + r : 2 + r, :] = src[at : at + 1, :]
    for r, (src, at) in enumerate(((up0, 0), (up0, 1), (up1, 0), (up1, 1))):
        out[7 + r : 8 + r, :] = src[at : at + 1, :]


def pack_sums(one, two, up0, up1):
    return pl.pallas_call(
        sums_kernel,
        in_specs=[pl.BlockSpec(memory_space=pltpu.VMEM)] * 4,
        out_specs=pl.BlockSpec(memory_space=pltpu.VMEM),
        out_shape=jax.ShapeDtypeStruct((16, one.shape[1]), F32),
        compiler_params=params(4 << 20),
        cost_estimate=cost(0, 1 << 20),
        name="pack_sums",
    )(one, two, up0, up1)


def grad_rows_kernel(top, jb, lo, ls, ro, rs, *rest):
    ka, sa, kb, sb = rest[-4:]
    j = pl.program_id(0)
    half = ka.shape[1]
    got = (dg(lo[...], ro[...], TN) + dg(ls[...], rs[...], TN)).astype(BF)

    @pl.when(j % 2 == 0)
    def _():
        ka[0] = got[:half]

    @pl.when(j % 2 == 1)
    def _():
        sa[0] = got[:half]

    @pl.when(j < top)
    def _():
        kb[0] = got[half:]

    @pl.when(j >= top)
    def _():
        sb[0] = got[half:]


def grad_down(g_own, g_sib, df_own, df_sib, jb, nf, deps=()):
    n, hidden = g_own.shape
    width = df_own.shape[1]
    part = hidden // (2 * nf)
    top = nf // 2
    left = pl.BlockSpec((n, part), lambda j, jb: (0, jb[j]))
    right = pl.BlockSpec((n, width), lambda j, jb: (0, 0))
    out = lambda at: pl.BlockSpec((1, part // 2, width), lambda j, jb: (at(j), 0, 0))
    return pl.pallas_call(
        functools.partial(grad_rows_kernel, top),
        grid_spec=pltpu.PrefetchScalarGridSpec(
            num_scalar_prefetch=1,
            grid=(nf,),
            in_specs=[left, left, right, right] + [ANY] * len(deps),
            out_specs=[
                out(lambda j: j // 2),
                out(lambda j: j // 2),
                out(lambda j: jnp.minimum(j, top - 1)),
                out(lambda j: jnp.maximum(j - top, 0)),
            ],
        ),
        out_shape=[jax.ShapeDtypeStruct((top, part // 2, width), BF)] * 4,
        compiler_params=params(FULL),
        cost_estimate=cost(2 * n * hidden * width, 2 * n * hidden + 4 * n * width + hidden * width),
        name="grad_down",
    )(jb, g_own, g_sib, df_own, df_sib, *deps)


class Job:
    def __init__(self, left, rights):
        self.left, self.rights = left, rights


EXTRA = 16


def grad_cols_kernel(jobs, nl, nf, block, keeps, extra, sum_blocks, *refs):
    pos = 1
    step = pl.program_id(0)
    lefts, rights = [], []
    for spans in jobs:
        lefts.append((refs[pos : pos + nl], refs[pos + nl : pos + 2 * nl]))
        pos += 2 * nl
    for spans in jobs:
        for _ in spans:
            rights.append((refs[pos], refs[pos + 1]))
            pos += 2
    if sum_blocks:
        vec_own, vec_sib = refs[pos : pos + 2]
    outs = refs[len(refs) - len(jobs) - 4 : len(refs) - len(jobs)]
    lts = refs[len(refs) - len(jobs) :]
    n, wide = lefts[0][0][0].shape
    part = nl * wide // nf
    half = part // 2
    at = 0
    for (los, lss), spans, lt in zip(lefts, jobs, lts):

        @pl.when(step == spans[0][0])
        def _():
            for j in range(nl):
                lt[j * wide : (j + 1) * wide, 0:n] = los[j][...].T
                lt[j * wide : (j + 1) * wide, n : 2 * n] = lss[j][...].T

        for begin, count in spans:
            own, sib = rights[at]
            at += 1

            @pl.when((step >= begin) & (step < begin + count))
            def _():
                both = jnp.concatenate([own[0], sib[0]], 0)
                got = dg(lt[...], both, NN).astype(BF)
                for out, (which, side) in zip(outs, keeps):
                    for m, j in enumerate(which):
                        out[m, 0:half, :] = got[j * part + side * half : j * part + (side + 1) * half]
                if extra:
                    tile = jnp.zeros((EXTRA, block), F32)
                    if sum_blocks:
                        tile = jnp.where(step < sum_blocks, vec_own[...] + vec_sib[...], 0.0)
                    columns = jnp.sum(both.astype(F32), 0, keepdims=True)
                    tile = jnp.where(lax.broadcasted_iota(jnp.int32, (EXTRA, block), 0) == 0, columns, tile).astype(BF)
                    for out in outs:
                        for m in range(out.shape[0]):
                            out[m, half : half + EXTRA, :] = tile


def grad_cols(jobs, jb, nf, block, name, deps=(), extra=False, vecs=None):
    n, width = jobs[0].left[0].shape
    part = width // (2 * nf)
    spans, step = [], 0
    in_specs, operands, right_specs, right_ops = [], [], [], []
    for job in jobs:
        mine = []
        pick = lambda z: z.reshape(n, 2 * nf, part)[:, jb].reshape(n, nf * part)
        for z in job.left:
            if part % LANES == 0:
                nl = nf
                in_specs += [pl.BlockSpec((n, part), lambda i, jb, j=j: (0, jb[j])) for j in range(nf)]
                operands += [z] * nf
            else:
                nl = 1
                in_specs += [pl.BlockSpec((n, nf * part), lambda i, jb: (0, 0))]
                operands += [pick(z)]
        for own, sib in job.rights:
            planes, _, cols = own.shape
            per = cols // block
            count = planes * per

            def at(i, jb, step=step, count=count, per=per):
                k = jnp.clip(i - step, 0, count - 1)
                return (k // per, 0, k % per)

            right_specs += [pl.BlockSpec((1, n, block), at)] * 2
            right_ops += [own, sib]
            mine.append((step, count))
            step += count
        spans.append(mine)
    half = part // 2
    sum_blocks = 0
    if vecs is not None:
        sum_blocks = vecs[0].shape[1] // block
        right_specs += [pl.BlockSpec((EXTRA, block), lambda i, jb: (0, jnp.minimum(i, sum_blocks - 1)))] * 2
        right_ops += list(vecs)
    js = list(range(nf))
    top = nf // 2
    keeps = [([j for j in js if not j & 1], 0), ([j for j in js if j & 1], 0), ([j for j in js if j < top], 1), ([j for j in js if j >= top], 1)]
    lines = half + (EXTRA if extra else 0)
    out_spec = pl.BlockSpec((nf // 2, lines, block), lambda i, jb: (0, 0, i))
    out_shape = jax.ShapeDtypeStruct((nf // 2, lines, step * block), BF)
    return pl.pallas_call(
        functools.partial(grad_cols_kernel, spans, nl, nf, block, keeps, extra, sum_blocks),
        grid_spec=pltpu.PrefetchScalarGridSpec(
            num_scalar_prefetch=1,
            grid=(step,),
            in_specs=in_specs + right_specs + [ANY] * len(deps),
            out_specs=[out_spec] * 4,
            scratch_shapes=[pltpu.VMEM((nf * part, 2 * n), BF)] * len(jobs),
        ),
        out_shape=[out_shape] * 4,
        compiler_params=params(),
        cost_estimate=cost(2 * n * width * step * block, 4 * n * (step * block + width // 2)),
        name=name,
    )(jb, *operands, *right_ops, *deps)


def input_kernel(got, part, groups, place, ids, dr_ref, *rest):
    n = len(got.arrays)
    d_refs, pieces = rest[1 : 1 + groups], rest[1 + groups : 1 + groups + n]
    out_ref, wq, wk, wv, sems = rest[-5:]
    targets = qkv_targets(part, wq, wk, wv)

    @pl.when(pl.program_id(0) == 0)
    def _():
        moves = got.copies(pieces, ids, targets, sems)
        for c in moves:
            c.start()
        for c in moves:
            c.wait()

    total = dr_ref[...]
    for k, w in enumerate((wq, wk, wv)):
        d = jnp.concatenate([r[k] for r in d_refs], 1)
        total += dg(d, w[...], NT)
    out_ref[...] = total


def input_part(dr, grads, got, ids, place, nb, deps=(), block=256):
    n, width = dr.shape
    steps = n // 2 // block
    rows = pl.BlockSpec((block, width), lambda i, ids: (i + ids[ids.shape[0] - 2 + place] * steps, 0))
    three = lambda w: pl.BlockSpec((3, block, w), lambda i, ids: (0, i + ids[ids.shape[0] - 2 + place] * steps, 0))
    count = got.count(qkv_targets(width // nb, 0, 0, 0))
    return pl.pallas_call(
        functools.partial(input_kernel, got, width // nb, len(grads), place),
        grid_spec=pltpu.PrefetchScalarGridSpec(
            num_scalar_prefetch=1,
            grid=(steps,),
            in_specs=[rows, ANY] + [three(a.shape[2]) for a in grads] + [ANY] * (len(got.arrays) + len(deps)),
            out_specs=pl.BlockSpec((block, width), lambda i, ids: (i, 0)),
            scratch_shapes=[pltpu.VMEM((width, width), BF)] * 3 + [pltpu.SemaphoreType.DMA((count,))],
        ),
        out_shape=jax.ShapeDtypeStruct((n // 2, width), F32),
        compiler_params=params(FULL),
        cost_estimate=cost(3 * n * width * width, 7 * n * width + 6 * width * width),
        name="input_gradient",
    )(ids, dr, dr, *grads, *got.arrays, *deps)


def add_low(a, b):
    return (a[...].astype(F32) + b[...].astype(F32)).astype(BF)


SMALL = 16 << 20


def tile_of(cols):
    return cols // 2 if cols % (2 * LANES) == 0 else cols


def stage_kernel(last, odd, ka, ra, kb, rb, *rest):
    outs = rest[len(rest) - (2 if last else 4) :]
    a, b = add_low(ka, ra), add_low(kb, rb)
    m = a.shape[0]
    if last:
        swapped = odd[0] == 1
        outs[0][...] = jnp.where(swapped, b, a)
        outs[1][...] = jnp.where(swapped, a, b)
    else:
        for i in range(m // 2):
            outs[0][i], outs[1][i] = a[2 * i], a[2 * i + 1]
            outs[2][i], outs[3][i] = b[i], b[m // 2 + i]


def stage(odd, ka, ra, kb, rb, deps):
    m, rows, cols = ka.shape
    block = tile_of(cols)
    last = m == 1
    into = pl.BlockSpec((m, rows, block), lambda i, odd: (0, 0, i))
    mo = max(m // 2, 1)
    out = pl.BlockSpec((mo, rows, block), lambda i, odd: (0, 0, i))
    return pl.pallas_call(
        functools.partial(stage_kernel, last),
        grid_spec=pltpu.PrefetchScalarGridSpec(
            num_scalar_prefetch=1,
            grid=(cols // block,),
            in_specs=[into] * 4 + [ANY] * len(deps),
            out_specs=[out] * (2 if last else 4),
        ),
        out_shape=[jax.ShapeDtypeStruct((mo, rows, cols), BF)] * (2 if last else 4),
        compiler_params=params(9 << 20),
        cost_estimate=cost(0, 12 * m * rows * cols),
        name="sum_plane",
    )(odd, ka, ra, kb, rb, *deps)


def pair_sum_kernel(a, b, *rest):
    rest[-1][...] = add_low(a, b)


def pair_sum(a, b, deps):
    rows, cols = a.shape
    block = tile_of(cols)
    spec = pl.BlockSpec((rows, block), lambda i: (0, i))
    return pl.pallas_call(
        pair_sum_kernel,
        grid=(cols // block,),
        in_specs=[spec] * 2 + [ANY] * len(deps),
        out_specs=spec,
        out_shape=jax.ShapeDtypeStruct((rows, cols), BF),
        compiler_params=params(4 << 20),
        cost_estimate=cost(0, 6 * rows * cols),
        name="sum_rep",
    )(a, b, *deps)


def pick_kernel(odd, a, b, *rest):
    rest[-2][...], rest[-1][...] = a[...], b[...]


def pick(odd, v, deps=()):
    rows, cols = v.shape
    block = tile_of(cols)
    spec = lambda flip: pl.BlockSpec((rows // 2, block), lambda i, odd: ((odd[0] + flip) % 2, i))
    out = pl.BlockSpec((rows // 2, block), lambda i, odd: (0, i))
    return pl.pallas_call(
        pick_kernel,
        grid_spec=pltpu.PrefetchScalarGridSpec(
            num_scalar_prefetch=1, grid=(cols // block,), in_specs=[spec(0), spec(1)] + [ANY] * len(deps), out_specs=[out, out]
        ),
        out_shape=[jax.ShapeDtypeStruct((rows // 2, cols), BF)] * 2,
        compiler_params=params(4 << 20),
        cost_estimate=cost(0, 4 * rows * cols),
        name="pick_half",
    )(odd, v, v, *deps)


class RepChain:
    def __init__(self, kept, sent, nr, odd):
        self.kept, self.sent, self.nr, self.odd = kept, sent, nr, odd

    def rep_first(self, deps=()):
        self.kept = pair_sum(self.kept, swap(self.sent, "rep", self.nr, 1), deps)
        return (self.kept,)

    def rep_middle(self, deps=()):
        xor = 2
        while xor < self.nr:
            self.kept = pair_sum(self.kept, swap(self.kept, "rep", self.nr, xor), deps)
            xor *= 2
        return (self.kept,)

    def rep_middle_part(self, which, deps=()):
        if self.nr != 4:
            return self.rep_middle(deps) if which == 1 else ()
        rows = self.kept.shape[0] // 2
        part = self.kept[:rows] if which == 0 else self.kept[rows:]
        part = pair_sum(part, swap(part, "rep", self.nr, 2), deps)
        if which == 0:
            self.first_part = part
        else:
            self.kept = jnp.concatenate([self.first_part, part], 0)
        return (part,)

    def rep_last(self):
        self.other = swap(self.kept, "rep", self.nr, 1)
        return (self.other,)

    def halves(self):
        odd = self.odd[0] == 1
        return jnp.where(odd, self.other, self.kept).astype(F32), jnp.where(odd, self.kept, self.other).astype(F32)

    def result(self):
        return jnp.concatenate(self.halves(), 0)


class Chain(RepChain):
    def __init__(self, parts, nf, nr, odd):
        self.nf, self.nr, self.odd = nf, nr, odd
        self.ka, self.sa, self.kb, self.sb = parts
        self.level, self.bits = 0, nf.bit_length() - 1

    def plane(self, deps=()):
        a, b = self.level, self.bits - 1 - self.level
        ra, rb = swap(self.sa, "fsdp", self.nf, 1 << a), swap(self.sb, "fsdp", self.nf, 1 << b)
        self.level += 1
        out = stage(self.odd, self.ka, ra, self.kb, rb, deps)
        if self.level == self.bits:
            self.kept, self.sent = out[0][0], out[1][0]
        else:
            self.ka, self.sa, self.kb, self.sb = out
        return tuple(out)

    def rest(self, deps=()):
        out = ()
        while self.level < self.bits:
            out = self.plane(deps)
        return out


def join_kernel(odd, kept, other, *rest):
    out = rest[-1]
    rows = kept.shape[0]
    swapped = odd[0] == 1
    out[:rows, :] = jnp.where(swapped, other[...], kept[...]).astype(F32)
    out[rows:, :] = jnp.where(swapped, kept[...], other[...]).astype(F32)


def join(chain, deps=()):
    rows, cols = chain.kept.shape
    block = cols // 2
    spec = pl.BlockSpec((rows, block), lambda i, odd: (0, i))
    return pl.pallas_call(
        join_kernel,
        grid_spec=pltpu.PrefetchScalarGridSpec(
            num_scalar_prefetch=1,
            grid=(2,),
            in_specs=[spec] * 2 + [ANY] * len(deps),
            out_specs=pl.BlockSpec((2 * rows, block), lambda i, odd: (0, i)),
        ),
        out_shape=jax.ShapeDtypeStruct((2 * rows, cols), F32),
        compiler_params=params(8 << 20),
        cost_estimate=cost(0, 12 * rows * cols),
        name="join_halves",
    )(chain.odd, chain.kept, chain.other, *deps)


def finish_kernel(half, width, wide, counts, odd, *refs):
    n = len(counts)
    q, k, v, o, small, line = refs[2 * n :]
    for at in range(2):
        rows = slice(at * half, (at + 1) * half)
        group, lines = 0, []
        for i, count in enumerate(counts):
            both = jnp.where(odd[0] == at, refs[2 * i][...], refs[2 * i + 1][...]).astype(F32)
            col = 0
            if i == 0:
                o[rows, :] = both[:half, :width]
                if at == 0:
                    small[...] = both[half : half + EXTRA, :width]
                col = width
            lines.append(both[half : half + 8, col:])
            for _ in range(count):
                for out in (q, k, v):
                    out[rows, group * wide : (group + 1) * wide] = both[:half, col : col + wide]
                    col += wide
                group += 1
        if at == 0:
            line[...] = jnp.concatenate(lines, 1)


def finish(odd, chains, counts, half, width, wide):
    spec = pl.BlockSpec(memory_space=pltpu.VMEM)
    sds = jax.ShapeDtypeStruct
    return pl.pallas_call(
        functools.partial(finish_kernel, half, width, wide, counts),
        in_specs=[pl.BlockSpec(memory_space=pltpu.SMEM)] + [spec] * (2 * len(chains)),
        out_specs=[spec] * 6,
        out_shape=[sds((2 * half, width), F32)] * 4 + [sds((EXTRA, width), F32), sds((8, 3 * wide * sum(counts)), F32)],
        compiler_params=params(12 << 20),
        cost_estimate=cost(0, 6 << 20),
        name="finish",
    )(odd, *[z for c in chains for z in (c.kept, c.other)])


def body(tokens, segment_ids, padding, cotangent, w_query, w_key, w_value, w_out, b_query, b_value, b_out,
         gain_one, shift_one, w_up, b_up, w_down, b_down, gain_two, shift_two, *, nr, nf, ns):
    _, part_len, width = tokens.shape
    f, c = lax.axis_index("fsdp"), lax.axis_index("seq")
    rel = [((f ^ j) * 2 + (c ^ p)) for j in range(nf) for p in range(2)]
    absolute = [(j * 2 + (c ^ p)) for j in range(nf) for p in range(2)]
    ids = jnp.stack(rel + absolute + [1 - c, c]).astype(jnp.int32)
    jb = jnp.stack(rel[::2]).astype(jnp.int32)
    jb_abs = jnp.stack(absolute[::2]).astype(jnp.int32)
    core = c.astype(jnp.int32).reshape(1)
    odd = (lax.axis_index("rep") & 1).astype(jnp.int32).reshape(1)
    sib_of = lambda z: swap(z, "seq", ns, 1)
    nb = 2 * nf
    part = width // nb

    qkv_shard = pack_first(
        [b_query, b_value, b_out, gain_one, shift_one, b_down, gain_two, shift_two, b_up], [w_query, w_key, w_value]
    )
    first = gather_start(qkv_shard, nf)
    x, x_sib, ct = pair_up(core, [(tokens, sib_of(tokens), 2), (cotangent, sib_of(cotangent), 1)])
    marks = jnp.stack([segment_ids, padding])
    theirs = sib_of(marks)
    own = c == 0
    mine_m, their_m = jnp.where(own, marks[:, 0], marks[:, 1]), jnp.where(own, theirs[:, 0], theirs[:, 1])
    whole = jnp.where(own, jnp.concatenate([mine_m, their_m], 1), jnp.concatenate([their_m, mine_m], 1))
    qf, kf = seg_features(whole[0], whole[1])
    (up_shard,) = split_rows(
        [w_up, w_out], [(0, 0, part, 0, 0, 0), (1, 0, part, 0, 0, 4 * width)], [(part, 5 * width)], (), "pack_up"
    )
    far = gather_far(first, nf, (x, qf, up_shard))
    gate = tuple(far) or tuple(first)
    got_qkv, _ = gather_end(qkv_shard, first, far, nf, ns)
    first_up = gather_start(after(up_shard, *gate), nf)
    q, k, v, vecs, bup = project(x, got_qkv, ids, nb)

    pairs = width // LANES
    groups = 4
    each = pairs // groups
    fwd = [attn_fwd(q, k, v, qf, kf, 0, each)]
    fwd.append(attn_fwd(q, k, v, qf, kf, each, each, (fwd[0][0],)))
    far_up = gather_far(first_up, nf, (fwd[1][0],))
    full_down = lax.all_gather(after(w_down, fwd[1][0], *first_up), ("fsdp", "seq"), axis=0, tiled=True)
    fwd.append(attn_fwd(q, k, v, qf, kf, 2 * each, 2 * each, (fwd[1][0],) + tuple(first_up)))
    got_up, swaps = gather_end(up_shard, first_up, far_up, nf, ns, (fwd[2][0],))
    lf = [(fwd[0][1], 0), (fwd[1][1], 0), (fwd[2][1], 0), (fwd[2][1], each)]

    a_all, y, yb, normed, inverse, g, gp = up_part(x, vecs, bup, [r[0] for r in fwd], got_up, ids, nb)
    a_sib, yb_sib, g_sib = sib_of(a_all), sib_of(yb), sib_of(g)
    out, df, dr, sums_two = down_part(g, y, ct, vecs, full_down)
    df_sib = sib_of(after(df, yb_sib, a_sib))
    dh0, sum_up0 = hidden_part(df, gp, full_down, 0, (yb_sib, a_sib))
    dh0_sib = sib_of(after(dh0, df_sib, g_sib))
    dh1, sum_up1 = hidden_part(df, gp, full_down, 1, (dh0, df_sib, g_sib))
    dh1_sib = sib_of(after(dh1, dh0_sib))
    g_down = grad_down(g, g_sib, df, df_sib, jb, nf, (dh1, dh0_sib))
    chain_down = Chain(after(g_down, dh1_sib), nf, nr, odd)
    g_up = grad_cols([Job((yb, yb_sib), [(dh0[None], dh0_sib[None]), (dh1[None], dh1_sib[None])])], jb, nf, 512, "grad_up", (g_down[0],))
    now = chain_down.plane((g_up[0],))
    g_up = after(g_up, *now)
    out_sib = sib_of(after(out, *now))
    chain_up = Chain(g_up, nf, nr, odd)
    dr1, do, da, sums_one = back_part((dh0, dh1), dr, normed, inverse, vecs, got_up, ids, nb, now + (g_up[0],))
    now = chain_up.plane((da,)) + chain_down.rest((da,))
    do_sib = sib_of(after(do, *now))
    sums = pack_sums(*after((sums_one, sums_two, sum_up0, sum_up1), *now))

    grads, sibs = [], []

    def run(i, deps):
        grads.append(attn_bwd(q, k, v, da, a_all, lf[i][0], kf, i * each, each, lf[i][1], deps))
        return (grads[-1],)

    def send(i, deps):
        sibs.append(sib_of(after(grads[i], *deps)))

    dep = run(0, (da,) + now)
    now = chain_up.rest(dep) + chain_down.rep_first(dep)
    send(0, now)
    output = unpair_up(core, *after((out, out_sib), *now), part_len)
    sums_sib = sib_of(after(sums, *now))
    dep = run(1, dep + now + (output, do_sib, sums_sib, sibs[0]))
    now = chain_up.rep_first(dep) + chain_down.rep_middle(dep)
    chain_down.rep_last()
    send(1, now)
    g_one = grad_cols(
        [Job((a_all, a_sib), [(do[None], do_sib[None])]), Job((x, x_sib), [(grads[0], sibs[0])])],
        jb, nf, 256, "grad_out_qkv", dep + now, True, (sums, sums_sib),
    )
    dep = (g_one[0],)
    now = chain_up.rep_middle_part(0, dep)
    chain_one = Chain(after(g_one, *now), nf, nr, odd)
    dep = run(2, dep + now + (sibs[1],))
    final_down = join(chain_down, dep)
    now = chain_one.plane(dep) + chain_up.rep_middle_part(1, dep) + (final_down,)
    send(2, now)
    chain_up.rep_last()
    g_two = grad_cols([Job((x, x_sib), [(grads[i], sibs[i]) for i in (1, 2)])], jb, nf, 256, "grad_qkv", dep + now, True)
    dep = (g_two[0],)
    now = chain_one.rest(dep)
    chain_two = Chain(after(g_two, *now), nf, nr, odd)
    dep = run(3, dep + now)
    final_up = join(chain_up, dep)
    now = chain_two.plane(dep) + chain_one.rep_first(dep) + (final_up,)
    send(3, now)
    g_three = grad_cols([Job((x, x_sib), [(grads[3], sibs[3])])], jb, nf, 256, "grad_qkv", dep + now, True)
    dep = (g_three[0],)
    now = chain_two.rest(dep)
    chain_three = Chain(after(g_three, *now), nf, nr, odd)
    send_half = input_part(dr1, grads, got_qkv, ids, 0, nb, dep + now)
    dep = (send_half,)
    now = chain_three.plane(dep) + chain_one.rep_middle(dep) + chain_two.rep_first(dep)
    chain_one.rep_last()
    their_half = sib_of(after(send_half, *now))
    keep_half = input_part(dr1, grads, got_qkv, ids, 1, nb, dep + now)
    dep = (keep_half,)
    now = chain_three.rest(dep) + chain_two.rep_middle(dep)
    chain_two.rep_last()
    input_grad = unpair_up(core, *after((keep_half, their_half), *now), part_len)
    chain_three.rep_first()
    chain_three.rep_middle((input_grad,))
    chain_three.rep_last()
    half = part // 2
    wide = each * LANES
    final_q, final_k, final_v, final_out, small, line = finish(odd, (chain_one, chain_two, chain_three), (1, 2, 1), half, width, wide)
    line = line[0].reshape(groups, 3, wide)
    vectors = jnp.concatenate([line[:, 0].reshape(1, width), line[:, 2].reshape(1, width), small[1:7]], 0)
    own_block = 2 * f + c
    v8 = lax.dynamic_slice(vectors, (0, own_block * part), (8, part))
    final_bup = lax.dynamic_slice(small[7:11].reshape(-1), (own_block * 4 * part,), (4 * part,))
    return (output, input_grad, final_q, final_k, final_v, final_out, v8[0], v8[1], v8[2], v8[3], v8[4],
            final_up, final_bup, final_down, v8[5], v8[6], v8[7])


def solution(mesh):
    tok = P(("rep", "fsdp"), "seq", None)
    ids = P(("rep", "fsdp"), "seq")
    mat = P(("fsdp", "seq"), None)
    vec = P(("fsdp", "seq"))
    sizes = mesh.shape
    return jax.shard_map(
        functools.partial(body, nr=sizes["rep"], nf=sizes["fsdp"], ns=sizes["seq"]),
        mesh=mesh,
        in_specs=(tok, ids, ids, tok) + (mat,) * 4 + (vec,) * 5 + (mat, vec, mat) + (vec,) * 3,
        out_specs=(tok, tok) + (mat,) * 4 + (vec,) * 5 + (mat, vec, mat) + (vec,) * 3,
        check_vma=False,
    )
```

```python
import functools
import math
import jax
import jax.numpy as jnp
from jax import lax
from jax.experimental import pallas as pl
from jax.experimental.pallas import tpu as pltpu
from jax.sharding import PartitionSpec as P

F32 = jnp.float32
BF = jnp.bfloat16
HEAD_DIM = 64
LANES = 128
EPSILON = 1e-05
ROOT_HALF = 0.7071067811865476
INV_ROOT_TAU = 0.3989422804014327
NT = (((1,), (1,)), ((), ()))
TN = (((0,), (0,)), ((), ()))
NN = (((1,), (0,)), ((), ()))
VMEM = 48 << 20
FULL = 58 << 20
SHRINK = 1
ANY = pl.BlockSpec(memory_space=pl.ANY)


def dg(a, b, dims):
    return lax.dot_general(a, b, dims, preferred_element_type=F32)


def params(limit=VMEM):
    return pltpu.CompilerParams(vmem_limit_bytes=limit)


def cost(flops, bytes_accessed, trans=0):
    return pl.CostEstimate(flops=flops // SHRINK, bytes_accessed=bytes_accessed // SHRINK, transcendentals=trans // SHRINK)


def swap(x, axis, size, xor):
    return lax.ppermute(x, axis, [(i, i ^ xor) for i in range(size)])


def after(x, *deps):
    return lax.optimization_barrier((x,) + deps)[0]


class Gathered:
    def __init__(self, arrays, entries, half):
        self.arrays, self.entries, self.half = arrays, entries, half

    def copies(self, refs, ids, targets, sems):
        out = []
        for which, index, base, half, slot in self.entries:
            low = half * self.half
            for first, rows, dest, stride, offset, *column in targets:
                a, b = max(first, low), min(first + rows, low + self.half)
                if a >= b:
                    continue
                place = (*index, pl.ds(base + a - low, b - a))
                if column:
                    place += (pl.ds(column[0], dest.shape[1]),)
                src = refs[which].at[place]
                start = pl.multiple_of(ids[slot] * stride + (offset + a - first), 16)
                out.append(pltpu.make_async_copy(src, dest.at[pl.ds(start, b - a)], sems.at[len(out)]))
        return out

    def count(self, targets):
        n = 0
        for _, _, _, half, _ in self.entries:
            low = half * self.half
            n += sum(max(t[0], low) < min(t[0] + t[1], low + self.half) for t in targets)
        return n


def gather_start(shard, nf):
    if nf == 4:
        return [swap(shard, "fsdp", nf, 1), swap(shard, "fsdp", nf, 2)]
    return [lax.all_gather(shard, "fsdp", axis=0)]


def gather_far(first, nf, deps=()):
    if nf == 4:
        half = first[0].shape[0] // 2
        shape = (half, first[0].shape[1])
        one, two = split_rows(first, [(0, 0, half, 0, 0, 0), (1, half, half, 1, 0, 0)], [shape, shape], deps, "cut_halves")
        return [swap(one, "fsdp", nf, 2), swap(two, "fsdp", nf, 1)]
    return []


def gather_end(shard, first, far, nf, ns, late=(), early=()):
    half = shard.shape[0] // 2
    if nf == 4:
        arrays = [shard, *first, *far]
        entries = [(w, (), h * half, h, 2 * w) for w in range(3) for h in range(2)]
        entries += [(3, (), 0, 0, 6), (4, (), 0, 1, 6)]
    else:
        arrays = list(first)
        entries = [(0, (f,), h * half, h, 2 * nf + 2 * f) for f in range(nf) for h in range(2)]
    n = len(arrays)
    swaps = [swap(after(a, *early) if early else a, "seq", ns, 1) for a in arrays[: n - len(far)]]
    swaps += [swap(after(a, *late), "seq", ns, 1) for a in arrays[n - len(far) :]]
    arrays = arrays + swaps
    entries = entries + [(w + n, i, r, h, s + 1) for w, i, r, h, s in entries]
    return Gathered(arrays, entries, half), swaps


BIAS_ROWS = 32


def split_kernel(moves, nin, nout, *refs):
    ins, outs, sems = refs[:nin], refs[len(refs) - nout - 1 : -1], refs[-1]
    copies = [
        pltpu.make_async_copy(ins[s].at[pl.ds(first, rows)], outs[d].at[pl.ds(to, rows), pl.ds(col, ins[s].shape[1])], sems.at[i])
        for i, (s, first, rows, d, to, col) in enumerate(moves)
    ]
    for m in copies:
        m.start()
    for m in copies:
        m.wait()


def split_rows(ins, moves, out_shapes, deps, name):
    return pl.pallas_call(
        functools.partial(split_kernel, moves, len(ins), len(out_shapes)),
        in_specs=[ANY] * (len(ins) + len(deps)),
        out_specs=[pl.BlockSpec(memory_space=pltpu.VMEM)] * len(out_shapes),
        out_shape=[jax.ShapeDtypeStruct(o, BF) for o in out_shapes],
        scratch_shapes=[pltpu.SemaphoreType.DMA((len(moves),))],
        compiler_params=params(58 << 20),
        cost_estimate=cost(0, 1 << 20),
        name=name,
    )(*ins, *deps)


def bias_kernel(nvec, *refs):
    vecs, mats, out = refs[:nvec], refs[nvec : nvec + 3], refs[nvec + 3]
    held, tile, sems = refs[nvec + 4 : 2 * nvec + 4], refs[-2], refs[-1]
    part = mats[0].shape[0]
    moves = [pltpu.make_async_copy(m, out.at[pl.ds(i * part, part)], sems.at[i]) for i, m in enumerate(mats)]
    small = [pltpu.make_async_copy(v, h, sems.at[3 + i]) for i, (v, h) in enumerate(zip(vecs, held))]
    for m in small + moves:
        m.start()
    tile[...] = jnp.zeros_like(tile)
    for m in small:
        m.wait()
    for i in range(8):
        tile[0:1, i * part : (i + 1) * part] = held[i][...].astype(F32).reshape(1, part)
    tile[1:2, 0 : 4 * part] = held[8][...].astype(F32).reshape(1, 4 * part)
    out[3 * part :, :] = tile[...].astype(BF)
    for m in moves:
        m.wait()


def pack_first(vecs, mats):
    part, width = mats[0].shape
    n = len(vecs)
    return pl.pallas_call(
        functools.partial(bias_kernel, n),
        in_specs=[ANY] * (n + 3),
        out_specs=pl.BlockSpec(memory_space=pltpu.VMEM),
        out_shape=jax.ShapeDtypeStruct((3 * part + BIAS_ROWS, width), BF),
        scratch_shapes=[pltpu.VMEM(v.shape, BF) for v in vecs] + [pltpu.VMEM((BIAS_ROWS, width), F32), pltpu.SemaphoreType.DMA((n + 3,))],
        compiler_params=params(58 << 20),
        cost_estimate=cost(0, 1 << 20),
        name="pack_first",
    )(*vecs, *mats)


def pair_kernel(count, core, *refs):
    ins, outs, sems = refs[: 2 * len(count)], refs[len(refs) - 1 - sum(count) : -1], refs[-1]
    c = core[0]
    at, moves = 0, []
    for i, n in enumerate(count):
        mine, theirs = ins[2 * i], ins[2 * i + 1]
        half = mine.shape[1]
        for k in range(n):
            which = c if k == 0 else 1 - c
            for src, place in ((mine, c), (theirs, 1 - c)):
                start = pl.multiple_of(place * half, half)
                moves.append(pltpu.make_async_copy(src.at[which], outs[at].at[pl.ds(start, half)], sems.at[len(moves)]))
            at += 1
    for m in moves:
        m.start()
    for m in moves:
        m.wait()


def pair_up(core, items, deps=()):
    count = [n for _, _, n in items]
    flat = [z for a, b, _ in items for z in (a, b)]
    shapes = [jax.ShapeDtypeStruct((2 * a.shape[1], a.shape[2]), a.dtype) for a, _, n in items for _ in range(n)]
    return pl.pallas_call(
        functools.partial(pair_kernel, count),
        grid_spec=pltpu.PrefetchScalarGridSpec(
            num_scalar_prefetch=1,
            grid=(1,),
            in_specs=[ANY] * (len(flat) + len(deps)),
            out_specs=[pl.BlockSpec(z.shape, lambda i, core: (0, 0)) for z in shapes],
            scratch_shapes=[pltpu.SemaphoreType.DMA((2 * len(shapes),))],
        ),
        out_shape=shapes,
        compiler_params=params(58 << 20),
        cost_estimate=cost(0, 1 << 20),
        name="pair_up",
    )(core, *flat, *deps)


def unpair_kernel(core, own, theirs, *rest):
    out, sems = rest[-2:]
    c = core[0]
    half = out.shape[1]
    start = pl.multiple_of(c * half, half)
    cut = lambda z: z.at[pl.ds(start, half)] if z.shape[0] > half else z
    one = pltpu.make_async_copy(cut(own), out.at[c], sems.at[0])
    two = pltpu.make_async_copy(cut(theirs), out.at[1 - c], sems.at[1])
    one.start()
    two.start()
    one.wait()
    two.wait()


def unpair_up(core, own, theirs, half, deps=()):
    width = own.shape[1]
    return pl.pallas_call(
        unpair_kernel,
        grid_spec=pltpu.PrefetchScalarGridSpec(
            num_scalar_prefetch=1,
            grid=(1,),
            in_specs=[ANY] * (2 + len(deps)),
            out_specs=pl.BlockSpec((2, half, width), lambda i, core: (0, 0, 0)),
            scratch_shapes=[pltpu.SemaphoreType.DMA((2,))],
        ),
        out_shape=jax.ShapeDtypeStruct((2, half, width), own.dtype),
        compiler_params=params(58 << 20),
        cost_estimate=cost(0, 1 << 20),
        name="unpair",
    )(core, own, theirs, *deps)


def qkv_kernel(got, ids, x_ref, *rest):
    n = len(got.arrays)
    pieces = rest[:n]
    q_ref, k_ref, v_ref, p_ref, b_ref, wq, wk, wv, wb, sems = rest[-10:]
    width = x_ref.shape[1]
    nb = wb.shape[0] // BIAS_ROWS
    part = width // nb
    targets = qkv_targets(part, wq, wk, wv, wb)

    @pl.when(pl.program_id(0) == 0)
    def _():
        moves = got.copies(pieces, ids, targets, sems)
        for m in moves:
            m.start()
        for m in moves:
            m.wait()
        for b in range(nb):
            rows = wb[b * BIAS_ROWS : b * BIAS_ROWS + 16, :].astype(F32)
            for vec in range(8):
                p_ref[vec : vec + 1, b * part : (b + 1) * part] = rows[0:1, vec * part : (vec + 1) * part]
            b_ref[0:1, b * 4 * part : (b + 1) * 4 * part] = rows[1:2, 0 : 4 * part]

    x = x_ref[...]
    q_ref[...] = (dg(x, wq[...], NN) + p_ref[0:1, :]).astype(BF)
    k_ref[...] = dg(x, wk[...], NN).astype(BF)
    v_ref[...] = (dg(x, wv[...], NN) + p_ref[1:2, :]).astype(BF)


def qkv_targets(part, wq, wk, wv, wb=None):
    t = [(0, part, wq, part, 0), (part, part, wk, part, 0), (2 * part, part, wv, part, 0)]
    return t if wb is None else t + [(3 * part, BIAS_ROWS, wb, BIAS_ROWS, 0)]


def project(x, got, ids, nb, deps=(), block=256):
    n, width = x.shape
    grid = n // block
    rows = pl.BlockSpec((block, width), lambda i, ids: (i, 0))
    whole = lambda shape: pl.BlockSpec(shape, lambda i, ids: (0, 0))
    count = got.count(qkv_targets(width // nb, 0, 0, 0, 0))
    return pl.pallas_call(
        functools.partial(qkv_kernel, got),
        grid_spec=pltpu.PrefetchScalarGridSpec(
            num_scalar_prefetch=1,
            grid=(grid,),
            in_specs=[rows] + [ANY] * (len(got.arrays) + len(deps)),
            out_specs=[rows, rows, rows, whole((8, width)), whole((1, 4 * width))],
            scratch_shapes=[pltpu.VMEM((width, width), BF)] * 3
            + [pltpu.VMEM((nb * BIAS_ROWS, width), BF), pltpu.SemaphoreType.DMA((count,))],
        ),
        out_shape=[jax.ShapeDtypeStruct((n, width), BF)] * 3
        + [jax.ShapeDtypeStruct((8, width), F32), jax.ShapeDtypeStruct((1, 4 * width), F32)],
        compiler_params=params(FULL),
        cost_estimate=cost(6 * n * width * width, 2 * n * width * 4 + 6 * width * width),
        name="project",
    )(ids, x, *got.arrays, *deps)


def split3(v):
    hi=v.astype(BF); r=v-hi.astype(F32); mid=r.astype(BF); lo=(r-mid.astype(F32)).astype(BF)
    return hi,mid,lo
def attn_fwd_kernel(qb, q_ref,k_ref,v_ref,qf_ref,kf_ref,*rest):
    a_ref,lf_ref=rest[-2:]
    n=q_ref.shape[0]
    lane=lax.broadcasted_iota(jnp.int32,(n,LANES),1)
    left=lane<HEAD_DIM
    q=q_ref[...]*jnp.asarray(0.125,BF); k=k_ref[...]; v=v_ref[...]
    qf=qf_ref[...]; kf=kf_ref[...]
    one=jnp.ones_like(v)
    sides=[]
    for h in range(2):
        own=left if h==0 else ~left
        sides.append((jnp.where(own,q,qf),jnp.where(own,k,kf),jnp.where(own,v,one)))
    lq=lax.broadcasted_iota(jnp.int32,(qb,LANES),1)
    leftq=lq<HEAD_DIM
    for c in range(n//qb):
        rows=slice(c*qb,(c+1)*qb)
        res=[]; lse=[]
        for h in range(2):
            qa,ka,va=sides[h]
            s=dg(qa[rows],ka,NT)
            m=jnp.max(s,-1,keepdims=True)
            p=jnp.exp(s-m).astype(BF)
            o=dg(p,va,NN)
            tot=o[:,64:65] if h==0 else o[:,0:1]
            res.append(o/tot)
            lse.append(m+jnp.log(tot))
        a_ref[rows,:]=jnp.where(leftq,res[0],res[1]).astype(BF)
        lm=jnp.where(leftq,lse[1],lse[0])
        hi,mid,lo=split3(lm)
        j=lq%HEAD_DIM
        base=qf[rows]
        lf_ref[rows,:]=jnp.where(j==4,hi,jnp.where(j==5,mid,jnp.where(j==6,lo,base)))
def attn_fwd(q,k,v,qf,kf,first,npair,deps=(),qb=512):
    n=q.shape[0]
    blk=pl.BlockSpec((n,LANES),lambda i:(0,i+first))
    whole=pl.BlockSpec((n,LANES),lambda i:(0,0))
    out=pl.BlockSpec((n,LANES),lambda i:(0,i))
    return pl.pallas_call(functools.partial(attn_fwd_kernel,qb),grid=(npair,),
        in_specs=[blk,blk,blk,whole,whole]+[ANY]*len(deps),out_specs=[out,out],
        out_shape=[jax.ShapeDtypeStruct((n,npair*LANES),BF)]*2,
        compiler_params=pltpu.CompilerParams(vmem_limit_bytes=FULL),
        cost_estimate=cost(npair*2*2*2*n*n*256,npair*n*LANES*2*5),
        name="attend_forward")(q,k,v,qf,kf,*deps)
def attn_bwd_kernel(qb,q_ref,k_ref,v_ref,da_ref,a_ref,lf_ref,kf_ref,*rest):
    d_ref,dka,dva=rest[-3:]
    n=q_ref.shape[0]
    lane=lax.broadcasted_iota(jnp.int32,(n,LANES),1)
    left=lane<HEAD_DIM
    q=q_ref[...]*jnp.asarray(0.125,BF); k=k_ref[...]; v=v_ref[...]; da=da_ref[...]
    lf=lf_ref[...]; kf=kf_ref[...]
    prod=da.astype(F32)*a_ref[...].astype(F32)
    j=lane%HEAD_DIM
    zero=jnp.zeros_like(q)
    minus=jnp.where((j>=4)&(j<7),jnp.asarray(-1,BF),jnp.asarray(0,BF))
    sides=[]
    for h in range(2):
        own=left if h==0 else ~left
        d=jnp.sum(jnp.where(own,prod,0.0),-1,keepdims=True)
        hi,mid,lo=split3(d)
        df=jnp.where(j==4,hi,jnp.where(j==5,mid,jnp.where(j==6,lo,zero)))
        sides.append((jnp.where(own,q,lf),jnp.where(own,k,kf),jnp.where(own,v,minus),jnp.where(own,da,df),
                      jnp.where(own,q,zero),jnp.where(own,da,zero)))
    kt=k.T
    for c in range(n//qb):
        rows=slice(c*qb,(c+1)*qb)
        dqs=[]; dk=None; dv=None
        for h in range(2):
            qa,ka,va,daa,qz,daz=sides[h]
            s=dg(ka,qa[rows],NT)
            p=jnp.exp(s)
            dp=dg(va,daa[rows],NT)
            ds=(p*dp).astype(BF)
            pb=p.astype(BF)
            x=dg(pb,daz[rows],NN); dv=x if dv is None else dv+x
            y=dg(ds,qz[rows],NN); dk=y if dk is None else dk+y
            dqs.append(dg(kt[h*64:(h+1)*64],ds,NN))
        d_ref[0,rows,:]=(jnp.concatenate(dqs,0).T*0.125).astype(BF)
        if c==0: dka[...]=dk; dva[...]=dv
        else: dka[...]+=dk; dva[...]+=dv
    d_ref[1]=dka[...].astype(BF)
    d_ref[2]=dva[...].astype(BF)
def attn_bwd(q,k,v,da,a,lf,kf,first,npair,skip=0,deps=(),qb=256):
    n=q.shape[0]
    blk=pl.BlockSpec((n,LANES),lambda i:(0,i+first))
    whole=pl.BlockSpec((n,LANES),lambda i:(0,0))
    own=pl.BlockSpec((n,LANES),lambda i:(0,i+skip))
    out=pl.BlockSpec((3,n,LANES),lambda i:(0,0,i))
    return pl.pallas_call(functools.partial(attn_bwd_kernel,qb),grid=(npair,),
        in_specs=[blk]*5+[own,whole]+[ANY]*len(deps),out_specs=out,
        out_shape=jax.ShapeDtypeStruct((3,n,npair*LANES),BF),
        scratch_shapes=[pltpu.VMEM((n,LANES),F32)]*2,
        compiler_params=pltpu.CompilerParams(vmem_limit_bytes=VMEM),
        cost_estimate=cost(npair*2*5*2*n*n*256,npair*n*LANES*2*9),
        name="attend_backward")(q,k,v,da,a,lf,kf,*deps)
def seg_features(seg,pad):
    n=seg.shape[0]
    j=lax.broadcasted_iota(jnp.int32,(n,LANES),1)%HEAD_DIM
    same=(seg[:,None]==j)
    qf=jnp.where((j<4)&same,1.0,0.0).astype(BF)
    kf=jnp.where(j<4,jnp.where(same&(pad[:,None]>0),0.0,-1e30),jnp.where(j<7,-1.0,0.0)).astype(BF)
    return qf,kf


def up_kernel(got, part, ids, x_ref, p_ref, bup_ref, *rest):
    n = len(got.arrays)
    a_refs = rest[: len(rest) - n - 11]
    pieces = rest[len(rest) - n - 11 : len(rest) - 11]
    a_all, y_ref, yb_ref, n_ref, s_ref, g_ref, gp_ref, wu, wo, sems, sems_out = rest[-11:]
    width = x_ref.shape[1]
    targets = [(0, part, wu, part, 0, 0)]

    @pl.when(pl.program_id(0) == 0)
    def _():
        moves = got.copies(pieces, ids, [(0, part, wo, part, 0, 4 * width)], sems_out)
        for m in moves + got.copies(pieces, ids, targets, sems):
            m.start()
        for m in moves:
            m.wait()

    a = jnp.concatenate([r[...] for r in a_refs], 1)
    a_all[...] = a
    r = x_ref[...].astype(F32) + dg(a, wo[...], NN) + p_ref[2:3, :]
    c = r - jnp.mean(r, -1, keepdims=True)
    s = lax.rsqrt(jnp.mean(c * c, -1, keepdims=True) + EPSILON)
    normed = c * s
    y = normed * p_ref[3:4, :] + p_ref[4:5, :]
    y_ref[...] = y
    n_ref[...] = normed.astype(BF)
    s_ref[...] = s
    yb = y.astype(BF)
    yb_ref[...] = yb

    @pl.when(pl.program_id(0) == 0)
    def _():
        for m in got.copies(pieces, ids, targets, sems):
            m.wait()

    step = 512
    for k in range(0, 4 * width, step):
        h = dg(yb, wu[:, k : k + step], NN) + bup_ref[:, k : k + step]
        phi = 0.5 + 0.5 * lax.erf(h * ROOT_HALF)
        g_ref[:, k : k + step] = (h * phi).astype(BF)
        gp_ref[:, k : k + step] = (phi + h * (jnp.exp(-0.5 * h * h) * INV_ROOT_TAU)).astype(BF)


def up_part(x, vecs, bup, a_parts, got, ids, nb, block=256):
    n, width = x.shape
    part = width // nb
    rows = lambda w: pl.BlockSpec((block, w), lambda i, ids: (i, 0))
    whole = lambda shape: pl.BlockSpec(shape, lambda i, ids: (0, 0))
    count = got.count([(0, part, 0, 0, 0)])
    sds = jax.ShapeDtypeStruct
    return pl.pallas_call(
        functools.partial(up_kernel, got, part),
        grid_spec=pltpu.PrefetchScalarGridSpec(
            num_scalar_prefetch=1,
            grid=(n // block,),
            in_specs=[rows(width), whole((8, width)), whole((1, 4 * width))]
            + [rows(a.shape[1]) for a in a_parts]
            + [ANY] * len(got.arrays),
            out_specs=[rows(width), rows(width), rows(width), rows(width), rows(1), rows(4 * width), rows(4 * width)],
            scratch_shapes=[pltpu.VMEM((width, 4 * width), BF), pltpu.VMEM((width, width), BF)] + [pltpu.SemaphoreType.DMA((count,))] * 2,
        ),
        out_shape=[
            sds((n, width), BF),
            sds((n, width), F32),
            sds((n, width), BF),
            sds((n, width), BF),
            sds((n, 1), F32),
            sds((n, 4 * width), BF),
            sds((n, 4 * width), BF),
        ],
        compiler_params=params(FULL),
        cost_estimate=cost(10 * n * width * width, 28 * n * width + 10 * width * width, 8 * n * width),
        name="out_norm_up",
    )(ids, x, vecs, bup, *a_parts, *got.arrays)


def down_kernel(g_ref, y_ref, c_ref, p_ref, wd, o_ref, df_ref, dr_ref, sum_ref):
    @pl.when(pl.program_id(0) == 0)
    def _():
        sum_ref[...] = jnp.zeros_like(sum_ref)

    r = y_ref[...] + dg(g_ref[...], wd[...], NN) + p_ref[5:6, :]
    c = r - jnp.mean(r, -1, keepdims=True)
    s = lax.rsqrt(jnp.mean(c * c, -1, keepdims=True) + EPSILON)
    normed = c * s
    gain = p_ref[6:7, :]
    o_ref[...] = (normed * gain + p_ref[7:8, :]).astype(BF)
    ct = c_ref[...].astype(F32)
    e = ct * gain
    dr = s * (e - jnp.mean(e, -1, keepdims=True) - normed * jnp.mean(e * normed, -1, keepdims=True))
    dr_ref[...] = dr
    df = dr.astype(BF)
    df_ref[...] = df
    sum_ref[0:1, :] += jnp.sum(ct * normed, 0, keepdims=True)
    sum_ref[1:2, :] += jnp.sum(ct, 0, keepdims=True)
    sum_ref[2:3, :] += jnp.sum(df.astype(F32), 0, keepdims=True)


def down_part(g, y, ct, vecs, w_down, block=256):
    n, width = y.shape
    rows = lambda w: pl.BlockSpec((block, w), lambda i: (i, 0))
    whole = lambda shape: pl.BlockSpec(shape, lambda i: (0, 0))
    sds = jax.ShapeDtypeStruct
    return pl.pallas_call(
        down_kernel,
        grid=(n // block,),
        in_specs=[rows(4 * width), rows(width), rows(width), whole((8, width)), whole((4 * width, width))],
        out_specs=[rows(width), rows(width), rows(width), whole((8, width))],
        out_shape=[sds((n, width), BF), sds((n, width), BF), sds((n, width), F32), sds((8, width), F32)],
        compiler_params=params(FULL),
        cost_estimate=cost(8 * n * width * width, 22 * n * width + 8 * width * width),
        name="down_norm",
    )(g, y, ct, vecs, w_down)


def hidden_kernel(df_ref, gp_ref, wd, *rest):
    dh_ref, bup_ref = rest[-2:]

    @pl.when(pl.program_id(0) == 0)
    def _():
        bup_ref[...] = jnp.zeros_like(bup_ref)

    df = df_ref[...]
    width = df.shape[1]
    step = 512
    for k in range(0, dh_ref.shape[1], step):
        dh = (dg(df, wd[k : k + step, :], NT) * gp_ref[:, k : k + step].astype(F32)).astype(BF)
        dh_ref[:, k : k + step] = dh
        row, col = k // width, k % width
        bup_ref[row : row + 1, col : col + step] += jnp.sum(dh.astype(F32), 0, keepdims=True)


def hidden_part(df, gp, w_down, which, deps=(), block=256):
    n, width = df.shape
    cols = w_down.shape[0] // 2
    rows = pl.BlockSpec((block, width), lambda i: (i, 0))
    return pl.pallas_call(
        hidden_kernel,
        grid=(n // block,),
        in_specs=[rows, pl.BlockSpec((block, cols), lambda i: (i, which)), pl.BlockSpec((cols, width), lambda i: (which, 0))]
        + [ANY] * len(deps),
        out_specs=[pl.BlockSpec((block, cols), lambda i: (i, 0)), pl.BlockSpec((8, width), lambda i: (0, 0))],
        out_shape=[jax.ShapeDtypeStruct((n, cols), BF), jax.ShapeDtypeStruct((8, width), F32)],
        compiler_params=params(FULL),
        cost_estimate=cost(2 * n * width * cols, n * (2 * width + 4 * cols) + 2 * width * cols),
        name="hidden_gradient",
    )(df, gp, w_down, *deps)


def back_kernel(up, part, ids, dh_ref, dh2_ref, dr_ref, n_ref, s_ref, p_ref, *rest):
    nu = len(up.arrays)
    pu = rest[:nu]
    dr1_ref, do_ref, da_ref, sum_ref, wu, wo, su, so = rest[-8:]
    width = dr_ref.shape[1]

    @pl.when(pl.program_id(0) == 0)
    def _():
        moves = up.copies(pu, ids, [(0, part, wu, part, 0, 0)], su) + up.copies(pu, ids, [(0, part, wo, part, 0, 4 * width)], so)
        for m in moves:
            m.start()
        sum_ref[...] = jnp.zeros_like(sum_ref)
        for m in moves:
            m.wait()

    cut = dh_ref.shape[1]
    dy = dr_ref[...] + dg(dh_ref[...], wu[:, :cut], NT) + dg(dh2_ref[...], wu[:, cut:], NT)
    normed = n_ref[...].astype(F32)
    e = dy * p_ref[3:4, :]
    dr = s_ref[...] * (e - jnp.mean(e, -1, keepdims=True) - normed * jnp.mean(e * normed, -1, keepdims=True))
    dr1_ref[...] = dr
    do = dr.astype(BF)
    do_ref[...] = do
    da_ref[...] = dg(do, wo[...], NT).astype(BF)
    sum_ref[0:1, :] += jnp.sum(dy * normed, 0, keepdims=True)
    sum_ref[1:2, :] += jnp.sum(dy, 0, keepdims=True)
    sum_ref[2:3, :] += jnp.sum(do.astype(F32), 0, keepdims=True)


def back_part(dh, dr, normed, inverse, vecs, up, ids, nb, deps=(), block=256):
    n, width = dr.shape
    part = width // nb
    rows = lambda w: pl.BlockSpec((block, w), lambda i, ids: (i, 0))
    whole = lambda shape: pl.BlockSpec(shape, lambda i, ids: (0, 0))
    sds = jax.ShapeDtypeStruct
    return pl.pallas_call(
        functools.partial(back_kernel, up, part),
        grid_spec=pltpu.PrefetchScalarGridSpec(
            num_scalar_prefetch=1,
            grid=(n // block,),
            in_specs=[rows(2 * width), rows(2 * width), rows(width), rows(width), rows(1), whole((8, width))]
            + [ANY] * (len(up.arrays) + len(deps)),
            out_specs=[rows(width), rows(width), rows(width), whole((8, width))],
            scratch_shapes=[pltpu.VMEM((width, 4 * width), BF), pltpu.VMEM((width, width), BF)]
            + [pltpu.SemaphoreType.DMA((up.count([(0, part, 0, 0, 0)]),))] * 2,
        ),
        out_shape=[sds((n, width), F32), sds((n, width), BF), sds((n, width), BF), sds((8, width), F32)],
        compiler_params=params(FULL),
        cost_estimate=cost(10 * n * width * width, 22 * n * width + 10 * width * width),
        name="norm_backward",
    )(ids, *dh, dr, normed, inverse, vecs, *up.arrays, *deps)


def sums_kernel(one, two, up0, up1, *rest):
    out = rest[-1]
    out[...] = jnp.zeros_like(out)
    for r, (src, at) in enumerate(((one, 2), (one, 0), (one, 1), (two, 2), (two, 0), (two, 1))):
        out[1 + r : 2 + r, :] = src[at : at + 1, :]
    for r, (src, at) in enumerate(((up0, 0), (up0, 1), (up1, 0), (up1, 1))):
        out[7 + r : 8 + r, :] = src[at : at + 1, :]


def pack_sums(one, two, up0, up1):
    return pl.pallas_call(
        sums_kernel,
        in_specs=[pl.BlockSpec(memory_space=pltpu.VMEM)] * 4,
        out_specs=pl.BlockSpec(memory_space=pltpu.VMEM),
        out_shape=jax.ShapeDtypeStruct((16, one.shape[1]), F32),
        compiler_params=params(4 << 20),
        cost_estimate=cost(0, 1 << 20),
        name="pack_sums",
    )(one, two, up0, up1)


def grad_rows_kernel(top, jb, lo, ls, ro, rs, *rest):
    ka, sa, kb, sb = rest[-4:]
    j = pl.program_id(0)
    half = ka.shape[1]
    got = (dg(lo[...], ro[...], TN) + dg(ls[...], rs[...], TN)).astype(BF)

    @pl.when(j % 2 == 0)
    def _():
        ka[0] = got[:half]

    @pl.when(j % 2 == 1)
    def _():
        sa[0] = got[:half]

    @pl.when(j < top)
    def _():
        kb[0] = got[half:]

    @pl.when(j >= top)
    def _():
        sb[0] = got[half:]


def grad_down(g_own, g_sib, df_own, df_sib, jb, nf, deps=()):
    n, hidden = g_own.shape
    width = df_own.shape[1]
    part = hidden // (2 * nf)
    top = nf // 2
    left = pl.BlockSpec((n, part), lambda j, jb: (0, jb[j]))
    right = pl.BlockSpec((n, width), lambda j, jb: (0, 0))
    out = lambda at: pl.BlockSpec((1, part // 2, width), lambda j, jb: (at(j), 0, 0))
    return pl.pallas_call(
        functools.partial(grad_rows_kernel, top),
        grid_spec=pltpu.PrefetchScalarGridSpec(
            num_scalar_prefetch=1,
            grid=(nf,),
            in_specs=[left, left, right, right] + [ANY] * len(deps),
            out_specs=[
                out(lambda j: j // 2),
                out(lambda j: j // 2),
                out(lambda j: jnp.minimum(j, top - 1)),
                out(lambda j: jnp.maximum(j - top, 0)),
            ],
        ),
        out_shape=[jax.ShapeDtypeStruct((top, part // 2, width), BF)] * 4,
        compiler_params=params(FULL),
        cost_estimate=cost(2 * n * hidden * width, 2 * n * hidden + 4 * n * width + hidden * width),
        name="grad_down",
    )(jb, g_own, g_sib, df_own, df_sib, *deps)


class Job:
    def __init__(self, left, rights):
        self.left, self.rights = left, rights


EXTRA = 16


def grad_cols_kernel(jobs, nl, nf, block, keeps, extra, sum_blocks, *refs):
    pos = 1
    step = pl.program_id(0)
    lefts, rights = [], []
    for spans in jobs:
        lefts.append((refs[pos : pos + nl], refs[pos + nl : pos + 2 * nl]))
        pos += 2 * nl
    for spans in jobs:
        for _ in spans:
            rights.append((refs[pos], refs[pos + 1]))
            pos += 2
    if sum_blocks:
        vec_own, vec_sib = refs[pos : pos + 2]
    outs = refs[len(refs) - len(jobs) - 4 : len(refs) - len(jobs)]
    lts = refs[len(refs) - len(jobs) :]
    n, wide = lefts[0][0][0].shape
    part = nl * wide // nf
    half = part // 2
    at = 0
    for (los, lss), spans, lt in zip(lefts, jobs, lts):

        @pl.when(step == spans[0][0])
        def _():
            for j in range(nl):
                lt[j * wide : (j + 1) * wide, 0:n] = los[j][...].T
                lt[j * wide : (j + 1) * wide, n : 2 * n] = lss[j][...].T

        for begin, count in spans:
            own, sib = rights[at]
            at += 1

            @pl.when((step >= begin) & (step < begin + count))
            def _():
                both = jnp.concatenate([own[0], sib[0]], 0)
                got = dg(lt[...], both, NN).astype(BF)
                for out, (which, side) in zip(outs, keeps):
                    for m, j in enumerate(which):
                        out[m, 0:half, :] = got[j * part + side * half : j * part + (side + 1) * half]
                if extra:
                    tile = jnp.zeros((EXTRA, block), F32)
                    if sum_blocks:
                        tile = jnp.where(step < sum_blocks, vec_own[...] + vec_sib[...], 0.0)
                    columns = jnp.sum(both.astype(F32), 0, keepdims=True)
                    tile = jnp.where(lax.broadcasted_iota(jnp.int32, (EXTRA, block), 0) == 0, columns, tile).astype(BF)
                    for out in outs:
                        for m in range(out.shape[0]):
                            out[m, half : half + EXTRA, :] = tile


def grad_cols(jobs, jb, nf, block, name, deps=(), extra=False, vecs=None):
    n, width = jobs[0].left[0].shape
    part = width // (2 * nf)
    spans, step = [], 0
    in_specs, operands, right_specs, right_ops = [], [], [], []
    for job in jobs:
        mine = []
        pick = lambda z: z.reshape(n, 2 * nf, part)[:, jb].reshape(n, nf * part)
        for z in job.left:
            if part % LANES == 0:
                nl = nf
                in_specs += [pl.BlockSpec((n, part), lambda i, jb, j=j: (0, jb[j])) for j in range(nf)]
                operands += [z] * nf
            else:
                nl = 1
                in_specs += [pl.BlockSpec((n, nf * part), lambda i, jb: (0, 0))]
                operands += [pick(z)]
        for own, sib in job.rights:
            planes, _, cols = own.shape
            per = cols // block
            count = planes * per

            def at(i, jb, step=step, count=count, per=per):
                k = jnp.clip(i - step, 0, count - 1)
                return (k // per, 0, k % per)

            right_specs += [pl.BlockSpec((1, n, block), at)] * 2
            right_ops += [own, sib]
            mine.append((step, count))
            step += count
        spans.append(mine)
    half = part // 2
    sum_blocks = 0
    if vecs is not None:
        sum_blocks = vecs[0].shape[1] // block
        right_specs += [pl.BlockSpec((EXTRA, block), lambda i, jb: (0, jnp.minimum(i, sum_blocks - 1)))] * 2
        right_ops += list(vecs)
    js = list(range(nf))
    top = nf // 2
    keeps = [([j for j in js if not j & 1], 0), ([j for j in js if j & 1], 0), ([j for j in js if j < top], 1), ([j for j in js if j >= top], 1)]
    lines = half + (EXTRA if extra else 0)
    out_spec = pl.BlockSpec((nf // 2, lines, block), lambda i, jb: (0, 0, i))
    out_shape = jax.ShapeDtypeStruct((nf // 2, lines, step * block), BF)
    return pl.pallas_call(
        functools.partial(grad_cols_kernel, spans, nl, nf, block, keeps, extra, sum_blocks),
        grid_spec=pltpu.PrefetchScalarGridSpec(
            num_scalar_prefetch=1,
            grid=(step,),
            in_specs=in_specs + right_specs + [ANY] * len(deps),
            out_specs=[out_spec] * 4,
            scratch_shapes=[pltpu.VMEM((nf * part, 2 * n), BF)] * len(jobs),
        ),
        out_shape=[out_shape] * 4,
        compiler_params=params(),
        cost_estimate=cost(2 * n * width * step * block, 4 * n * (step * block + width // 2)),
        name=name,
    )(jb, *operands, *right_ops, *deps)


def input_kernel(got, part, groups, place, ids, dr_ref, *rest):
    n = len(got.arrays)
    d_refs, pieces = rest[1 : 1 + groups], rest[1 + groups : 1 + groups + n]
    out_ref, wq, wk, wv, sems = rest[-5:]
    targets = qkv_targets(part, wq, wk, wv)

    @pl.when(pl.program_id(0) == 0)
    def _():
        moves = got.copies(pieces, ids, targets, sems)
        for c in moves:
            c.start()
        for c in moves:
            c.wait()

    total = dr_ref[...]
    for k, w in enumerate((wq, wk, wv)):
        d = jnp.concatenate([r[k] for r in d_refs], 1)
        total += dg(d, w[...], NT)
    out_ref[...] = total


def input_part(dr, grads, got, ids, place, nb, deps=(), block=256):
    n, width = dr.shape
    steps = n // 2 // block
    rows = pl.BlockSpec((block, width), lambda i, ids: (i + ids[ids.shape[0] - 2 + place] * steps, 0))
    three = lambda w: pl.BlockSpec((3, block, w), lambda i, ids: (0, i + ids[ids.shape[0] - 2 + place] * steps, 0))
    count = got.count(qkv_targets(width // nb, 0, 0, 0))
    return pl.pallas_call(
        functools.partial(input_kernel, got, width // nb, len(grads), place),
        grid_spec=pltpu.PrefetchScalarGridSpec(
            num_scalar_prefetch=1,
            grid=(steps,),
            in_specs=[rows, ANY] + [three(a.shape[2]) for a in grads] + [ANY] * (len(got.arrays) + len(deps)),
            out_specs=pl.BlockSpec((block, width), lambda i, ids: (i, 0)),
            scratch_shapes=[pltpu.VMEM((width, width), BF)] * 3 + [pltpu.SemaphoreType.DMA((count,))],
        ),
        out_shape=jax.ShapeDtypeStruct((n // 2, width), F32),
        compiler_params=params(FULL),
        cost_estimate=cost(3 * n * width * width, 7 * n * width + 6 * width * width),
        name="input_gradient",
    )(ids, dr, dr, *grads, *got.arrays, *deps)


def add_low(a, b):
    return (a[...].astype(F32) + b[...].astype(F32)).astype(BF)


SMALL = 16 << 20


def tile_of(cols):
    return cols // 2 if cols % (2 * LANES) == 0 else cols


def stage_kernel(last, odd, ka, ra, kb, rb, *rest):
    outs = rest[len(rest) - (2 if last else 4) :]
    a, b = add_low(ka, ra), add_low(kb, rb)
    m = a.shape[0]
    if last:
        swapped = odd[0] == 1
        outs[0][...] = jnp.where(swapped, b, a)
        outs[1][...] = jnp.where(swapped, a, b)
    else:
        for i in range(m // 2):
            outs[0][i], outs[1][i] = a[2 * i], a[2 * i + 1]
            outs[2][i], outs[3][i] = b[i], b[m // 2 + i]


def stage(odd, ka, ra, kb, rb, deps):
    m, rows, cols = ka.shape
    block = tile_of(cols)
    last = m == 1
    into = pl.BlockSpec((m, rows, block), lambda i, odd: (0, 0, i))
    mo = max(m // 2, 1)
    out = pl.BlockSpec((mo, rows, block), lambda i, odd: (0, 0, i))
    return pl.pallas_call(
        functools.partial(stage_kernel, last),
        grid_spec=pltpu.PrefetchScalarGridSpec(
            num_scalar_prefetch=1,
            grid=(cols // block,),
            in_specs=[into] * 4 + [ANY] * len(deps),
            out_specs=[out] * (2 if last else 4),
        ),
        out_shape=[jax.ShapeDtypeStruct((mo, rows, cols), BF)] * (2 if last else 4),
        compiler_params=params(9 << 20),
        cost_estimate=cost(0, 12 * m * rows * cols),
        name="sum_plane",
    )(odd, ka, ra, kb, rb, *deps)


def pair_sum_kernel(a, b, *rest):
    rest[-1][...] = add_low(a, b)


def pair_sum(a, b, deps):
    rows, cols = a.shape
    block = tile_of(cols)
    spec = pl.BlockSpec((rows, block), lambda i: (0, i))
    return pl.pallas_call(
        pair_sum_kernel,
        grid=(cols // block,),
        in_specs=[spec] * 2 + [ANY] * len(deps),
        out_specs=spec,
        out_shape=jax.ShapeDtypeStruct((rows, cols), BF),
        compiler_params=params(4 << 20),
        cost_estimate=cost(0, 6 * rows * cols),
        name="sum_rep",
    )(a, b, *deps)


def pick_kernel(odd, a, b, *rest):
    rest[-2][...], rest[-1][...] = a[...], b[...]


def pick(odd, v, deps=()):
    rows, cols = v.shape
    block = tile_of(cols)
    spec = lambda flip: pl.BlockSpec((rows // 2, block), lambda i, odd: ((odd[0] + flip) % 2, i))
    out = pl.BlockSpec((rows // 2, block), lambda i, odd: (0, i))
    return pl.pallas_call(
        pick_kernel,
        grid_spec=pltpu.PrefetchScalarGridSpec(
            num_scalar_prefetch=1, grid=(cols // block,), in_specs=[spec(0), spec(1)] + [ANY] * len(deps), out_specs=[out, out]
        ),
        out_shape=[jax.ShapeDtypeStruct((rows // 2, cols), BF)] * 2,
        compiler_params=params(4 << 20),
        cost_estimate=cost(0, 4 * rows * cols),
        name="pick_half",
    )(odd, v, v, *deps)


class RepChain:
    def __init__(self, kept, sent, nr, odd):
        self.kept, self.sent, self.nr, self.odd = kept, sent, nr, odd

    def rep_first(self, deps=()):
        self.kept = pair_sum(self.kept, swap(self.sent, "rep", self.nr, 1), deps)
        return (self.kept,)

    def rep_middle(self, deps=()):
        xor = 2
        while xor < self.nr:
            self.kept = pair_sum(self.kept, swap(self.kept, "rep", self.nr, xor), deps)
            xor *= 2
        return (self.kept,)

    def rep_middle_part(self, which, deps=()):
        if self.nr != 4:
            return self.rep_middle(deps) if which == 1 else ()
        rows = self.kept.shape[0] // 2
        part = self.kept[:rows] if which == 0 else self.kept[rows:]
        part = pair_sum(part, swap(part, "rep", self.nr, 2), deps)
        if which == 0:
            self.first_part = part
        else:
            self.kept = jnp.concatenate([self.first_part, part], 0)
        return (part,)

    def rep_last(self):
        self.other = swap(self.kept, "rep", self.nr, 1)
        return (self.other,)

    def halves(self):
        odd = self.odd[0] == 1
        return jnp.where(odd, self.other, self.kept).astype(F32), jnp.where(odd, self.kept, self.other).astype(F32)

    def result(self):
        return jnp.concatenate(self.halves(), 0)


class Chain(RepChain):
    def __init__(self, parts, nf, nr, odd):
        self.nf, self.nr, self.odd = nf, nr, odd
        self.ka, self.sa, self.kb, self.sb = parts
        self.level, self.bits = 0, nf.bit_length() - 1

    def plane(self, deps=()):
        a, b = self.level, self.bits - 1 - self.level
        ra, rb = swap(self.sa, "fsdp", self.nf, 1 << a), swap(self.sb, "fsdp", self.nf, 1 << b)
        self.level += 1
        out = stage(self.odd, self.ka, ra, self.kb, rb, deps)
        if self.level == self.bits:
            self.kept, self.sent = out[0][0], out[1][0]
        else:
            self.ka, self.sa, self.kb, self.sb = out
        return tuple(out)

    def rest(self, deps=()):
        out = ()
        while self.level < self.bits:
            out = self.plane(deps)
        return out


def join_kernel(odd, kept, other, *rest):
    out = rest[-1]
    rows = kept.shape[0]
    swapped = odd[0] == 1
    out[:rows, :] = jnp.where(swapped, other[...], kept[...]).astype(F32)
    out[rows:, :] = jnp.where(swapped, kept[...], other[...]).astype(F32)


def join(chain, deps=()):
    rows, cols = chain.kept.shape
    block = cols // 2
    spec = pl.BlockSpec((rows, block), lambda i, odd: (0, i))
    return pl.pallas_call(
        join_kernel,
        grid_spec=pltpu.PrefetchScalarGridSpec(
            num_scalar_prefetch=1,
            grid=(2,),
            in_specs=[spec] * 2 + [ANY] * len(deps),
            out_specs=pl.BlockSpec((2 * rows, block), lambda i, odd: (0, i)),
        ),
        out_shape=jax.ShapeDtypeStruct((2 * rows, cols), F32),
        compiler_params=params(8 << 20),
        cost_estimate=cost(0, 12 * rows * cols),
        name="join_halves",
    )(chain.odd, chain.kept, chain.other, *deps)


def finish_kernel(half, width, wide, counts, odd, *refs):
    n = len(counts)
    q, k, v, o, small, line = refs[2 * n :]
    for at in range(2):
        rows = slice(at * half, (at + 1) * half)
        group, lines = 0, []
        for i, count in enumerate(counts):
            both = jnp.where(odd[0] == at, refs[2 * i][...], refs[2 * i + 1][...]).astype(F32)
            col = 0
            if i == 0:
                o[rows, :] = both[:half, :width]
                if at == 0:
                    small[...] = both[half : half + EXTRA, :width]
                col = width
            lines.append(both[half : half + 8, col:])
            for _ in range(count):
                for out in (q, k, v):
                    out[rows, group * wide : (group + 1) * wide] = both[:half, col : col + wide]
                    col += wide
                group += 1
        if at == 0:
            line[...] = jnp.concatenate(lines, 1)


def finish(odd, chains, counts, half, width, wide):
    spec = pl.BlockSpec(memory_space=pltpu.VMEM)
    sds = jax.ShapeDtypeStruct
    return pl.pallas_call(
        functools.partial(finish_kernel, half, width, wide, counts),
        in_specs=[pl.BlockSpec(memory_space=pltpu.SMEM)] + [spec] * (2 * len(chains)),
        out_specs=[spec] * 6,
        out_shape=[sds((2 * half, width), F32)] * 4 + [sds((EXTRA, width), F32), sds((8, 3 * wide * sum(counts)), F32)],
        compiler_params=params(12 << 20),
        cost_estimate=cost(0, 6 << 20),
        name="finish",
    )(odd, *[z for c in chains for z in (c.kept, c.other)])


def body(tokens, segment_ids, padding, cotangent, w_query, w_key, w_value, w_out, b_query, b_value, b_out,
         gain_one, shift_one, w_up, b_up, w_down, b_down, gain_two, shift_two, *, nr, nf, ns):
    _, part_len, width = tokens.shape
    f, c = lax.axis_index("fsdp"), lax.axis_index("seq")
    rel = [((f ^ j) * 2 + (c ^ p)) for j in range(nf) for p in range(2)]
    absolute = [(j * 2 + (c ^ p)) for j in range(nf) for p in range(2)]
    ids = jnp.stack(rel + absolute + [1 - c, c]).astype(jnp.int32)
    jb = jnp.stack(rel[::2]).astype(jnp.int32)
    jb_abs = jnp.stack(absolute[::2]).astype(jnp.int32)
    core = c.astype(jnp.int32).reshape(1)
    odd = (lax.axis_index("rep") & 1).astype(jnp.int32).reshape(1)
    sib_of = lambda z: swap(z, "seq", ns, 1)
    nb = 2 * nf
    part = width // nb

    qkv_shard = pack_first(
        [b_query, b_value, b_out, gain_one, shift_one, b_down, gain_two, shift_two, b_up], [w_query, w_key, w_value]
    )
    first = gather_start(qkv_shard, nf)
    x, x_sib, ct = pair_up(core, [(tokens, sib_of(tokens), 2), (cotangent, sib_of(cotangent), 1)])
    marks = jnp.stack([segment_ids, padding])
    theirs = sib_of(marks)
    own = c == 0
    mine_m, their_m = jnp.where(own, marks[:, 0], marks[:, 1]), jnp.where(own, theirs[:, 0], theirs[:, 1])
    whole = jnp.where(own, jnp.concatenate([mine_m, their_m], 1), jnp.concatenate([their_m, mine_m], 1))
    qf, kf = seg_features(whole[0], whole[1])
    (up_shard,) = split_rows(
        [w_up, w_out], [(0, 0, part, 0, 0, 0), (1, 0, part, 0, 0, 4 * width)], [(part, 5 * width)], (), "pack_up"
    )
    far = gather_far(first, nf, (up_shard,))
    gate = tuple(far) or tuple(first)
    got_qkv, _ = gather_end(qkv_shard, first, far, nf, ns, (), (x, qf))
    first_up = gather_start(after(up_shard, x, *gate), nf)
    q, k, v, vecs, bup = project(x, got_qkv, ids, nb)

    pairs = width // LANES
    groups = 4
    each = pairs // groups
    fwd = [attn_fwd(q, k, v, qf, kf, 0, each)]
    fwd.append(attn_fwd(q, k, v, qf, kf, each, each, (fwd[0][0],)))
    far_up = gather_far(first_up, nf, (fwd[1][0],))
    full_down = lax.all_gather(after(w_down, fwd[1][0], *first_up), ("fsdp", "seq"), axis=0, tiled=True)
    fwd.append(attn_fwd(q, k, v, qf, kf, 2 * each, 2 * each, (fwd[1][0],) + tuple(first_up)))
    got_up, swaps = gather_end(up_shard, first_up, far_up, nf, ns, (fwd[2][0],))
    lf = [(fwd[0][1], 0), (fwd[1][1], 0), (fwd[2][1], 0), (fwd[2][1], each)]

    a_all, y, yb, normed, inverse, g, gp = up_part(x, vecs, bup, [r[0] for r in fwd], got_up, ids, nb)
    a_sib, yb_sib, g_sib = sib_of(a_all), sib_of(yb), sib_of(g)
    out, df, dr, sums_two = down_part(g, y, ct, vecs, full_down)
    df_sib = sib_of(after(df, yb_sib, a_sib))
    dh0, sum_up0 = hidden_part(df, gp, full_down, 0, (yb_sib, a_sib))
    dh0_sib = sib_of(after(dh0, df_sib, g_sib))
    dh1, sum_up1 = hidden_part(df, gp, full_down, 1, (dh0, df_sib, g_sib))
    dh1_sib = sib_of(after(dh1, dh0_sib))
    g_down = grad_down(g, g_sib, df, df_sib, jb, nf, (dh1, dh0_sib))
    chain_down = Chain(after(g_down, dh1_sib), nf, nr, odd)
    g_up = grad_cols([Job((yb, yb_sib), [(dh0[None], dh0_sib[None]), (dh1[None], dh1_sib[None])])], jb, nf, 1024, "grad_up", (g_down[0],))
    out_sib = sib_of(after(out, dh0_sib))
    output = unpair_up(core, *after((out, out_sib), g_up[0]), part_len)
    now = chain_down.plane((g_up[0], output))
    g_up = after(g_up, *now)
    chain_up = Chain(g_up, nf, nr, odd)
    dr1, do, da, sums_one = back_part((dh0, dh1), dr, normed, inverse, vecs, got_up, ids, nb, now + (g_up[0],))
    now = chain_down.rest((da,))
    do_sib = sib_of(after(do, *now))
    sums = pack_sums(*after((sums_one, sums_two, sum_up0, sum_up1), *now))

    grads, sibs = [], []

    def run(i, deps):
        grads.append(attn_bwd(q, k, v, da, a_all, lf[i][0], kf, i * each, each, lf[i][1], deps))
        return (grads[-1],)

    def send(i, deps):
        sibs.append(sib_of(after(grads[i], *deps)))

    dep = run(0, (da,) + now)
    now = chain_up.plane(dep) + chain_down.rep_first(dep)
    send(0, now)
    sums_sib = sib_of(after(sums, *now))
    dep = run(1, dep + now + (output, do_sib, sums_sib, sibs[0]))
    now = chain_up.rest(dep) + chain_down.rep_middle(dep)
    chain_down.rep_last()
    send(1, now)
    g_one = grad_cols(
        [Job((a_all, a_sib), [(do[None], do_sib[None])]), Job((x, x_sib), [(grads[0], sibs[0])])],
        jb, nf, 256, "grad_out_qkv", dep + now, True, (sums, sums_sib),
    )
    dep = (g_one[0],)
    now = chain_up.rep_first(dep)
    chain_one = Chain(after(g_one, *now), nf, nr, odd)
    dep = run(2, dep + now + (sibs[1],))
    final_down = join(chain_down, dep)
    now = chain_one.plane(dep) + chain_up.rep_middle_part(0, dep) + (final_down,)
    send(2, now)
    g_two = grad_cols([Job((x, x_sib), [(grads[i], sibs[i]) for i in (1, 2)])], jb, nf, 256, "grad_qkv", dep + now, True)
    dep = (g_two[0],)
    now = chain_one.rest(dep) + chain_up.rep_middle_part(1, dep)
    chain_up.rep_last()
    chain_two = Chain(after(g_two, *now), nf, nr, odd)
    dep = run(3, dep + now)
    now = chain_two.plane(dep) + chain_one.rep_first(dep)
    send(3, now)
    g_three = grad_cols([Job((x, x_sib), [(grads[3], sibs[3])])], jb, nf, 256, "grad_qkv", dep + now, True)
    dep = (g_three[0],)
    now = chain_two.rest(dep)
    chain_three = Chain(after(g_three, *now), nf, nr, odd)
    send_half = input_part(dr1, grads, got_qkv, ids, 0, nb, dep + now)
    dep = (send_half,)
    now = chain_three.plane(dep) + chain_one.rep_middle(dep) + chain_two.rep_first(dep)
    chain_one.rep_last()
    their_half = sib_of(after(send_half, *now))
    keep_half = input_part(dr1, grads, got_qkv, ids, 1, nb, dep + now)
    dep = (keep_half,)
    now = chain_three.rest(dep) + chain_two.rep_middle(dep)
    final_up = join(chain_up, dep + now)
    chain_two.rep_last()
    input_grad = unpair_up(core, *after((keep_half, their_half), *now), part_len)
    chain_three.rep_first()
    chain_three.rep_middle((input_grad,))
    chain_three.rep_last()
    half = part // 2
    wide = each * LANES
    final_q, final_k, final_v, final_out, small, line = finish(odd, (chain_one, chain_two, chain_three), (1, 2, 1), half, width, wide)
    line = line[0].reshape(groups, 3, wide)
    vectors = jnp.concatenate([line[:, 0].reshape(1, width), line[:, 2].reshape(1, width), small[1:7]], 0)
    own_block = 2 * f + c
    v8 = lax.dynamic_slice(vectors, (0, own_block * part), (8, part))
    final_bup = lax.dynamic_slice(small[7:11].reshape(-1), (own_block * 4 * part,), (4 * part,))
    return (output, input_grad, final_q, final_k, final_v, final_out, v8[0], v8[1], v8[2], v8[3], v8[4],
            final_up, final_bup, final_down, v8[5], v8[6], v8[7])


def solution(mesh):
    tok = P(("rep", "fsdp"), "seq", None)
    ids = P(("rep", "fsdp"), "seq")
    mat = P(("fsdp", "seq"), None)
    vec = P(("fsdp", "seq"))
    sizes = mesh.shape
    return jax.shard_map(
        functools.partial(body, nr=sizes["rep"], nf=sizes["fsdp"], ns=sizes["seq"]),
        mesh=mesh,
        in_specs=(tok, ids, ids, tok) + (mat,) * 4 + (vec,) * 5 + (mat, vec, mat) + (vec,) * 3,
        out_specs=(tok, tok) + (mat,) * 4 + (vec,) * 5 + (mat, vec, mat) + (vec,) * 3,
        check_vma=False,
    )
```

```python
import functools
import math
import jax
import jax.numpy as jnp
from jax import lax
from jax.experimental import pallas as pl
from jax.experimental.pallas import tpu as pltpu
from jax.sharding import PartitionSpec as P

F32 = jnp.float32
BF = jnp.bfloat16
HEAD_DIM = 64
LANES = 128
EPSILON = 1e-05
ROOT_HALF = 0.7071067811865476
INV_ROOT_TAU = 0.3989422804014327
NT = (((1,), (1,)), ((), ()))
TN = (((0,), (0,)), ((), ()))
NN = (((1,), (0,)), ((), ()))
VMEM = 48 << 20
FULL = 58 << 20
SHRINK = 1
ANY = pl.BlockSpec(memory_space=pl.ANY)


def dg(a, b, dims):
    return lax.dot_general(a, b, dims, preferred_element_type=F32)


def params(limit=VMEM):
    return pltpu.CompilerParams(vmem_limit_bytes=limit)


def cost(flops, bytes_accessed, trans=0):
    return pl.CostEstimate(flops=flops // SHRINK, bytes_accessed=bytes_accessed // SHRINK, transcendentals=trans // SHRINK)


def swap(x, axis, size, xor):
    return lax.ppermute(x, axis, [(i, i ^ xor) for i in range(size)])


def after(x, *deps):
    return lax.optimization_barrier((x,) + deps)[0]


class Gathered:
    def __init__(self, arrays, entries, half):
        self.arrays, self.entries, self.half = arrays, entries, half

    def copies(self, refs, ids, targets, sems):
        out = []
        for which, index, base, half, slot in self.entries:
            low = half * self.half
            for first, rows, dest, stride, offset, *column in targets:
                a, b = max(first, low), min(first + rows, low + self.half)
                if a >= b:
                    continue
                place = (*index, pl.ds(base + a - low, b - a))
                if column:
                    place += (pl.ds(column[0], dest.shape[1]),)
                src = refs[which].at[place]
                start = pl.multiple_of(ids[slot] * stride + (offset + a - first), 16)
                out.append(pltpu.make_async_copy(src, dest.at[pl.ds(start, b - a)], sems.at[len(out)]))
        return out

    def count(self, targets):
        n = 0
        for _, _, _, half, _ in self.entries:
            low = half * self.half
            n += sum(max(t[0], low) < min(t[0] + t[1], low + self.half) for t in targets)
        return n


def gather_start(shard, nf):
    if nf == 4:
        return [swap(shard, "fsdp", nf, 1), swap(shard, "fsdp", nf, 2)]
    return [lax.all_gather(shard, "fsdp", axis=0)]


def gather_far(first, nf, deps=()):
    if nf == 4:
        half = first[0].shape[0] // 2
        shape = (half, first[0].shape[1])
        one, two = split_rows(first, [(0, 0, half, 0, 0, 0), (1, half, half, 1, 0, 0)], [shape, shape], deps, "cut_halves")
        return [swap(one, "fsdp", nf, 2), swap(two, "fsdp", nf, 1)]
    return []


def gather_end(shard, first, far, nf, ns, late=(), early=()):
    half = shard.shape[0] // 2
    if nf == 4:
        arrays = [shard, *first, *far]
        entries = [(w, (), h * half, h, 2 * w) for w in range(3) for h in range(2)]
        entries += [(3, (), 0, 0, 6), (4, (), 0, 1, 6)]
    else:
        arrays = list(first)
        entries = [(0, (f,), h * half, h, 2 * nf + 2 * f) for f in range(nf) for h in range(2)]
    n = len(arrays)
    swaps = [swap(after(a, *early) if early else a, "seq", ns, 1) for a in arrays[: n - len(far)]]
    swaps += [swap(after(a, *late), "seq", ns, 1) for a in arrays[n - len(far) :]]
    arrays = arrays + swaps
    entries = entries + [(w + n, i, r, h, s + 1) for w, i, r, h, s in entries]
    return Gathered(arrays, entries, half), swaps


BIAS_ROWS = 32


def split_kernel(moves, nin, nout, *refs):
    ins, outs, sems = refs[:nin], refs[len(refs) - nout - 1 : -1], refs[-1]
    copies = [
        pltpu.make_async_copy(ins[s].at[pl.ds(first, rows)], outs[d].at[pl.ds(to, rows), pl.ds(col, ins[s].shape[1])], sems.at[i])
        for i, (s, first, rows, d, to, col) in enumerate(moves)
    ]
    for m in copies:
        m.start()
    for m in copies:
        m.wait()


def split_rows(ins, moves, out_shapes, deps, name):
    return pl.pallas_call(
        functools.partial(split_kernel, moves, len(ins), len(out_shapes)),
        in_specs=[ANY] * (len(ins) + len(deps)),
        out_specs=[pl.BlockSpec(memory_space=pltpu.VMEM)] * len(out_shapes),
        out_shape=[jax.ShapeDtypeStruct(o, BF) for o in out_shapes],
        scratch_shapes=[pltpu.SemaphoreType.DMA((len(moves),))],
        compiler_params=params(58 << 20),
        cost_estimate=cost(0, 1 << 20),
        name=name,
    )(*ins, *deps)


def bias_kernel(nvec, *refs):
    vecs, mats, out = refs[:nvec], refs[nvec : nvec + 3], refs[nvec + 3]
    held, tile, sems = refs[nvec + 4 : 2 * nvec + 4], refs[-2], refs[-1]
    part = mats[0].shape[0]
    moves = [pltpu.make_async_copy(m, out.at[pl.ds(i * part, part)], sems.at[i]) for i, m in enumerate(mats)]
    small = [pltpu.make_async_copy(v, h, sems.at[3 + i]) for i, (v, h) in enumerate(zip(vecs, held))]
    for m in small + moves:
        m.start()
    tile[...] = jnp.zeros_like(tile)
    for m in small:
        m.wait()
    for i in range(8):
        tile[0:1, i * part : (i + 1) * part] = held[i][...].astype(F32).reshape(1, part)
    tile[1:2, 0 : 4 * part] = held[8][...].astype(F32).reshape(1, 4 * part)
    out[3 * part :, :] = tile[...].astype(BF)
    for m in moves:
        m.wait()


def pack_first(vecs, mats):
    part, width = mats[0].shape
    n = len(vecs)
    return pl.pallas_call(
        functools.partial(bias_kernel, n),
        in_specs=[ANY] * (n + 3),
        out_specs=pl.BlockSpec(memory_space=pltpu.VMEM),
        out_shape=jax.ShapeDtypeStruct((3 * part + BIAS_ROWS, width), BF),
        scratch_shapes=[pltpu.VMEM(v.shape, BF) for v in vecs] + [pltpu.VMEM((BIAS_ROWS, width), F32), pltpu.SemaphoreType.DMA((n + 3,))],
        compiler_params=params(58 << 20),
        cost_estimate=cost(0, 1 << 20),
        name="pack_first",
    )(*vecs, *mats)


def pair_kernel(count, core, *refs):
    ins, outs, sems = refs[: 2 * len(count)], refs[len(refs) - 1 - sum(count) : -1], refs[-1]
    c = core[0]
    at, moves = 0, []
    for i, n in enumerate(count):
        mine, theirs = ins[2 * i], ins[2 * i + 1]
        half = mine.shape[1]
        for k in range(n):
            which = c if k == 0 else 1 - c
            for src, place in ((mine, c), (theirs, 1 - c)):
                start = pl.multiple_of(place * half, half)
                moves.append(pltpu.make_async_copy(src.at[which], outs[at].at[pl.ds(start, half)], sems.at[len(moves)]))
            at += 1
    for m in moves:
        m.start()
    for m in moves:
        m.wait()


def pair_up(core, items, deps=()):
    count = [n for _, _, n in items]
    flat = [z for a, b, _ in items for z in (a, b)]
    shapes = [jax.ShapeDtypeStruct((2 * a.shape[1], a.shape[2]), a.dtype) for a, _, n in items for _ in range(n)]
    return pl.pallas_call(
        functools.partial(pair_kernel, count),
        grid_spec=pltpu.PrefetchScalarGridSpec(
            num_scalar_prefetch=1,
            grid=(1,),
            in_specs=[ANY] * (len(flat) + len(deps)),
            out_specs=[pl.BlockSpec(z.shape, lambda i, core: (0, 0)) for z in shapes],
            scratch_shapes=[pltpu.SemaphoreType.DMA((2 * len(shapes),))],
        ),
        out_shape=shapes,
        compiler_params=params(58 << 20),
        cost_estimate=cost(0, 1 << 20),
        name="pair_up",
    )(core, *flat, *deps)


def unpair_kernel(core, own, theirs, *rest):
    out, sems = rest[-2:]
    c = core[0]
    half = out.shape[1]
    start = pl.multiple_of(c * half, half)
    cut = lambda z: z.at[pl.ds(start, half)] if z.shape[0] > half else z
    one = pltpu.make_async_copy(cut(own), out.at[c], sems.at[0])
    two = pltpu.make_async_copy(cut(theirs), out.at[1 - c], sems.at[1])
    one.start()
    two.start()
    one.wait()
    two.wait()


def unpair_up(core, own, theirs, half, deps=()):
    width = own.shape[1]
    return pl.pallas_call(
        unpair_kernel,
        grid_spec=pltpu.PrefetchScalarGridSpec(
            num_scalar_prefetch=1,
            grid=(1,),
            in_specs=[ANY] * (2 + len(deps)),
            out_specs=pl.BlockSpec((2, half, width), lambda i, core: (0, 0, 0)),
            scratch_shapes=[pltpu.SemaphoreType.DMA((2,))],
        ),
        out_shape=jax.ShapeDtypeStruct((2, half, width), own.dtype),
        compiler_params=params(58 << 20),
        cost_estimate=cost(0, 1 << 20),
        name="unpair",
    )(core, own, theirs, *deps)


def qkv_kernel(got, ids, x_ref, *rest):
    n = len(got.arrays)
    pieces = rest[:n]
    q_ref, k_ref, v_ref, p_ref, b_ref, wq, wk, wv, wb, sems = rest[-10:]
    width = x_ref.shape[1]
    nb = wb.shape[0] // BIAS_ROWS
    part = width // nb
    targets = qkv_targets(part, wq, wk, wv, wb)

    @pl.when(pl.program_id(0) == 0)
    def _():
        moves = got.copies(pieces, ids, targets, sems)
        for m in moves:
            m.start()
        for m in moves:
            m.wait()
        for b in range(nb):
            rows = wb[b * BIAS_ROWS : b * BIAS_ROWS + 16, :].astype(F32)
            for vec in range(8):
                p_ref[vec : vec + 1, b * part : (b + 1) * part] = rows[0:1, vec * part : (vec + 1) * part]
            b_ref[0:1, b * 4 * part : (b + 1) * 4 * part] = rows[1:2, 0 : 4 * part]

    x = x_ref[...]
    q_ref[...] = (dg(x, wq[...], NN) + p_ref[0:1, :]).astype(BF)
    k_ref[...] = dg(x, wk[...], NN).astype(BF)
    v_ref[...] = (dg(x, wv[...], NN) + p_ref[1:2, :]).astype(BF)


def qkv_targets(part, wq, wk, wv, wb=None):
    t = [(0, part, wq, part, 0), (part, part, wk, part, 0), (2 * part, part, wv, part, 0)]
    return t if wb is None else t + [(3 * part, BIAS_ROWS, wb, BIAS_ROWS, 0)]


def project(x, got, ids, nb, deps=(), block=256):
    n, width = x.shape
    grid = n // block
    rows = pl.BlockSpec((block, width), lambda i, ids: (i, 0))
    whole = lambda shape: pl.BlockSpec(shape, lambda i, ids: (0, 0))
    count = got.count(qkv_targets(width // nb, 0, 0, 0, 0))
    return pl.pallas_call(
        functools.partial(qkv_kernel, got),
        grid_spec=pltpu.PrefetchScalarGridSpec(
            num_scalar_prefetch=1,
            grid=(grid,),
            in_specs=[rows] + [ANY] * (len(got.arrays) + len(deps)),
            out_specs=[rows, rows, rows, whole((8, width)), whole((1, 4 * width))],
            scratch_shapes=[pltpu.VMEM((width, width), BF)] * 3
            + [pltpu.VMEM((nb * BIAS_ROWS, width), BF), pltpu.SemaphoreType.DMA((count,))],
        ),
        out_shape=[jax.ShapeDtypeStruct((n, width), BF)] * 3
        + [jax.ShapeDtypeStruct((8, width), F32), jax.ShapeDtypeStruct((1, 4 * width), F32)],
        compiler_params=params(FULL),
        cost_estimate=cost(6 * n * width * width, 2 * n * width * 4 + 6 * width * width),
        name="project",
    )(ids, x, *got.arrays, *deps)


def split3(v):
    hi=v.astype(BF); r=v-hi.astype(F32); mid=r.astype(BF); lo=(r-mid.astype(F32)).astype(BF)
    return hi,mid,lo
def attn_fwd_kernel(qb, q_ref,k_ref,v_ref,qf_ref,kf_ref,*rest):
    a_ref,lf_ref=rest[-2:]
    n=q_ref.shape[0]
    lane=lax.broadcasted_iota(jnp.int32,(n,LANES),1)
    left=lane<HEAD_DIM
    q=q_ref[...]*jnp.asarray(0.125,BF); k=k_ref[...]; v=v_ref[...]
    qf=qf_ref[...]; kf=kf_ref[...]
    one=jnp.ones_like(v)
    sides=[]
    for h in range(2):
        own=left if h==0 else ~left
        sides.append((jnp.where(own,q,qf),jnp.where(own,k,kf),jnp.where(own,v,one)))
    lq=lax.broadcasted_iota(jnp.int32,(qb,LANES),1)
    leftq=lq<HEAD_DIM
    for c in range(n//qb):
        rows=slice(c*qb,(c+1)*qb)
        res=[]; lse=[]
        for h in range(2):
            qa,ka,va=sides[h]
            s=dg(qa[rows],ka,NT)
            m=jnp.max(s,-1,keepdims=True)
            p=jnp.exp(s-m).astype(BF)
            o=dg(p,va,NN)
            tot=o[:,64:65] if h==0 else o[:,0:1]
            res.append(o/tot)
            lse.append(m+jnp.log(tot))
        a_ref[rows,:]=jnp.where(leftq,res[0],res[1]).astype(BF)
        lm=jnp.where(leftq,lse[1],lse[0])
        hi,mid,lo=split3(lm)
        j=lq%HEAD_DIM
        base=qf[rows]
        lf_ref[rows,:]=jnp.where(j==4,hi,jnp.where(j==5,mid,jnp.where(j==6,lo,base)))
def attn_fwd(q,k,v,qf,kf,first,npair,deps=(),qb=512):
    n=q.shape[0]
    blk=pl.BlockSpec((n,LANES),lambda i:(0,i+first))
    whole=pl.BlockSpec((n,LANES),lambda i:(0,0))
    out=pl.BlockSpec((n,LANES),lambda i:(0,i))
    return pl.pallas_call(functools.partial(attn_fwd_kernel,qb),grid=(npair,),
        in_specs=[blk,blk,blk,whole,whole]+[ANY]*len(deps),out_specs=[out,out],
        out_shape=[jax.ShapeDtypeStruct((n,npair*LANES),BF)]*2,
        compiler_params=pltpu.CompilerParams(vmem_limit_bytes=FULL),
        cost_estimate=cost(npair*2*2*2*n*n*256,npair*n*LANES*2*5),
        name="attend_forward")(q,k,v,qf,kf,*deps)
def attn_bwd_kernel(qb,q_ref,k_ref,v_ref,da_ref,a_ref,lf_ref,kf_ref,*rest):
    d_ref,dka,dva=rest[-3:]
    n=q_ref.shape[0]
    lane=lax.broadcasted_iota(jnp.int32,(n,LANES),1)
    left=lane<HEAD_DIM
    q=q_ref[...]*jnp.asarray(0.125,BF); k=k_ref[...]; v=v_ref[...]; da=da_ref[...]
    lf=lf_ref[...]; kf=kf_ref[...]
    prod=da.astype(F32)*a_ref[...].astype(F32)
    j=lane%HEAD_DIM
    zero=jnp.zeros_like(q)
    minus=jnp.where((j>=4)&(j<7),jnp.asarray(-1,BF),jnp.asarray(0,BF))
    sides=[]
    for h in range(2):
        own=left if h==0 else ~left
        d=jnp.sum(jnp.where(own,prod,0.0),-1,keepdims=True)
        hi,mid,lo=split3(d)
        df=jnp.where(j==4,hi,jnp.where(j==5,mid,jnp.where(j==6,lo,zero)))
        sides.append((jnp.where(own,q,lf),jnp.where(own,k,kf),jnp.where(own,v,minus),jnp.where(own,da,df),
                      jnp.where(own,q,zero),jnp.where(own,da,zero)))
    kt=k.T
    for c in range(n//qb):
        rows=slice(c*qb,(c+1)*qb)
        dqs=[]; dk=None; dv=None
        for h in range(2):
            qa,ka,va,daa,qz,daz=sides[h]
            s=dg(ka,qa[rows],NT)
            p=jnp.exp(s)
            dp=dg(va,daa[rows],NT)
            ds=(p*dp).astype(BF)
            pb=p.astype(BF)
            x=dg(pb,daz[rows],NN); dv=x if dv is None else dv+x
            y=dg(ds,qz[rows],NN); dk=y if dk is None else dk+y
            dqs.append(dg(kt[h*64:(h+1)*64],ds,NN))
        d_ref[0,rows,:]=(jnp.concatenate(dqs,0).T*0.125).astype(BF)
        if c==0: dka[...]=dk; dva[...]=dv
        else: dka[...]+=dk; dva[...]+=dv
    d_ref[1]=dka[...].astype(BF)
    d_ref[2]=dva[...].astype(BF)
def attn_bwd(q,k,v,da,a,lf,kf,first,npair,skip=0,deps=(),qb=256):
    n=q.shape[0]
    blk=pl.BlockSpec((n,LANES),lambda i:(0,i+first))
    whole=pl.BlockSpec((n,LANES),lambda i:(0,0))
    own=pl.BlockSpec((n,LANES),lambda i:(0,i+skip))
    out=pl.BlockSpec((3,n,LANES),lambda i:(0,0,i))
    return pl.pallas_call(functools.partial(attn_bwd_kernel,qb),grid=(npair,),
        in_specs=[blk]*5+[own,whole]+[ANY]*len(deps),out_specs=out,
        out_shape=jax.ShapeDtypeStruct((3,n,npair*LANES),BF),
        scratch_shapes=[pltpu.VMEM((n,LANES),F32)]*2,
        compiler_params=pltpu.CompilerParams(vmem_limit_bytes=VMEM),
        cost_estimate=cost(npair*2*5*2*n*n*256,npair*n*LANES*2*9),
        name="attend_backward")(q,k,v,da,a,lf,kf,*deps)
def seg_features(seg,pad):
    n=seg.shape[0]
    j=lax.broadcasted_iota(jnp.int32,(n,LANES),1)%HEAD_DIM
    same=(seg[:,None]==j)
    qf=jnp.where((j<4)&same,1.0,0.0).astype(BF)
    kf=jnp.where(j<4,jnp.where(same&(pad[:,None]>0),0.0,-1e30),jnp.where(j<7,-1.0,0.0)).astype(BF)
    return qf,kf


def up_kernel(got, part, ids, x_ref, p_ref, bup_ref, *rest):
    n = len(got.arrays)
    a_refs = rest[: len(rest) - n - 11]
    pieces = rest[len(rest) - n - 11 : len(rest) - 11]
    a_all, y_ref, yb_ref, n_ref, s_ref, g_ref, gp_ref, wu, wo, sems, sems_out = rest[-11:]
    width = x_ref.shape[1]
    targets = [(0, part, wu, part, 0, 0)]

    @pl.when(pl.program_id(0) == 0)
    def _():
        moves = got.copies(pieces, ids, [(0, part, wo, part, 0, 4 * width)], sems_out)
        for m in moves + got.copies(pieces, ids, targets, sems):
            m.start()
        for m in moves:
            m.wait()

    a = jnp.concatenate([r[...] for r in a_refs], 1)
    a_all[...] = a
    r = x_ref[...].astype(F32) + dg(a, wo[...], NN) + p_ref[2:3, :]
    c = r - jnp.mean(r, -1, keepdims=True)
    s = lax.rsqrt(jnp.mean(c * c, -1, keepdims=True) + EPSILON)
    normed = c * s
    y = normed * p_ref[3:4, :] + p_ref[4:5, :]
    y_ref[...] = y
    n_ref[...] = normed.astype(BF)
    s_ref[...] = s
    yb = y.astype(BF)
    yb_ref[...] = yb

    @pl.when(pl.program_id(0) == 0)
    def _():
        for m in got.copies(pieces, ids, targets, sems):
            m.wait()

    step = 512
    for k in range(0, 4 * width, step):
        h = dg(yb, wu[:, k : k + step], NN) + bup_ref[:, k : k + step]
        phi = 0.5 + 0.5 * lax.erf(h * ROOT_HALF)
        g_ref[:, k : k + step] = (h * phi).astype(BF)
        gp_ref[:, k : k + step] = (phi + h * (jnp.exp(-0.5 * h * h) * INV_ROOT_TAU)).astype(BF)


def up_part(x, vecs, bup, a_parts, got, ids, nb, block=256):
    n, width = x.shape
    part = width // nb
    rows = lambda w: pl.BlockSpec((block, w), lambda i, ids: (i, 0))
    whole = lambda shape: pl.BlockSpec(shape, lambda i, ids: (0, 0))
    count = got.count([(0, part, 0, 0, 0)])
    sds = jax.ShapeDtypeStruct
    return pl.pallas_call(
        functools.partial(up_kernel, got, part),
        grid_spec=pltpu.PrefetchScalarGridSpec(
            num_scalar_prefetch=1,
            grid=(n // block,),
            in_specs=[rows(width), whole((8, width)), whole((1, 4 * width))]
            + [rows(a.shape[1]) for a in a_parts]
            + [ANY] * len(got.arrays),
            out_specs=[rows(width), rows(width), rows(width), rows(width), rows(1), rows(4 * width), rows(4 * width)],
            scratch_shapes=[pltpu.VMEM((width, 4 * width), BF), pltpu.VMEM((width, width), BF)] + [pltpu.SemaphoreType.DMA((count,))] * 2,
        ),
        out_shape=[
            sds((n, width), BF),
            sds((n, width), F32),
            sds((n, width), BF),
            sds((n, width), BF),
            sds((n, 1), F32),
            sds((n, 4 * width), BF),
            sds((n, 4 * width), BF),
        ],
        compiler_params=params(FULL),
        cost_estimate=cost(10 * n * width * width, 28 * n * width + 10 * width * width, 8 * n * width),
        name="out_norm_up",
    )(ids, x, vecs, bup, *a_parts, *got.arrays)


def down_kernel(g_ref, y_ref, c_ref, p_ref, wd, o_ref, df_ref, dr_ref, sum_ref):
    @pl.when(pl.program_id(0) == 0)
    def _():
        sum_ref[...] = jnp.zeros_like(sum_ref)

    r = y_ref[...] + dg(g_ref[...], wd[...], NN) + p_ref[5:6, :]
    c = r - jnp.mean(r, -1, keepdims=True)
    s = lax.rsqrt(jnp.mean(c * c, -1, keepdims=True) + EPSILON)
    normed = c * s
    gain = p_ref[6:7, :]
    o_ref[...] = (normed * gain + p_ref[7:8, :]).astype(BF)
    ct = c_ref[...].astype(F32)
    e = ct * gain
    dr = s * (e - jnp.mean(e, -1, keepdims=True) - normed * jnp.mean(e * normed, -1, keepdims=True))
    dr_ref[...] = dr
    df = dr.astype(BF)
    df_ref[...] = df
    sum_ref[0:1, :] += jnp.sum(ct * normed, 0, keepdims=True)
    sum_ref[1:2, :] += jnp.sum(ct, 0, keepdims=True)
    sum_ref[2:3, :] += jnp.sum(df.astype(F32), 0, keepdims=True)


def down_part(g, y, ct, vecs, w_down, block=256):
    n, width = y.shape
    rows = lambda w: pl.BlockSpec((block, w), lambda i: (i, 0))
    whole = lambda shape: pl.BlockSpec(shape, lambda i: (0, 0))
    sds = jax.ShapeDtypeStruct
    return pl.pallas_call(
        down_kernel,
        grid=(n // block,),
        in_specs=[rows(4 * width), rows(width), rows(width), whole((8, width)), whole((4 * width, width))],
        out_specs=[rows(width), rows(width), rows(width), whole((8, width))],
        out_shape=[sds((n, width), BF), sds((n, width), BF), sds((n, width), F32), sds((8, width), F32)],
        compiler_params=params(FULL),
        cost_estimate=cost(8 * n * width * width, 22 * n * width + 8 * width * width),
        name="down_norm",
    )(g, y, ct, vecs, w_down)


def hidden_kernel(df_ref, gp_ref, wd, *rest):
    dh_ref, bup_ref = rest[-2:]

    @pl.when(pl.program_id(0) == 0)
    def _():
        bup_ref[...] = jnp.zeros_like(bup_ref)

    df = df_ref[...]
    width = df.shape[1]
    step = 512
    for k in range(0, dh_ref.shape[1], step):
        dh = (dg(df, wd[k : k + step, :], NT) * gp_ref[:, k : k + step].astype(F32)).astype(BF)
        dh_ref[:, k : k + step] = dh
        row, col = k // width, k % width
        bup_ref[row : row + 1, col : col + step] += jnp.sum(dh.astype(F32), 0, keepdims=True)


def hidden_part(df, gp, w_down, which, deps=(), block=256):
    n, width = df.shape
    cols = w_down.shape[0] // 2
    rows = pl.BlockSpec((block, width), lambda i: (i, 0))
    return pl.pallas_call(
        hidden_kernel,
        grid=(n // block,),
        in_specs=[rows, pl.BlockSpec((block, cols), lambda i: (i, which)), pl.BlockSpec((cols, width), lambda i: (which, 0))]
        + [ANY] * len(deps),
        out_specs=[pl.BlockSpec((block, cols), lambda i: (i, 0)), pl.BlockSpec((8, width), lambda i: (0, 0))],
        out_shape=[jax.ShapeDtypeStruct((n, cols), BF), jax.ShapeDtypeStruct((8, width), F32)],
        compiler_params=params(FULL),
        cost_estimate=cost(2 * n * width * cols, n * (2 * width + 4 * cols) + 2 * width * cols),
        name="hidden_gradient",
    )(df, gp, w_down, *deps)


def back_kernel(up, part, ids, dh_ref, dh2_ref, dr_ref, n_ref, s_ref, p_ref, *rest):
    nu = len(up.arrays)
    pu = rest[:nu]
    dr1_ref, do_ref, da_ref, sum_ref, wu, wo, su, so = rest[-8:]
    width = dr_ref.shape[1]

    @pl.when(pl.program_id(0) == 0)
    def _():
        moves = up.copies(pu, ids, [(0, part, wu, part, 0, 0)], su) + up.copies(pu, ids, [(0, part, wo, part, 0, 4 * width)], so)
        for m in moves:
            m.start()
        sum_ref[...] = jnp.zeros_like(sum_ref)
        for m in moves:
            m.wait()

    cut = dh_ref.shape[1]
    dy = dr_ref[...] + dg(dh_ref[...], wu[:, :cut], NT) + dg(dh2_ref[...], wu[:, cut:], NT)
    normed = n_ref[...].astype(F32)
    e = dy * p_ref[3:4, :]
    dr = s_ref[...] * (e - jnp.mean(e, -1, keepdims=True) - normed * jnp.mean(e * normed, -1, keepdims=True))
    dr1_ref[...] = dr
    do = dr.astype(BF)
    do_ref[...] = do
    da_ref[...] = dg(do, wo[...], NT).astype(BF)
    sum_ref[0:1, :] += jnp.sum(dy * normed, 0, keepdims=True)
    sum_ref[1:2, :] += jnp.sum(dy, 0, keepdims=True)
    sum_ref[2:3, :] += jnp.sum(do.astype(F32), 0, keepdims=True)


def back_part(dh, dr, normed, inverse, vecs, up, ids, nb, deps=(), block=256):
    n, width = dr.shape
    part = width // nb
    rows = lambda w: pl.BlockSpec((block, w), lambda i, ids: (i, 0))
    whole = lambda shape: pl.BlockSpec(shape, lambda i, ids: (0, 0))
    sds = jax.ShapeDtypeStruct
    return pl.pallas_call(
        functools.partial(back_kernel, up, part),
        grid_spec=pltpu.PrefetchScalarGridSpec(
            num_scalar_prefetch=1,
            grid=(n // block,),
            in_specs=[rows(2 * width), rows(2 * width), rows(width), rows(width), rows(1), whole((8, width))]
            + [ANY] * (len(up.arrays) + len(deps)),
            out_specs=[rows(width), rows(width), rows(width), whole((8, width))],
            scratch_shapes=[pltpu.VMEM((width, 4 * width), BF), pltpu.VMEM((width, width), BF)]
            + [pltpu.SemaphoreType.DMA((up.count([(0, part, 0, 0, 0)]),))] * 2,
        ),
        out_shape=[sds((n, width), F32), sds((n, width), BF), sds((n, width), BF), sds((8, width), F32)],
        compiler_params=params(FULL),
        cost_estimate=cost(10 * n * width * width, 22 * n * width + 10 * width * width),
        name="norm_backward",
    )(ids, *dh, dr, normed, inverse, vecs, *up.arrays, *deps)


def sums_kernel(one, two, up0, up1, *rest):
    out = rest[-1]
    out[...] = jnp.zeros_like(out)
    for r, (src, at) in enumerate(((one, 2), (one, 0), (one, 1), (two, 2), (two, 0), (two, 1))):
        out[1 + r : 2 + r, :] = src[at : at + 1, :]
    for r, (src, at) in enumerate(((up0, 0), (up0, 1), (up1, 0), (up1, 1))):
        out[7 + r : 8 + r, :] = src[at : at + 1, :]


def pack_sums(one, two, up0, up1):
    return pl.pallas_call(
        sums_kernel,
        in_specs=[pl.BlockSpec(memory_space=pltpu.VMEM)] * 4,
        out_specs=pl.BlockSpec(memory_space=pltpu.VMEM),
        out_shape=jax.ShapeDtypeStruct((16, one.shape[1]), F32),
        compiler_params=params(4 << 20),
        cost_estimate=cost(0, 1 << 20),
        name="pack_sums",
    )(one, two, up0, up1)


def grad_rows_kernel(top, jb, lo, ls, ro, rs, *rest):
    ka, sa, kb, sb = rest[-4:]
    j = pl.program_id(0)
    half = ka.shape[1]
    got = (dg(lo[...], ro[...], TN) + dg(ls[...], rs[...], TN)).astype(BF)

    @pl.when(j % 2 == 0)
    def _():
        ka[0] = got[:half]

    @pl.when(j % 2 == 1)
    def _():
        sa[0] = got[:half]

    @pl.when(j < top)
    def _():
        kb[0] = got[half:]

    @pl.when(j >= top)
    def _():
        sb[0] = got[half:]


def grad_down(g_own, g_sib, df_own, df_sib, jb, nf, deps=()):
    n, hidden = g_own.shape
    width = df_own.shape[1]
    part = hidden // (2 * nf)
    top = nf // 2
    left = pl.BlockSpec((n, part), lambda j, jb: (0, jb[j]))
    right = pl.BlockSpec((n, width), lambda j, jb: (0, 0))
    out = lambda at: pl.BlockSpec((1, part // 2, width), lambda j, jb: (at(j), 0, 0))
    return pl.pallas_call(
        functools.partial(grad_rows_kernel, top),
        grid_spec=pltpu.PrefetchScalarGridSpec(
            num_scalar_prefetch=1,
            grid=(nf,),
            in_specs=[left, left, right, right] + [ANY] * len(deps),
            out_specs=[
                out(lambda j: j // 2),
                out(lambda j: j // 2),
                out(lambda j: jnp.minimum(j, top - 1)),
                out(lambda j: jnp.maximum(j - top, 0)),
            ],
        ),
        out_shape=[jax.ShapeDtypeStruct((top, part // 2, width), BF)] * 4,
        compiler_params=params(FULL),
        cost_estimate=cost(2 * n * hidden * width, 2 * n * hidden + 4 * n * width + hidden * width),
        name="grad_down",
    )(jb, g_own, g_sib, df_own, df_sib, *deps)


class Job:
    def __init__(self, left, rights):
        self.left, self.rights = left, rights


EXTRA = 16


def grad_cols_kernel(jobs, nl, nf, block, keeps, extra, sum_blocks, *refs):
    pos = 1
    step = pl.program_id(0)
    lefts, rights = [], []
    for spans in jobs:
        lefts.append((refs[pos : pos + nl], refs[pos + nl : pos + 2 * nl]))
        pos += 2 * nl
    for spans in jobs:
        for _ in spans:
            rights.append((refs[pos], refs[pos + 1]))
            pos += 2
    if sum_blocks:
        vec_own, vec_sib = refs[pos : pos + 2]
    outs = refs[len(refs) - len(jobs) - 4 : len(refs) - len(jobs)]
    lts = refs[len(refs) - len(jobs) :]
    n, wide = lefts[0][0][0].shape
    part = nl * wide // nf
    half = part // 2
    at = 0
    for (los, lss), spans, lt in zip(lefts, jobs, lts):

        @pl.when(step == spans[0][0])
        def _():
            for j in range(nl):
                lt[j * wide : (j + 1) * wide, 0:n] = los[j][...].T
                lt[j * wide : (j + 1) * wide, n : 2 * n] = lss[j][...].T

        for begin, count in spans:
            own, sib = rights[at]
            at += 1

            @pl.when((step >= begin) & (step < begin + count))
            def _():
                both = jnp.concatenate([own[0], sib[0]], 0)
                got = dg(lt[...], both, NN).astype(BF)
                for out, (which, side) in zip(outs, keeps):
                    for m, j in enumerate(which):
                        out[m, 0:half, :] = got[j * part + side * half : j * part + (side + 1) * half]
                if extra:
                    tile = jnp.zeros((EXTRA, block), F32)
                    if sum_blocks:
                        tile = jnp.where(step < sum_blocks, vec_own[...] + vec_sib[...], 0.0)
                    columns = jnp.sum(both.astype(F32), 0, keepdims=True)
                    tile = jnp.where(lax.broadcasted_iota(jnp.int32, (EXTRA, block), 0) == 0, columns, tile).astype(BF)
                    for out in outs:
                        for m in range(out.shape[0]):
                            out[m, half : half + EXTRA, :] = tile


def grad_cols(jobs, jb, nf, block, name, deps=(), extra=False, vecs=None):
    n, width = jobs[0].left[0].shape
    part = width // (2 * nf)
    spans, step = [], 0
    in_specs, operands, right_specs, right_ops = [], [], [], []
    for job in jobs:
        mine = []
        pick = lambda z: z.reshape(n, 2 * nf, part)[:, jb].reshape(n, nf * part)
        for z in job.left:
            if part % LANES == 0:
                nl = nf
                in_specs += [pl.BlockSpec((n, part), lambda i, jb, j=j: (0, jb[j])) for j in range(nf)]
                operands += [z] * nf
            else:
                nl = 1
                in_specs += [pl.BlockSpec((n, nf * part), lambda i, jb: (0, 0))]
                operands += [pick(z)]
        for own, sib in job.rights:
            planes, _, cols = own.shape
            per = cols // block
            count = planes * per

            def at(i, jb, step=step, count=count, per=per):
                k = jnp.clip(i - step, 0, count - 1)
                return (k // per, 0, k % per)

            right_specs += [pl.BlockSpec((1, n, block), at)] * 2
            right_ops += [own, sib]
            mine.append((step, count))
            step += count
        spans.append(mine)
    half = part // 2
    sum_blocks = 0
    if vecs is not None:
        sum_blocks = vecs[0].shape[1] // block
        right_specs += [pl.BlockSpec((EXTRA, block), lambda i, jb: (0, jnp.minimum(i, sum_blocks - 1)))] * 2
        right_ops += list(vecs)
    js = list(range(nf))
    top = nf // 2
    keeps = [([j for j in js if not j & 1], 0), ([j for j in js if j & 1], 0), ([j for j in js if j < top], 1), ([j for j in js if j >= top], 1)]
    lines = half + (EXTRA if extra else 0)
    out_spec = pl.BlockSpec((nf // 2, lines, block), lambda i, jb: (0, 0, i))
    out_shape = jax.ShapeDtypeStruct((nf // 2, lines, step * block), BF)
    return pl.pallas_call(
        functools.partial(grad_cols_kernel, spans, nl, nf, block, keeps, extra, sum_blocks),
        grid_spec=pltpu.PrefetchScalarGridSpec(
            num_scalar_prefetch=1,
            grid=(step,),
            in_specs=in_specs + right_specs + [ANY] * len(deps),
            out_specs=[out_spec] * 4,
            scratch_shapes=[pltpu.VMEM((nf * part, 2 * n), BF)] * len(jobs),
        ),
        out_shape=[out_shape] * 4,
        compiler_params=params(),
        cost_estimate=cost(2 * n * width * step * block, 4 * n * (step * block + width // 2)),
        name=name,
    )(jb, *operands, *right_ops, *deps)


def input_kernel(got, part, groups, place, ids, dr_ref, *rest):
    n = len(got.arrays)
    d_refs, pieces = rest[1 : 1 + groups], rest[1 + groups : 1 + groups + n]
    out_ref, wq, wk, wv, sems = rest[-5:]
    targets = qkv_targets(part, wq, wk, wv)

    @pl.when(pl.program_id(0) == 0)
    def _():
        moves = got.copies(pieces, ids, targets, sems)
        for c in moves:
            c.start()
        for c in moves:
            c.wait()

    total = dr_ref[...]
    for k, w in enumerate((wq, wk, wv)):
        d = jnp.concatenate([r[k] for r in d_refs], 1)
        total += dg(d, w[...], NT)
    out_ref[...] = total


def input_part(dr, grads, got, ids, place, nb, deps=(), block=256):
    n, width = dr.shape
    steps = n // 2 // block
    rows = pl.BlockSpec((block, width), lambda i, ids: (i + ids[ids.shape[0] - 2 + place] * steps, 0))
    three = lambda w: pl.BlockSpec((3, block, w), lambda i, ids: (0, i + ids[ids.shape[0] - 2 + place] * steps, 0))
    count = got.count(qkv_targets(width // nb, 0, 0, 0))
    return pl.pallas_call(
        functools.partial(input_kernel, got, width // nb, len(grads), place),
        grid_spec=pltpu.PrefetchScalarGridSpec(
            num_scalar_prefetch=1,
            grid=(steps,),
            in_specs=[rows, ANY] + [three(a.shape[2]) for a in grads] + [ANY] * (len(got.arrays) + len(deps)),
            out_specs=pl.BlockSpec((block, width), lambda i, ids: (i, 0)),
            scratch_shapes=[pltpu.VMEM((width, width), BF)] * 3 + [pltpu.SemaphoreType.DMA((count,))],
        ),
        out_shape=jax.ShapeDtypeStruct((n // 2, width), F32),
        compiler_params=params(FULL),
        cost_estimate=cost(3 * n * width * width, 7 * n * width + 6 * width * width),
        name="input_gradient",
    )(ids, dr, dr, *grads, *got.arrays, *deps)


def add_low(a, b):
    return (a[...].astype(F32) + b[...].astype(F32)).astype(BF)


SMALL = 16 << 20


def tile_of(cols):
    return cols // 2 if cols % (2 * LANES) == 0 else cols


def stage_kernel(last, odd, ka, ra, kb, rb, *rest):
    outs = rest[len(rest) - (2 if last else 4) :]
    a, b = add_low(ka, ra), add_low(kb, rb)
    m = a.shape[0]
    if last:
        swapped = odd[0] == 1
        outs[0][...] = jnp.where(swapped, b, a)
        outs[1][...] = jnp.where(swapped, a, b)
    else:
        for i in range(m // 2):
            outs[0][i], outs[1][i] = a[2 * i], a[2 * i + 1]
            outs[2][i], outs[3][i] = b[i], b[m // 2 + i]


def stage(odd, ka, ra, kb, rb, deps):
    m, rows, cols = ka.shape
    block = tile_of(cols)
    last = m == 1
    into = pl.BlockSpec((m, rows, block), lambda i, odd: (0, 0, i))
    mo = max(m // 2, 1)
    out = pl.BlockSpec((mo, rows, block), lambda i, odd: (0, 0, i))
    return pl.pallas_call(
        functools.partial(stage_kernel, last),
        grid_spec=pltpu.PrefetchScalarGridSpec(
            num_scalar_prefetch=1,
            grid=(cols // block,),
            in_specs=[into] * 4 + [ANY] * len(deps),
            out_specs=[out] * (2 if last else 4),
        ),
        out_shape=[jax.ShapeDtypeStruct((mo, rows, cols), BF)] * (2 if last else 4),
        compiler_params=params(9 << 20),
        cost_estimate=cost(0, 12 * m * rows * cols),
        name="sum_plane",
    )(odd, ka, ra, kb, rb, *deps)


def pair_sum_kernel(a, b, *rest):
    rest[-1][...] = add_low(a, b)


def pair_sum(a, b, deps):
    rows, cols = a.shape
    block = tile_of(cols)
    spec = pl.BlockSpec((rows, block), lambda i: (0, i))
    return pl.pallas_call(
        pair_sum_kernel,
        grid=(cols // block,),
        in_specs=[spec] * 2 + [ANY] * len(deps),
        out_specs=spec,
        out_shape=jax.ShapeDtypeStruct((rows, cols), BF),
        compiler_params=params(4 << 20),
        cost_estimate=cost(0, 6 * rows * cols),
        name="sum_rep",
    )(a, b, *deps)


def pick_kernel(odd, a, b, *rest):
    rest[-2][...], rest[-1][...] = a[...], b[...]


def pick(odd, v, deps=()):
    rows, cols = v.shape
    block = tile_of(cols)
    spec = lambda flip: pl.BlockSpec((rows // 2, block), lambda i, odd: ((odd[0] + flip) % 2, i))
    out = pl.BlockSpec((rows // 2, block), lambda i, odd: (0, i))
    return pl.pallas_call(
        pick_kernel,
        grid_spec=pltpu.PrefetchScalarGridSpec(
            num_scalar_prefetch=1, grid=(cols // block,), in_specs=[spec(0), spec(1)] + [ANY] * len(deps), out_specs=[out, out]
        ),
        out_shape=[jax.ShapeDtypeStruct((rows // 2, cols), BF)] * 2,
        compiler_params=params(4 << 20),
        cost_estimate=cost(0, 4 * rows * cols),
        name="pick_half",
    )(odd, v, v, *deps)


class RepChain:
    def __init__(self, kept, sent, nr, odd):
        self.kept, self.sent, self.nr, self.odd = kept, sent, nr, odd

    def rep_first(self, deps=()):
        self.kept = pair_sum(self.kept, swap(self.sent, "rep", self.nr, 1), deps)
        return (self.kept,)

    def rep_middle(self, deps=()):
        xor = 2
        while xor < self.nr:
            self.kept = pair_sum(self.kept, swap(self.kept, "rep", self.nr, xor), deps)
            xor *= 2
        return (self.kept,)

    def rep_middle_part(self, which, deps=()):
        if self.nr != 4:
            return self.rep_middle(deps) if which == 1 else ()
        rows = self.kept.shape[0] // 2
        part = self.kept[:rows] if which == 0 else self.kept[rows:]
        part = pair_sum(part, swap(part, "rep", self.nr, 2), deps)
        if which == 0:
            self.first_part = part
        else:
            self.kept = jnp.concatenate([self.first_part, part], 0)
        return (part,)

    def rep_last(self):
        self.other = swap(self.kept, "rep", self.nr, 1)
        return (self.other,)

    def halves(self):
        odd = self.odd[0] == 1
        return jnp.where(odd, self.other, self.kept).astype(F32), jnp.where(odd, self.kept, self.other).astype(F32)

    def result(self):
        return jnp.concatenate(self.halves(), 0)


class Chain(RepChain):
    def __init__(self, parts, nf, nr, odd):
        self.nf, self.nr, self.odd = nf, nr, odd
        self.ka, self.sa, self.kb, self.sb = parts
        self.level, self.bits = 0, nf.bit_length() - 1

    def plane(self, deps=()):
        a, b = self.level, self.bits - 1 - self.level
        ra, rb = swap(self.sa, "fsdp", self.nf, 1 << a), swap(self.sb, "fsdp", self.nf, 1 << b)
        self.level += 1
        out = stage(self.odd, self.ka, ra, self.kb, rb, deps)
        if self.level == self.bits:
            self.kept, self.sent = out[0][0], out[1][0]
        else:
            self.ka, self.sa, self.kb, self.sb = out
        return tuple(out)

    def rest(self, deps=()):
        out = ()
        while self.level < self.bits:
            out = self.plane(deps)
        return out


def join_kernel(odd, kept, other, *rest):
    out = rest[-1]
    rows = kept.shape[0]
    swapped = odd[0] == 1
    out[:rows, :] = jnp.where(swapped, other[...], kept[...]).astype(F32)
    out[rows:, :] = jnp.where(swapped, kept[...], other[...]).astype(F32)


def join(chain, deps=()):
    rows, cols = chain.kept.shape
    block = cols // 2
    spec = pl.BlockSpec((rows, block), lambda i, odd: (0, i))
    return pl.pallas_call(
        join_kernel,
        grid_spec=pltpu.PrefetchScalarGridSpec(
            num_scalar_prefetch=1,
            grid=(2,),
            in_specs=[spec] * 2 + [ANY] * len(deps),
            out_specs=pl.BlockSpec((2 * rows, block), lambda i, odd: (0, i)),
        ),
        out_shape=jax.ShapeDtypeStruct((2 * rows, cols), F32),
        compiler_params=params(8 << 20),
        cost_estimate=cost(0, 12 * rows * cols),
        name="join_halves",
    )(chain.odd, chain.kept, chain.other, *deps)


def finish_kernel(half, width, wide, counts, odd, *refs):
    n = len(counts)
    q, k, v, o, small, line = refs[2 * n :]
    for at in range(2):
        rows = slice(at * half, (at + 1) * half)
        group, lines = 0, []
        for i, count in enumerate(counts):
            both = jnp.where(odd[0] == at, refs[2 * i][...], refs[2 * i + 1][...]).astype(F32)
            col = 0
            if i == 0:
                o[rows, :] = both[:half, :width]
                if at == 0:
                    small[...] = both[half : half + EXTRA, :width]
                col = width
            lines.append(both[half : half + 8, col:])
            for _ in range(count):
                for out in (q, k, v):
                    out[rows, group * wide : (group + 1) * wide] = both[:half, col : col + wide]
                    col += wide
                group += 1
        if at == 0:
            line[...] = jnp.concatenate(lines, 1)


def finish(odd, chains, counts, half, width, wide):
    spec = pl.BlockSpec(memory_space=pltpu.VMEM)
    sds = jax.ShapeDtypeStruct
    return pl.pallas_call(
        functools.partial(finish_kernel, half, width, wide, counts),
        in_specs=[pl.BlockSpec(memory_space=pltpu.SMEM)] + [spec] * (2 * len(chains)),
        out_specs=[spec] * 6,
        out_shape=[sds((2 * half, width), F32)] * 4 + [sds((EXTRA, width), F32), sds((8, 3 * wide * sum(counts)), F32)],
        compiler_params=params(12 << 20),
        cost_estimate=cost(0, 6 << 20),
        name="finish",
    )(odd, *[z for c in chains for z in (c.kept, c.other)])


def body(tokens, segment_ids, padding, cotangent, w_query, w_key, w_value, w_out, b_query, b_value, b_out,
         gain_one, shift_one, w_up, b_up, w_down, b_down, gain_two, shift_two, *, nr, nf, ns):
    _, part_len, width = tokens.shape
    f, c = lax.axis_index("fsdp"), lax.axis_index("seq")
    rel = [((f ^ j) * 2 + (c ^ p)) for j in range(nf) for p in range(2)]
    absolute = [(j * 2 + (c ^ p)) for j in range(nf) for p in range(2)]
    ids = jnp.stack(rel + absolute + [1 - c, c]).astype(jnp.int32)
    jb = jnp.stack(rel[::2]).astype(jnp.int32)
    jb_abs = jnp.stack(absolute[::2]).astype(jnp.int32)
    core = c.astype(jnp.int32).reshape(1)
    odd = (lax.axis_index("rep") & 1).astype(jnp.int32).reshape(1)
    sib_of = lambda z: swap(z, "seq", ns, 1)
    nb = 2 * nf
    part = width // nb

    qkv_shard = pack_first(
        [b_query, b_value, b_out, gain_one, shift_one, b_down, gain_two, shift_two, b_up], [w_query, w_key, w_value]
    )
    first = gather_start(qkv_shard, nf)
    x, x_sib, ct = pair_up(core, [(tokens, sib_of(tokens), 2), (cotangent, sib_of(cotangent), 1)])
    marks = jnp.stack([segment_ids, padding])
    theirs = sib_of(marks)
    own = c == 0
    mine_m, their_m = jnp.where(own, marks[:, 0], marks[:, 1]), jnp.where(own, theirs[:, 0], theirs[:, 1])
    whole = jnp.where(own, jnp.concatenate([mine_m, their_m], 1), jnp.concatenate([their_m, mine_m], 1))
    qf, kf = seg_features(whole[0], whole[1])
    (up_shard,) = split_rows(
        [w_up, w_out], [(0, 0, part, 0, 0, 0), (1, 0, part, 0, 0, 4 * width)], [(part, 5 * width)], (), "pack_up"
    )
    far = gather_far(first, nf, (up_shard,))
    gate = tuple(far) or tuple(first)
    got_qkv, _ = gather_end(qkv_shard, first, far, nf, ns, (), (x, qf))
    first_up = gather_start(after(up_shard, x, *gate), nf)
    q, k, v, vecs, bup = project(x, got_qkv, ids, nb)

    pairs = width // LANES
    groups = 4
    each = pairs // groups
    fwd = [attn_fwd(q, k, v, qf, kf, 0, each)]
    fwd.append(attn_fwd(q, k, v, qf, kf, each, each, (fwd[0][0],)))
    far_up = gather_far(first_up, nf, (fwd[1][0],))
    full_down = lax.all_gather(after(w_down, fwd[1][0], *far_up), ("fsdp", "seq"), axis=0, tiled=True)
    fwd.append(attn_fwd(q, k, v, qf, kf, 2 * each, 2 * each, (fwd[1][0],) + tuple(first_up)))
    got_up, swaps = gather_end(up_shard, first_up, far_up, nf, ns, (fwd[2][0],))
    lf = [(fwd[0][1], 0), (fwd[1][1], 0), (fwd[2][1], 0), (fwd[2][1], each)]

    a_all, y, yb, normed, inverse, g, gp = up_part(x, vecs, bup, [r[0] for r in fwd], got_up, ids, nb)
    a_sib, yb_sib, g_sib = sib_of(a_all), sib_of(yb), sib_of(g)
    out, df, dr, sums_two = down_part(g, y, ct, vecs, full_down)
    df_sib = sib_of(after(df, yb_sib, a_sib))
    dh0, sum_up0 = hidden_part(df, gp, full_down, 0, (yb_sib, a_sib))
    dh0_sib = sib_of(after(dh0, df_sib, g_sib))
    dh1, sum_up1 = hidden_part(df, gp, full_down, 1, (dh0, df_sib, g_sib))
    dh1_sib = sib_of(after(dh1, dh0_sib))
    g_down = grad_down(g, g_sib, df, df_sib, jb, nf, (dh1, dh0_sib))
    chain_down = Chain(after(g_down, dh1_sib), nf, nr, odd)
    g_up = grad_cols([Job((yb, yb_sib), [(dh0[None], dh0_sib[None]), (dh1[None], dh1_sib[None])])], jb, nf, 1024, "grad_up", (g_down[0],))
    out_sib = sib_of(after(out, dh0_sib))
    output = unpair_up(core, *after((out, out_sib), g_up[0]), part_len)
    now = chain_down.plane((g_up[0], output))
    g_up = after(g_up, *now)
    chain_up = Chain(g_up, nf, nr, odd)
    dr1, do, da, sums_one = back_part((dh0, dh1), dr, normed, inverse, vecs, got_up, ids, nb, now + (g_up[0],))
    now = chain_down.rest((da,))
    do_sib = sib_of(after(do, *now))
    sums = pack_sums(*after((sums_one, sums_two, sum_up0, sum_up1), *now))

    grads, sibs = [], []

    def run(i, deps):
        grads.append(attn_bwd(q, k, v, da, a_all, lf[i][0], kf, i * each, each, lf[i][1], deps))
        return (grads[-1],)

    def send(i, deps):
        sibs.append(sib_of(after(grads[i], *deps)))

    dep = run(0, (da,) + now)
    now = chain_up.plane(dep) + chain_down.rep_first(dep)
    send(0, now)
    sums_sib = sib_of(after(sums, *now))
    dep = run(1, dep + now + (output, do_sib, sums_sib, sibs[0]))
    now = chain_up.rest(dep) + chain_down.rep_middle(dep)
    chain_down.rep_last()
    send(1, now)
    g_one = grad_cols(
        [Job((a_all, a_sib), [(do[None], do_sib[None])]), Job((x, x_sib), [(grads[0], sibs[0])])],
        jb, nf, 256, "grad_out_qkv", dep + now, True, (sums, sums_sib),
    )
    dep = (g_one[0],)
    now = chain_up.rep_first(dep)
    chain_one = Chain(after(g_one, *now), nf, nr, odd)
    dep = run(2, dep + now + (sibs[1],))
    final_down = join(chain_down, dep)
    now = chain_one.plane(dep) + chain_up.rep_middle_part(0, dep) + (final_down,)
    send(2, now)
    g_two = grad_cols([Job((x, x_sib), [(grads[i], sibs[i]) for i in (1, 2)])], jb, nf, 256, "grad_qkv", dep + now, True)
    dep = (g_two[0],)
    now = chain_one.rest(dep) + chain_up.rep_middle_part(1, dep)
    chain_up.rep_last()
    chain_two = Chain(after(g_two, *now), nf, nr, odd)
    dep = run(3, dep + now)
    now = chain_two.plane(dep) + chain_one.rep_first(dep)
    send(3, now)
    g_three = grad_cols([Job((x, x_sib), [(grads[3], sibs[3])])], jb, nf, 256, "grad_qkv", dep + now, True)
    dep = (g_three[0],)
    now = chain_two.rest(dep)
    chain_three = Chain(after(g_three, *now), nf, nr, odd)
    send_half = input_part(dr1, grads, got_qkv, ids, 0, nb, dep + now)
    dep = (send_half,)
    now = chain_three.plane(dep) + chain_one.rep_middle(dep) + chain_two.rep_first(dep)
    chain_one.rep_last()
    their_half = sib_of(after(send_half, *now))
    keep_half = input_part(dr1, grads, got_qkv, ids, 1, nb, dep + now)
    dep = (keep_half,)
    now = chain_three.rest(dep) + chain_two.rep_middle(dep)
    final_up = join(chain_up, dep + now)
    chain_two.rep_last()
    input_grad = unpair_up(core, *after((keep_half, their_half), *now), part_len)
    chain_three.rep_first()
    chain_three.rep_middle((input_grad,))
    chain_three.rep_last()
    half = part // 2
    wide = each * LANES
    final_q, final_k, final_v, final_out, small, line = finish(odd, (chain_one, chain_two, chain_three), (1, 2, 1), half, width, wide)
    line = line[0].reshape(groups, 3, wide)
    vectors = jnp.concatenate([line[:, 0].reshape(1, width), line[:, 2].reshape(1, width), small[1:7]], 0)
    own_block = 2 * f + c
    v8 = lax.dynamic_slice(vectors, (0, own_block * part), (8, part))
    final_bup = lax.dynamic_slice(small[7:11].reshape(-1), (own_block * 4 * part,), (4 * part,))
    return (output, input_grad, final_q, final_k, final_v, final_out, v8[0], v8[1], v8[2], v8[3], v8[4],
            final_up, final_bup, final_down, v8[5], v8[6], v8[7])


def solution(mesh):
    tok = P(("rep", "fsdp"), "seq", None)
    ids = P(("rep", "fsdp"), "seq")
    mat = P(("fsdp", "seq"), None)
    vec = P(("fsdp", "seq"))
    sizes = mesh.shape
    return jax.shard_map(
        functools.partial(body, nr=sizes["rep"], nf=sizes["fsdp"], ns=sizes["seq"]),
        mesh=mesh,
        in_specs=(tok, ids, ids, tok) + (mat,) * 4 + (vec,) * 5 + (mat, vec, mat) + (vec,) * 3,
        out_specs=(tok, tok) + (mat,) * 4 + (vec,) * 5 + (mat, vec, mat) + (vec,) * 3,
        check_vma=False,
    )
```
